32 devices in a mesh: groups: 2 (over y), bond: 4 (over z), mpo: 4 (over x, core).
Axes of the slice: x: 2, y: 2, z: 4, core: 2. Of those that a mesh axis runs over, the one named last changes fastest.
Arguments:
- psi: bfloat16 [8, 16, 128, 128], P(('groups', 'bond'), 'mpo'), parts along dimension 0, may hold values from -24 to 24
- left_env: bfloat16 [20, 8, 128, 128], P('mpo', ('groups', 'bond')), parts along dimension 1, may hold values from -0.5 to 0.5
- right_env: bfloat16 [20, 8, 128, 128], P(None, ('groups', 'bond')), parts along dimension 1, may hold values from -0.125 to 0.125
- site_one: bfloat16 [40, 20, 4, 4], P('groups'), parts along dimension 0, may hold values from -0.625 to 0.625
- site_two: bfloat16 [40, 20, 4, 4], P('groups'), parts along dimension 0, may hold values from -0.625 to 0.625
- mpo_charge: int32 [20], replicated, may hold values from -1 to 1
- left_sizes: int32 [8], P('groups'), parts along dimension 0, may hold values from 64 to 128, as said below
- right_sizes: int32 [8], P('groups'), parts along dimension 0, may hold values from 64 to 128, as said below
Outputs:
- image: bfloat16 [8, 16, 128, 128], P(('groups', 'bond'), 'mpo'), parts along dimension 0
- correction_image: bfloat16 [8, 16, 128, 128], P(('groups', 'bond'), 'mpo'), parts along dimension 0
The draws below stay inside these ranges and needn't reach their ends.
There are 2 independent parts, one for each index of `groups`. The reference program is written for one: setup_inputs(seed, part) draws one part's arguments, and reference() takes and returns one part's arrays. A program takes and returns all parts, laid end to end along the dimension named above; an argument that names none is the same for every part. Nothing has to cross between parts.
Inputs may be any that keep to these rules, and one draw needn't show every extreme that they name: `left_sizes`: live rows of a sector; some sector has 128 and some has 64. `right_sizes`: live rows of a sector; some sector has 128 and some has 64.
All inputs are finite; a program needn't handle non-finite values.
Results may differ from the reference program's by a relative error of at most 0.006.
The reference program's roundings to bfloat16 on the way count: a program that leaves them out, or rounds other values in their place, can miss the bound.
Values may be sent and summed in bfloat16 or wider, within the bound.
No kernel may reach another device: no remote copies, remote signals or barrier semaphores. Data moves between devices by JAX's collectives and lax.ppermute only.
A program may use at most 128 MiB of HBM per device.

```python
import jax
import jax.numpy as jnp
from jax import lax

W = 20
PH = 4
PP = 16
BC = 128
NSEC = 4
N_MPO = 4


def sector_sizes(key):
    first_key, second_key = jax.random.split(key)
    sizes = jax.random.randint(first_key, (NSEC,), BC // 2, BC + 1)
    spots = jax.random.permutation(second_key, NSEC)
    sizes = sizes.at[spots[0]].set(BC)
    sizes = sizes.at[spots[1]].set(BC // 2)
    return sizes.astype(jnp.int32)


def draw_left_sizes(key, part):
    key = jax.random.fold_in(key, 11)
    return sector_sizes(key)


def draw_right_sizes(key, part):
    key = jax.random.fold_in(key, 12)
    return sector_sizes(key)


def sector_growth(top):
    position = jnp.arange(NSEC, dtype=jnp.float32) / max(NSEC - 1, 1)
    return jnp.exp(position * jnp.log(top))[:, None, None, None]


def draw_psi(key, part):
    key = jax.random.fold_in(key, 13)
    values = jnp.clip(jax.random.normal(key, (NSEC, PP, BC, BC), jnp.float32), -6.0, 6.0)
    values = values * sector_growth(4.0)
    return values.astype(jnp.bfloat16)


def set_ends(values, rng, smallest, top_value):
    longest = values.shape.index(max(values.shape))
    spots = []
    for shift in (0, 1):
        where = [jax.random.randint(jax.random.fold_in(rng, axis), (), 0, length) for axis, length in enumerate(values.shape)]
        where[longest] = (where[longest] + shift) % values.shape[longest]
        spots.append(tuple(where))
    return values.at[spots[0]].set(smallest).at[spots[1]].set(top_value)


def block_levels(stream_key, shape, cuts, smallest, high):
    gain, own = 1.0, jax.random.fold_in(stream_key, 6)
    for dim, blocks in cuts:
        heights = jnp.exp(jax.random.uniform(jax.random.fold_in(own, dim), (blocks,), jnp.float32, smallest / len(cuts), high / len(cuts)))
        gain = gain * jnp.repeat(heights, shape[dim] // blocks).reshape([-1 if axis == dim else 1 for axis in range(len(shape))])
    return gain


def centred(stream_key, shape, width, limit, cuts=(), kind=jnp.bfloat16):
    factor_of = block_levels(stream_key, shape, cuts, -0.22, 0.18) if cuts else 1.0
    values = jax.random.normal(stream_key, shape, jnp.float32) * width * factor_of
    return jnp.minimum(jnp.maximum(values, -limit), limit).astype(kind)


def setup_inputs(seed: int = 0, part: int = 0) -> dict:
    key_of = jax.random.split(jax.random.key(seed), 9)
    part_keys = jax.random.split(jax.random.fold_in(key_of[8], part), 9)
    psi = draw_psi(jax.random.fold_in(jax.random.fold_in(key_of[8], part), 71), part)
    left_env = centred(part_keys[1], (W, NSEC, BC, BC), BC ** -0.5, 0.5, ((0, 4), (1, 4)))
    right_env = centred(part_keys[2], (W, NSEC, BC, BC), (W * BC) ** -0.5, 0.125, ((1, 4),))
    site_one = centred(part_keys[3], (W, W, PH, PH), (W * PH) ** -0.5, 0.625)
    site_two = centred(part_keys[4], (W, W, PH, PH), (W * PH) ** -0.5, 0.625)
    mpo_charge = set_ends(jax.random.randint(key_of[5], (W,), -1, 2), jax.random.fold_in(key_of[5], 1), -1, 1).astype(jnp.int32)
    left_sizes = draw_left_sizes(jax.random.fold_in(jax.random.fold_in(key_of[8], part), 71), part)
    right_sizes = draw_right_sizes(jax.random.fold_in(jax.random.fold_in(key_of[8], part), 71), part)
    return dict(psi=psi, left_env=left_env, right_env=right_env, site_one=site_one, site_two=site_two, mpo_charge=mpo_charge, left_sizes=left_sizes, right_sizes=right_sizes)


EPSILON = 1e-06
STATE_CHARGES = (0, 1, 1, 2)

def pair_charges():
    return [left + right for left in STATE_CHARGES for right in STATE_CHARGES]

def rounded(value):
    return lax.optimization_barrier(value.astype(jnp.bfloat16)).astype(jnp.float32)

def charge_allowed(weight, row_charge, column_charge):
    local_charge = jnp.array(STATE_CHARGES, jnp.int32)
    charge_step = local_charge[:, None] - local_charge[None, :]
    bond_step = column_charge[None, :] - row_charge[:, None]
    allowed = charge_step[None, None, :, :] == bond_step[:, :, None, None]
    return jnp.where(allowed, weight, jnp.zeros_like(weight))

def live_blocks(left_sizes, right_sizes):
    charges = jnp.array(pair_charges(), jnp.int32)
    sectors = jnp.arange(NSEC, dtype=jnp.int32)
    target = sectors[:, None] + charges[None, :]
    padded = jnp.concatenate([right_sizes, jnp.zeros((4,), jnp.int32)])
    right_live = jnp.take(padded, target)
    rows = jnp.arange(BC, dtype=jnp.int32)
    left_ok = rows[None, :] < left_sizes[:, None]
    right_ok = rows[None, None, :] < right_live[:, :, None]
    inside = target < NSEC
    return inside[:, :, None, None] & left_ok[:, None, :, None] & right_ok[:, :, None, :]

def apply_hamiltonian(vector, left_env, right_env, first_site, second_site, mpo_charge):
    zero_block = jnp.zeros((1, PP, BC, BC), jnp.bfloat16)
    padded = jnp.concatenate([zero_block, vector, zero_block], 0)
    right_pad = jnp.concatenate([right_env, jnp.zeros((W, 4, BC, BC), jnp.bfloat16)], 1)
    grouped_site = first_site.reshape(N_MPO, W // N_MPO, W, PH, PH).astype(jnp.float32)
    second_wide = second_site.astype(jnp.float32)

    def one_sector(sector):
        nearby = lax.dynamic_slice_in_dim(padded, sector, 3, 0)
        picked = jnp.take(nearby, (1 - mpo_charge).astype(jnp.int32), axis=0)
        left = lax.dynamic_index_in_dim(left_env, sector, 1, keepdims=False)
        left_done = rounded(jnp.einsum('wik,wpkj->wpij', left.astype(jnp.float32), picked.astype(jnp.float32)))
        left_done = left_done.reshape(N_MPO, W // N_MPO, PH, PH, BC, BC)
        middle = rounded(jnp.einsum('gwvxa,gwabij->gvxbij', grouped_site, left_done))
        mpo_done = rounded(jnp.einsum('vuyb,gvxbij->guxyij', second_wide, middle))
        mpo_done = mpo_done.reshape(N_MPO, W, PP, BC, BC)
        rights = lax.dynamic_slice_in_dim(right_pad, sector, 5, 1).astype(jnp.float32)
        right_pick = jnp.stack([rights[:, charge] for charge in pair_charges()], 1)
        return jnp.einsum('gupij,uplj->pil', mpo_done, right_pick)
    return lax.map(one_sector, jnp.arange(NSEC, dtype=jnp.int32))

def reference(psi, left_env, right_env, site_one, site_two, mpo_charge, left_sizes, right_sizes):
    live = live_blocks(left_sizes, right_sizes)
    first_site = charge_allowed(site_one, mpo_charge, mpo_charge)
    second_site = charge_allowed(site_two, mpo_charge, mpo_charge)
    vector = jnp.where(live, psi, jnp.zeros_like(psi))
    image = jnp.where(live, apply_hamiltonian(vector, left_env, right_env, first_site, second_site, mpo_charge), 0.0).astype(jnp.bfloat16)
    vector_full = vector.astype(jnp.float32)
    image_full = image.astype(jnp.float32)
    correlation = jnp.sum(vector_full * image_full)
    norm_sq = jnp.sum(vector_full * vector_full)
    rayleigh = correlation / norm_sq
    residual = image_full - rayleigh * vector_full
    squares = jnp.sum(residual * residual)
    scale = lax.rsqrt(squares / (NSEC * PP * BC * BC) + EPSILON)
    correction = (residual * scale).astype(jnp.bfloat16)
    second = jnp.where(live, apply_hamiltonian(correction, left_env, right_env, first_site, second_site, mpo_charge), 0.0).astype(jnp.bfloat16)
    return (image, second)
```

```python
import functools

import jax
import jax.numpy as jnp
from jax import lax
from jax.experimental import pallas as pl
from jax.experimental.pallas import tpu as pltpu
from jax.sharding import PartitionSpec as P

EPSILON = 1e-06
STATE_CHARGES = (0, 1, 1, 2)
STATES = len(STATE_CHARGES)
PAIRS = STATES * STATES
RIM = 4
F32 = jnp.float32
BF16 = jnp.bfloat16
NT = (((1,), (1,)), ((), ()))


def pair_charges():
    return [left + right for left in STATE_CHARGES for right in STATE_CHARGES]


def round_up(value, step):
    return -(-value // step) * step


def charge_allowed(weight, row_charge, column_charge):
    local_charge = jnp.array(STATE_CHARGES, jnp.int32)
    charge_step = local_charge[:, None] - local_charge[None, :]
    bond_step = column_charge[None, :] - row_charge[:, None]
    allowed = charge_step[None, None, :, :] == bond_step[:, :, None, None]
    return jnp.where(allowed, weight, jnp.zeros_like(weight))


def from_bond(value, step):
    count = lax.axis_size("bond")
    pairs = [(i + step, i) for i in range(count) if 0 <= i + step < count]
    return lax.ppermute(value, "bond", pairs)


def from_mpo(value, flip):
    count = lax.axis_size("mpo")
    return lax.ppermute(value, "mpo", [(i ^ flip, i) for i in range(count)])


def mpo_bits():
    count = lax.axis_size("mpo")
    bits = []
    while count > 1:
        count //= 2
        bits.append(count)
    return bits


def spread(value):
    pieces = {0: value}
    for bit in mpo_bits():
        pieces.update({r ^ bit: from_mpo(piece, bit) for r, piece in list(pieces.items())})
    return [pieces[r] for r in range(len(pieces))]


def merged(one, two):
    a1, b1, c1 = one[0:1], one[1:2], one[2:3]
    a2, b2, c2 = two[0:1], two[1:2], two[2:3]
    both = b1 + b2
    ratio1 = jnp.where(b1 > 0, a1 / jnp.where(b1 > 0, b1, 1.0), 0.0)
    ratio2 = jnp.where(b2 > 0, a2 / jnp.where(b2 > 0, b2, 1.0), 0.0)
    share = jnp.where(both > 0, b1 / jnp.where(both > 0, both, 1.0), 0.0) * b2
    gap = ratio1 - ratio2
    rest = jnp.zeros((one.shape[0] - 3, one.shape[1]), F32)
    return jnp.concatenate([a1 + a2, both, c1 + c2 + gap * gap * share, rest], 0)


def sector_limits(sizes_ref, sector, count):
    inside = (sector >= 0) & (sector < count)
    return jnp.where(inside, sizes_ref[jnp.clip(sector, 0, count - 1)], 0)


def state_charge(state):
    return (state + 1) // 2


class Plan:
    def __init__(self, n_mpo, n_bond, width, mpo_width):
        self.n_mpo = n_mpo
        self.n_bond = n_bond
        self.width = width
        self.w = mpo_width
        self.w_here = mpo_width // n_mpo
        self.w_pad = round_up(mpo_width, 8)
        self.rows = width // n_mpo
        self.k = STATES * self.w_pad
        self.far = min(RIM, n_bond - 1)


def fill_left(plan, charge_ref, own_left, piece_refs, wide, ls):
    me = lax.axis_index("mpo")
    wide[...] = jnp.zeros_like(wide)
    for r in range(plan.n_mpo):
        owner = lax.bitwise_xor(me, r)
        for t in range(plan.w_here):
            w = owner * plan.w_here + t
            if r == 0:
                block = own_left[t, pl.ds(pl.multiple_of(me * plan.rows, plan.rows), plan.rows), :]
            else:
                block = piece_refs[r - 1][t]
            block = block.astype(F32)
            for c, charge in enumerate((0, 1, -1)):
                factor = jnp.where(charge_ref[w] == charge, 1.0, 0.0).astype(F32)
                wide[c, pl.ds(w, plan.rows, stride=plan.w_pad), :] = block * factor
    for c in range(3):
        ls[:, c * plan.width : (c + 1) * plan.width] = wide[c].astype(BF16)


def fill_vector(plan, left_ref, right_ref, psi_refs, fs):
    me = lax.axis_index("mpo")
    here = lax.axis_index("bond")
    row = lax.broadcasted_iota(jnp.int32, (plan.width, plan.width), 0)
    column = lax.broadcasted_iota(jnp.int32, (plan.width, plan.width), 1)
    for c, step in enumerate((0, -1, 1)):
        sector = here + step
        row_ok = row < sector_limits(left_ref, sector, plan.n_bond)
        for r in range(plan.n_mpo):
            first = lax.bitwise_xor(me, r)
            for second in range(STATES):
                target = sector + state_charge(first) + STATE_CHARGES[second]
                ok = row_ok & (column < sector_limits(right_ref, target, plan.n_bond))
                block = psi_refs[r * 3 + c][0, second].astype(F32)
                fs[first * STATES + second, c * plan.width : (c + 1) * plan.width, :] = jnp.where(
                    ok, block, 0.0
                ).astype(BF16)


def left_phase(plan, fs, ls, xs):
    def step(index, carry):
        p = index * 2
        both = jnp.concatenate([fs[p], fs[p + 1]], axis=1)
        done = jnp.dot(ls[...], both, preferred_element_type=F32)
        xs[p] = done[:, : plan.width]
        xs[p + 1] = done[:, plan.width :]
        return carry

    lax.fori_loop(0, PAIRS // 2, step, 0)


def middle_phase(plan, groups, xs, first_ref, second_ref, ys):
    pad = plan.w_pad
    first = first_ref[...]
    second = second_ref[...]

    def step(index, carry):
        middle = []
        for b in range(STATES):
            columns = []
            for one in range(2):
                start = pl.multiple_of((index * 2 + one) * pad, pad)
                columns.append(
                    jnp.concatenate([xs[a * STATES + b, pl.ds(start, pad), :] for a in range(STATES)], 0)
                )
            column = jnp.concatenate(columns, 1).astype(BF16)
            middle.append(jnp.dot(first, column, preferred_element_type=F32))
        for s1 in range(STATES):
            total = None
            for g in range(groups):
                at = g * plan.k + s1 * pad
                column = jnp.concatenate([z[at : at + pad] for z in middle], 0).astype(BF16)
                term = jnp.dot(second, column, preferred_element_type=F32)
                if groups > 1:
                    term = term.astype(BF16).astype(F32)
                total = term if total is None else total + term
            for s2 in range(STATES):
                for one in range(2):
                    ys[s1 * STATES + s2, pl.ds(index * 2 + one, plan.w, stride=plan.rows), :] = total[
                        s2 * pad : s2 * pad + plan.w, one * plan.width : (one + 1) * plan.width
                    ]
        return carry

    lax.fori_loop(0, plan.rows // 2, step, 0)


def right_phase(plan, split, ys, own_right, right_refs):
    me = lax.axis_index("mpo")
    result = [None] * PAIRS
    for n in range(plan.far + 1):
        members = [p for p, charge in enumerate(pair_charges()) if charge == n]
        total = None
        for r in range(plan.n_mpo):
            if n == 0:
                owner = r
                blocks = [own_right[owner * plan.w_here + t, 0] for t in range(plan.w_here)]
            else:
                owner = lax.bitwise_xor(me, r)
                blocks = [right_refs[r][(n - 1) * plan.w_here + t] for t in range(plan.w_here)]
            right = jnp.concatenate(blocks, 1)
            lines = []
            for p in members:
                parts = []
                for t in range(plan.w_here):
                    start = (owner * plan.w_here + t) * plan.rows
                    if n > 0:
                        start = pl.multiple_of(start, plan.rows)
                    parts.append(ys[p, pl.ds(start, plan.rows), :])
                lines.append(jnp.concatenate(parts, 1))
            field = jnp.concatenate(lines, 0)
            high = field.astype(BF16)
            if split:
                low = (field - high.astype(F32)).astype(BF16)
                high = jnp.concatenate([high, low], 0)
            term = lax.dot_general(high, right, NT, preferred_element_type=F32)
            total = term if total is None else total + term
        if split:
            half = total.shape[0] // 2
            total = total[:half] + total[half:]
        for place, p in enumerate(members):
            result[p] = total[place * plan.rows : (place + 1) * plan.rows]
    return result


def masked_rows(plan, left_ref, right_ref, result):
    me = lax.axis_index("mpo")
    here = lax.axis_index("bond")
    shape = (plan.rows, plan.width)
    row = lax.broadcasted_iota(jnp.int32, shape, 0) + me * plan.rows
    column = lax.broadcasted_iota(jnp.int32, shape, 1)
    row_ok = row < sector_limits(left_ref, here, plan.n_bond)
    blocks = []
    for p, charge in enumerate(pair_charges()):
        if result[p] is None:
            blocks.append(jnp.zeros(shape, BF16))
            continue
        ok = row_ok & (column < sector_limits(right_ref, here + charge, plan.n_bond))
        blocks.append(jnp.where(ok, result[p], 0.0).astype(BF16))
    return blocks


def whole_sum(values):
    return jnp.sum(jnp.sum(values, axis=1, keepdims=True), axis=0, keepdims=True)


def first_kernel(plan, *refs):
    charge_ref, left_ref, right_ref = refs[:3]
    psi_refs = refs[3 : 3 + 3 * plan.n_mpo]
    rest = refs[3 + 3 * plan.n_mpo :]
    own_left, rest = rest[0], rest[1:]
    piece_refs, rest = rest[: plan.n_mpo - 1], rest[plan.n_mpo - 1 :]
    first_ref, second_ref, ys, fs, ls, wide, xs = rest
    fill_left(plan, charge_ref, own_left, piece_refs, wide, ls)
    fill_vector(plan, left_ref, right_ref, psi_refs, fs)
    left_phase(plan, fs, ls, xs)
    middle_phase(plan, plan.n_mpo, xs, first_ref, second_ref, ys)


def image_kernel(plan, left_ref, right_ref, ys, fs, own_right, *refs):
    right_refs, (image, sums) = refs[: plan.n_mpo], refs[plan.n_mpo :]
    me = lax.axis_index("mpo")
    result = right_phase(plan, True, ys, own_right, right_refs)
    blocks = masked_rows(plan, left_ref, right_ref, result)
    rows_here = pl.ds(pl.multiple_of(me * plan.rows, plan.rows), plan.rows)
    along = jnp.zeros((plan.rows, plan.width), F32)
    norm = jnp.zeros((plan.rows, plan.width), F32)
    for p, block in enumerate(blocks):
        image[p] = block
        vector = fs[p, rows_here, :].astype(F32)
        along = along + vector * block.astype(F32)
        norm = norm + vector * vector
    along = whole_sum(along)
    norm = whole_sum(norm)
    ratio = jnp.where(norm > 0, along / jnp.where(norm > 0, norm, 1.0), 0.0)
    across = jnp.zeros((plan.rows, plan.width), F32)
    for p, block in enumerate(blocks):
        left_over = block.astype(F32) - ratio * fs[p, rows_here, :].astype(F32)
        across = across + left_over * left_over
    across = whole_sum(across)
    line = lax.broadcasted_iota(jnp.int32, sums.shape, 0)
    sums[...] = jnp.where(line == 0, along, jnp.where(line == 1, norm, jnp.where(line == 2, across, 0.0)))


def second_kernel(plan, count_all, *refs):
    left_ref, right_ref, sums = refs[:3]
    image_refs = refs[3 : 3 + 3 * plan.n_mpo]
    vector, ls, first_ref, second_ref, own_right = refs[3 + 3 * plan.n_mpo : 8 + 3 * plan.n_mpo]
    right_refs = refs[8 + 3 * plan.n_mpo : 8 + 4 * plan.n_mpo]
    out, fs, xs, ys = refs[8 + 4 * plan.n_mpo :]
    me = lax.axis_index("mpo")
    rayleigh = sums[0:1, :] / sums[1:2, :]
    scale = lax.rsqrt(sums[2:3, :] / count_all + EPSILON)
    for r in range(plan.n_mpo):
        start = lax.bitwise_xor(me, r) * plan.rows
        for c in range(3):
            where = pl.ds(pl.multiple_of(c * plan.width + start, plan.rows), plan.rows)
            for p in range(PAIRS):
                block = image_refs[r * 3 + c][p].astype(F32)
                residual = block - rayleigh * vector[p, where, :].astype(F32)
                fs[p, where, :] = (residual * scale).astype(BF16)
    left_phase(plan, fs, ls, xs)
    groups = first_ref.shape[0] // plan.k
    middle_phase(plan, groups, xs, first_ref, second_ref, ys)
    result = right_phase(plan, groups > 1, ys, own_right, right_refs)
    for p, block in enumerate(masked_rows(plan, left_ref, right_ref, result)):
        out[p] = block


VMEM = pl.BlockSpec(memory_space=pltpu.VMEM)
SMEM = pl.BlockSpec(memory_space=pltpu.SMEM)
PARAMS = pltpu.CompilerParams(vmem_limit_bytes=48 * 1024 * 1024)


def shape_of(shape, dtype):
    return jax.ShapeDtypeStruct(shape, dtype)


def shards(psi, left_env, right_env, site_one, site_two, mpo_charge, left_sizes, right_sizes):
    n_mpo = lax.axis_size("mpo")
    n_bond = lax.axis_size("bond")
    width = psi.shape[2]
    plan = Plan(n_mpo, n_bond, width, right_env.shape[0])
    me = lax.axis_index("mpo")

    neighbours = [psi, from_bond(psi, -1), from_bond(psi, 1)]
    by_sector = [spread(block) for block in neighbours]
    psi_pieces = [by_sector[c][r] for r in range(n_mpo) for c in range(3)]

    left_mine = left_env[:, 0]
    left_pieces = []
    for r in range(1, n_mpo):
        start = lax.bitwise_xor(me, r) * plan.rows
        left_pieces.append(from_mpo(lax.dynamic_slice_in_dim(left_mine, start, plan.rows, 1), r))

    quarter = lax.dynamic_slice_in_dim(right_env[:, 0], me * plan.w_here, plan.w_here, 0)
    right_far = jnp.concatenate([from_bond(quarter, d) for d in range(1, plan.far + 1)], 0)
    right_pieces = spread(right_far)

    pad = plan.w_pad - plan.w
    first = charge_allowed(site_one, mpo_charge, mpo_charge)
    first = jnp.transpose(first, (2, 1, 3, 0))
    first = jnp.pad(first, ((0, 0), (0, pad), (0, 0), (0, pad)))
    group_of = jnp.arange(plan.w_pad, dtype=jnp.int32) // plan.w_here
    groups = jnp.arange(n_mpo, dtype=jnp.int32)
    mine = (group_of[None, :] == groups[:, None])[:, None, None, None, :]
    first_wide = jnp.where(mine, first[None], jnp.zeros_like(first[None]))
    first_wide = first_wide.reshape(n_mpo * plan.k, plan.k)
    second = charge_allowed(site_two, mpo_charge, mpo_charge)
    second = jnp.transpose(second, (2, 1, 3, 0))
    second = jnp.pad(second, ((0, 0), (0, pad), (0, 0), (0, pad))).reshape(plan.k, plan.k)

    field_shape = (PAIRS, 3 * width, width)
    left_shape = (plan.rows * plan.w_pad, 3 * width)
    x_shape = (PAIRS, plan.rows * plan.w_pad, width)
    y_shape = (PAIRS, plan.rows * plan.w, width)
    row_shape = (PAIRS, plan.rows, width)

    ys, vector, left_rows = pl.pallas_call(
        functools.partial(first_kernel, plan),
        out_shape=(shape_of(y_shape, F32), shape_of(field_shape, BF16), shape_of(left_shape, BF16)),
        in_specs=[SMEM] * 3 + [VMEM] * (3 * n_mpo + n_mpo + 2),
        out_specs=(VMEM, VMEM, VMEM),
        scratch_shapes=[pltpu.VMEM((3, left_shape[0], width), F32), pltpu.VMEM(x_shape, F32)],
        compiler_params=PARAMS,
        name="states_of_vector",
    )(mpo_charge, left_sizes, right_sizes, *psi_pieces, left_mine, *left_pieces, first_wide, second)

    image_rows, sums = pl.pallas_call(
        functools.partial(image_kernel, plan),
        out_shape=(shape_of(row_shape, BF16), shape_of((8, width), F32)),
        in_specs=[SMEM] * 2 + [VMEM] * (3 + n_mpo),
        out_specs=(VMEM, VMEM),
        compiler_params=PARAMS,
        name="image_rows",
    )(left_sizes, right_sizes, ys, vector, right_env, *right_pieces)

    neighbours = [image_rows, from_bond(image_rows, -1), from_bond(image_rows, 1)]
    by_sector = [spread(block) for block in neighbours]
    image_pieces = [by_sector[c][r] for r in range(n_mpo) for c in range(3)]

    for bit in mpo_bits():
        sums = merged(sums, from_mpo(sums, bit))
    reach = 1
    while reach < n_bond:
        partner = [(i ^ reach, i) for i in range(n_bond)]
        sums = merged(sums, lax.ppermute(sums, "bond", partner))
        reach *= 2

    count_all = n_bond * PAIRS * width * width
    second_rows = pl.pallas_call(
        functools.partial(second_kernel, plan, float(count_all)),
        out_shape=shape_of(row_shape, BF16),
        in_specs=[SMEM] * 2 + [VMEM] * (1 + 3 * n_mpo + 5 + n_mpo),
        out_specs=VMEM,
        scratch_shapes=[
            pltpu.VMEM(field_shape, BF16),
            pltpu.VMEM(x_shape, F32),
            pltpu.VMEM(y_shape, F32),
        ],
        compiler_params=PARAMS,
        name="correction_image_rows",
    )(
        left_sizes, right_sizes, sums, *image_pieces, vector, left_rows, first_wide, second, right_env,
        *right_pieces,
    )

    image = jnp.zeros((STATES, width, width), BF16)
    for r in range(n_mpo):
        rows_of = lax.bitwise_xor(me, r)
        block = lax.dynamic_slice_in_dim(by_sector[0][r], me * STATES, STATES, 0)
        image = lax.dynamic_update_slice_in_dim(image, block, rows_of * plan.rows, 1)
    result = lax.all_to_all(
        second_rows.reshape(n_mpo, STATES, plan.rows, width), "mpo", 0, 0, tiled=False
    )
    result = jnp.transpose(result, (1, 0, 2, 3)).reshape(STATES, width, width)
    return (image[None], result[None])


def solution(mesh):
    in_specs = (
        P(("groups", "bond"), "mpo", None, None),
        P("mpo", ("groups", "bond"), None, None),
        P(None, ("groups", "bond"), None, None),
        P("groups", None, None, None),
        P("groups", None, None, None),
        P(),
        P("groups"),
        P("groups"),
    )
    out_specs = (P(("groups", "bond"), "mpo", None, None), P(("groups", "bond"), "mpo", None, None))
    return jax.shard_map(shards, mesh=mesh, in_specs=in_specs, out_specs=out_specs, check_vma=False)
```

```python
import functools

import jax
import jax.numpy as jnp
from jax import lax
from jax.experimental import pallas as pl
from jax.experimental.pallas import tpu as pltpu
from jax.sharding import PartitionSpec as P

EPSILON = 1e-06
STATE_CHARGES = (0, 1, 1, 2)
STATES = len(STATE_CHARGES)
PAIRS = STATES * STATES
RIM = 4
F32 = jnp.float32
BF16 = jnp.bfloat16
NT = (((1,), (1,)), ((), ()))


def pair_charges():
    return [left + right for left in STATE_CHARGES for right in STATE_CHARGES]


def round_up(value, step):
    return -(-value // step) * step


def charge_allowed(weight, row_charge, column_charge):
    local_charge = jnp.array(STATE_CHARGES, jnp.int32)
    charge_step = local_charge[:, None] - local_charge[None, :]
    bond_step = column_charge[None, :] - row_charge[:, None]
    allowed = charge_step[None, None, :, :] == bond_step[:, :, None, None]
    return jnp.where(allowed, weight, jnp.zeros_like(weight))


def from_near(value, step, flip):
    n_bond, n_mpo = lax.axis_size("bond"), lax.axis_size("mpo")
    pairs = [
        ((i + step) * n_mpo + (j ^ flip), i * n_mpo + j)
        for i in range(n_bond)
        for j in range(n_mpo)
        if 0 <= i + step < n_bond
    ]
    return lax.ppermute(value, ("bond", "mpo"), pairs)


def mpo_bits():
    count = lax.axis_size("mpo")
    bits = []
    while count > 1:
        count //= 2
        bits.append(count)
    return bits


def spread(value, steps):
    pieces = {(step, 0): from_near(value, step, 0) if step else value for step in steps}
    for bit in mpo_bits():
        pieces.update({(step, r ^ bit): from_near(piece, 0, bit) for (step, r), piece in list(pieces.items())})
    return pieces


def merged(parts):
    along = sum(part[0:1] for part in parts)
    norm = sum(part[1:2] for part in parts)
    ratio = jnp.where(norm > 0, along / jnp.where(norm > 0, norm, 1.0), 0.0)
    across = jnp.zeros_like(along)
    for part in parts:
        own = jnp.where(part[1:2] > 0, part[0:1] / jnp.where(part[1:2] > 0, part[1:2], 1.0), 0.0)
        gap = own - ratio
        across = across + part[2:3] + gap * gap * part[1:2]
    rest = jnp.zeros((parts[0].shape[0] - 3, parts[0].shape[1]), F32)
    return jnp.concatenate([along, norm, across, rest], 0)


def summed_over_bond(sums):
    n_bond = lax.axis_size("bond")
    reach, parts = 1, [sums]
    while reach < n_bond:
        if reach > 1:
            parts = [merged(parts)]
        radix = min(4, n_bond // reach)
        parts = parts + [
            lax.ppermute(parts[0], "bond", [(i ^ (reach * k), i) for i in range(n_bond)])
            for k in range(1, radix)
        ]
        reach *= radix
    return parts


def sector_limits(sizes_ref, sector, count):
    inside = (sector >= 0) & (sector < count)
    return jnp.where(inside, sizes_ref[jnp.clip(sector, 0, count - 1)], 0)


def state_charge(state):
    return (state + 1) // 2


class Plan:
    def __init__(self, n_mpo, n_bond, width, mpo_width):
        self.n_mpo = n_mpo
        self.n_bond = n_bond
        self.width = width
        self.w = mpo_width
        self.w_here = mpo_width // n_mpo
        self.w_pad = round_up(mpo_width, 8)
        self.rows = width // n_mpo
        self.k = STATES * self.w_pad
        self.y_step = self.rows + 8
        self.far = min(RIM, n_bond - 1)


def fill_left(plan, charge_ref, left_near, wide, ls):
    me = lax.axis_index("mpo")
    wide[...] = jnp.zeros_like(wide)
    for r in range(plan.n_mpo):
        owner = lax.bitwise_xor(me, r)
        for t in range(plan.w_here):
            w = owner * plan.w_here + t
            block = left_near[r, t].astype(F32)
            for c, charge in enumerate((0, 1, -1)):
                factor = jnp.where(charge_ref[w] == charge, 1.0, 0.0).astype(F32)
                wide[c, pl.ds(w, plan.rows, stride=plan.w_pad), :] = block * factor
    for c in range(3):
        ls[:, c * plan.width : (c + 1) * plan.width] = wide[c].astype(BF16)


def fill_vector(plan, left_ref, right_ref, psi_near, fs):
    me = lax.axis_index("mpo")
    here = lax.axis_index("bond")
    row = lax.broadcasted_iota(jnp.int32, (plan.width, plan.width), 0)
    column = lax.broadcasted_iota(jnp.int32, (plan.width, plan.width), 1)
    for c, step in enumerate((0, -1, 1)):
        sector = here + step
        row_ok = row < sector_limits(left_ref, sector, plan.n_bond)
        for r in range(plan.n_mpo):
            first = lax.bitwise_xor(me, r)
            for second in range(STATES):
                target = sector + state_charge(first) + STATE_CHARGES[second]
                ok = row_ok & (column < sector_limits(right_ref, target, plan.n_bond))
                block = psi_near[r * 3 + c, second].astype(F32)
                fs[first * STATES + second, c * plan.width : (c + 1) * plan.width, :] = jnp.where(
                    ok, block, 0.0
                ).astype(BF16)


def left_phase(plan, fs, ls, xs):
    def step(index, carry):
        p = index * 2
        both = jnp.concatenate([fs[p], fs[p + 1]], axis=1)
        done = jnp.dot(ls[...], both, preferred_element_type=F32)
        xs[p] = done[:, : plan.width]
        xs[p + 1] = done[:, plan.width :]
        return carry

    lax.fori_loop(0, PAIRS // 2, step, 0, unroll=2)


def middle_phase(plan, groups, xs, first_ref, second_ref, ys):
    pad = plan.w_pad
    first = first_ref[...]
    second = second_ref[...]

    def step(index, carry):
        middle = []
        for b in range(STATES):
            columns = []
            for one in range(2):
                start = pl.multiple_of((index * 2 + one) * pad, pad)
                columns.append(
                    jnp.concatenate([xs[a * STATES + b, pl.ds(start, pad), :] for a in range(STATES)], 0)
                )
            column = jnp.concatenate(columns, 1).astype(BF16)
            middle.append(jnp.dot(first, column, preferred_element_type=F32))
        for s1 in range(STATES):
            total = None
            for g in range(groups):
                at = g * plan.k + s1 * pad
                column = jnp.concatenate([z[at : at + pad] for z in middle], 0).astype(BF16)
                term = jnp.dot(second, column, preferred_element_type=F32)
                if groups > 1:
                    term = term.astype(BF16).astype(F32)
                total = term if total is None else total + term
            for s2 in range(STATES):
                for one in range(2):
                    ys[s1 * STATES + s2, pl.ds(index * 2 + one, plan.w, stride=plan.y_step), :] = total[
                        s2 * pad : s2 * pad + plan.w, one * plan.width : (one + 1) * plan.width
                    ]
        return carry

    lax.fori_loop(0, plan.rows // 2, step, 0, unroll=2)


def right_phase(plan, split, ys, right_near, ready):
    result = [None] * PAIRS
    for n in range(plan.far + 1):
        ready(n)
        members = [p for p, charge in enumerate(pair_charges()) if charge == n]
        total = None
        for first in range(0, plan.w, plan.w_here):
            group = range(first, first + plan.w_here)
            right = jnp.concatenate([right_near[n, u] for u in group], 1)
            lines = []
            for p in members:
                parts = [ys[p, pl.ds(u * plan.y_step, plan.rows), :] for u in group]
                lines.append(jnp.concatenate(parts, 1))
            field = jnp.concatenate(lines, 0)
            high = field.astype(BF16)
            if split:
                low = (field - high.astype(F32)).astype(BF16)
                high = jnp.concatenate([high, low], 0)
            term = lax.dot_general(high, right, NT, preferred_element_type=F32)
            total = term if total is None else total + term
        if split:
            half = total.shape[0] // 2
            total = total[:half] + total[half:]
        for place, p in enumerate(members):
            result[p] = total[place * plan.rows : (place + 1) * plan.rows]
    return result


def right_copies(plan, own_ref, far_refs, right_near, sems):
    half = plan.w // 2
    core = lax.rem(lax.axis_index("mpo"), 2)
    copies = [[pltpu.make_async_copy(own_ref.at[:, 0], right_near.at[0], sems.at[0])]]
    for d in range(1, plan.far + 1):
        pair = []
        for other in range(2):
            start = lax.bitwise_xor(core, other) * half
            place = 2 * (d - 1) + other
            pair.append(
                pltpu.make_async_copy(
                    far_refs[place], right_near.at[d, pl.ds(start, half)], sems.at[1 + place]
                )
            )
        copies.append(pair)
    return copies


def masked_rows(plan, left_ref, right_ref, result):
    me = lax.axis_index("mpo")
    here = lax.axis_index("bond")
    shape = (plan.rows, plan.width)
    row = lax.broadcasted_iota(jnp.int32, shape, 0) + me * plan.rows
    column = lax.broadcasted_iota(jnp.int32, shape, 1)
    row_ok = row < sector_limits(left_ref, here, plan.n_bond)
    blocks = []
    for p, charge in enumerate(pair_charges()):
        if result[p] is None:
            blocks.append(jnp.zeros(shape, BF16))
            continue
        ok = row_ok & (column < sector_limits(right_ref, here + charge, plan.n_bond))
        blocks.append(jnp.where(ok, result[p], 0.0).astype(BF16))
    return blocks


def whole_sum(values):
    return jnp.sum(jnp.sum(values, axis=1, keepdims=True), axis=0, keepdims=True)


def first_kernel(plan, *refs):
    charge_ref, left_ref, right_ref = refs[:3]
    psi_refs = refs[3 : 3 + 3 * plan.n_mpo]
    left_refs = refs[3 + 3 * plan.n_mpo : 3 + 4 * plan.n_mpo]
    first_ref, second_ref, ys, fs_out, ls_out, fs, ls, wide, xs, left_near, psi_near, left_sem, psi_sem, out_sem = refs[
        3 + 4 * plan.n_mpo :
    ]
    me = lax.axis_index("mpo")
    rows_here = pl.ds(pl.multiple_of(me * plan.rows, plan.rows), plan.rows)
    left_copies = []
    for r, source in enumerate(left_refs):
        source = source.at[:, rows_here, :] if r == 0 else source
        left_copies.append(pltpu.make_async_copy(source, left_near.at[r], left_sem.at[r]))
    psi_copies = [
        pltpu.make_async_copy(source, psi_near.at[pl.ds(place, 1)], psi_sem.at[place])
        for place, source in enumerate(psi_refs)
    ]
    for copy in left_copies + psi_copies:
        copy.start()
    for copy in left_copies:
        copy.wait()
    fill_left(plan, charge_ref, left_near, wide, ls)
    ls_copy = pltpu.make_async_copy(ls, ls_out, out_sem.at[0])
    ls_copy.start()
    for copy in psi_copies:
        copy.wait()
    fill_vector(plan, left_ref, right_ref, psi_near, fs)
    fs_copy = pltpu.make_async_copy(fs, fs_out, out_sem.at[1])
    fs_copy.start()
    left_phase(plan, fs, ls, xs)
    middle_phase(plan, plan.n_mpo, xs, first_ref, second_ref, ys)
    ls_copy.wait()
    fs_copy.wait()


def image_kernel(plan, left_ref, right_ref, ys_ref, vector_ref, own_ref, *refs):
    far_refs, (image, ys, right_near, vector, y_sem, right_sem, v_sem) = refs[: 2 * plan.far], refs[2 * plan.far :]
    me = lax.axis_index("mpo")
    rows_here = pl.ds(pl.multiple_of(me * plan.rows, plan.rows), plan.rows)
    charges = pair_charges()
    y_copies = {
        p: pltpu.make_async_copy(ys_ref.at[p], ys.at[p], y_sem.at[p]) for p in range(PAIRS) if charges[p] <= plan.far
    }
    r_copies = right_copies(plan, own_ref, far_refs, right_near, right_sem)
    v_copy = pltpu.make_async_copy(vector_ref.at[:, rows_here, :], vector, v_sem)
    for n in range(plan.far + 1):
        for copy in r_copies[n] + [y_copies[p] for p in range(PAIRS) if charges[p] == n]:
            copy.start()
    v_copy.start()

    def ready(n):
        for copy in r_copies[n] + [y_copies[p] for p in range(PAIRS) if charges[p] == n]:
            copy.wait()

    result = right_phase(plan, True, ys, right_near, ready)
    blocks = masked_rows(plan, left_ref, right_ref, result)
    v_copy.wait()
    along = jnp.zeros((plan.rows, plan.width), F32)
    norm = jnp.zeros((plan.rows, plan.width), F32)
    for p, block in enumerate(blocks):
        image[p] = block
        field = vector[p].astype(F32)
        along = along + field * block.astype(F32)
        norm = norm + field * field
    along = whole_sum(along)
    norm = whole_sum(norm)
    ratio = jnp.where(norm > 0, along / jnp.where(norm > 0, norm, 1.0), 0.0)
    across = jnp.zeros((plan.rows, plan.width), F32)
    for p, block in enumerate(blocks):
        left_over = block.astype(F32) - ratio * vector[p].astype(F32)
        across = across + left_over * left_over
    across = whole_sum(across)
    line = lax.broadcasted_iota(jnp.int32, (8, plan.width), 0)
    sums = jnp.where(line == 0, along, jnp.where(line == 1, norm, jnp.where(line == 2, across, 0.0)))
    parts = []
    for _ in range(3):
        parts.append(sums.astype(BF16).astype(F32))
        sums = sums - parts[-1]
    parts.append(jnp.zeros((plan.rows - 24, plan.width), F32))
    image[PAIRS] = jnp.concatenate(parts, 0).astype(BF16)


def sums_of(piece):
    block = piece[PAIRS].astype(F32)
    return block[0:8] + block[8:16] + block[16:24]


def second_kernel(plan, count_all, n_parts, *refs):
    left_ref, right_ref = refs[:2]
    parts, refs = refs[2 : 2 + n_parts], refs[2 + n_parts :]
    image_refs, refs = refs[: 3 * plan.n_mpo], refs[3 * plan.n_mpo :]
    vector_ref, ls_ref, first_ref, second_ref, own_ref = refs[:5]
    far_refs, refs = refs[5 : 5 + 2 * plan.far], refs[5 + 2 * plan.far :]
    out, fs, xs, ys, image_near, vector, ls, right_near, image_sem, field_sem, right_sem = refs
    me = lax.axis_index("mpo")
    image_copies = [
        pltpu.make_async_copy(source.at[pl.ds(0, PAIRS)], image_near.at[place], image_sem.at[place])
        for place, source in enumerate(image_refs)
    ]
    v_copy = pltpu.make_async_copy(vector_ref, vector, field_sem.at[0])
    l_copy = pltpu.make_async_copy(ls_ref, ls, field_sem.at[1])
    r_copies = right_copies(plan, own_ref, far_refs, right_near, right_sem)
    for copy in [v_copy] + image_copies + [l_copy] + [copy for some in r_copies for copy in some]:
        copy.start()
    sums = merged([part[...] for part in parts])
    rayleigh = sums[0:1, :] / sums[1:2, :]
    scale = lax.rsqrt(sums[2:3, :] / count_all + EPSILON)
    v_copy.wait()
    for r in range(plan.n_mpo):
        start = lax.bitwise_xor(me, r) * plan.rows
        for c in range(3):
            image_copies[r * 3 + c].wait()
            where = pl.ds(pl.multiple_of(c * plan.width + start, plan.rows), plan.rows)
            for p in range(PAIRS):
                block = image_near[r * 3 + c, p].astype(F32)
                residual = block - rayleigh * vector[p, where, :].astype(F32)
                fs[p, where, :] = (residual * scale).astype(BF16)
    l_copy.wait()
    left_phase(plan, fs, ls, xs)
    middle_phase(plan, 1, xs, first_ref, second_ref, ys)

    def ready(n):
        for copy in r_copies[n]:
            copy.wait()

    result = right_phase(plan, False, ys, right_near, ready)
    for p, block in enumerate(masked_rows(plan, left_ref, right_ref, result)):
        out[p] = block


COST_A = 12_000_000_000
COST_B = 4_000_000_000
VMEM = pl.BlockSpec(memory_space=pltpu.VMEM)
ANY = pl.BlockSpec(memory_space=pl.ANY)
SMEM = pl.BlockSpec(memory_space=pltpu.SMEM)
PARAMS = pltpu.CompilerParams(vmem_limit_bytes=60 * 1024 * 1024)


def shape_of(shape, dtype):
    return jax.ShapeDtypeStruct(shape, dtype)


def shards(psi, left_env, right_env, site_one, site_two, mpo_charge, left_sizes, right_sizes):
    n_mpo = lax.axis_size("mpo")
    n_bond = lax.axis_size("bond")
    width = psi.shape[2]
    plan = Plan(n_mpo, n_bond, width, right_env.shape[0])
    me = lax.axis_index("mpo")

    steps = (0, -1, 1)
    by_sector = spread(psi, steps)
    psi_pieces = [by_sector[step, r] for r in range(n_mpo) for step in steps]

    left_mine = left_env[:, 0]
    left_pieces = []
    for r in range(1, n_mpo):
        start = lax.bitwise_xor(me, r) * plan.rows
        left_pieces.append(from_near(lax.dynamic_slice_in_dim(left_mine, start, plan.rows, 1), 0, r))

    half = plan.w // 2
    here = lax.dynamic_slice_in_dim(right_env[:, 0], lax.rem(me, 2) * half, half, 0)
    right_far = []
    for d in range(1, plan.far + 1):
        here = from_near(here, 1, 0)
        right_far.append(here)
    pad = plan.w_pad - plan.w
    first = charge_allowed(site_one, mpo_charge, mpo_charge)
    first = jnp.transpose(first, (2, 1, 3, 0))
    first = jnp.pad(first, ((0, 0), (0, pad), (0, 0), (0, pad)))
    group_of = jnp.arange(plan.w_pad, dtype=jnp.int32) // plan.w_here
    groups = jnp.arange(n_mpo, dtype=jnp.int32)
    mine = (group_of[None, :] == groups[:, None])[:, None, None, None, :]
    first_whole = first.reshape(plan.k, plan.k)
    first_wide = jnp.where(mine, first[None], jnp.zeros_like(first[None]))
    first_wide = first_wide.reshape(n_mpo * plan.k, plan.k)
    second = charge_allowed(site_two, mpo_charge, mpo_charge)
    second = jnp.transpose(second, (2, 1, 3, 0))
    second = jnp.pad(second, ((0, 0), (0, pad), (0, 0), (0, pad))).reshape(plan.k, plan.k)

    field_shape = (PAIRS, 3 * width, width)
    left_shape = (plan.rows * plan.w_pad, 3 * width)
    x_shape = (PAIRS, plan.rows * plan.w_pad, width)
    y_shape = (PAIRS, plan.y_step * plan.w, width)
    row_shape = (PAIRS, plan.rows, width)

    ys, vector, left_rows = pl.pallas_call(
        functools.partial(first_kernel, plan),
        out_shape=(shape_of(y_shape, F32), shape_of(field_shape, BF16), shape_of(left_shape, BF16)),
        in_specs=[SMEM] * 3 + [ANY] * (4 * n_mpo) + [VMEM] * 2,
        out_specs=(VMEM, ANY, ANY),
        scratch_shapes=[
            pltpu.VMEM(field_shape, BF16),
            pltpu.VMEM(left_shape, BF16),
            pltpu.VMEM((3, left_shape[0], width), F32),
            pltpu.VMEM(x_shape, F32),
            pltpu.VMEM((n_mpo, plan.w_here, plan.rows, width), BF16),
            pltpu.VMEM((3 * n_mpo,) + psi.shape[1:], BF16),
            pltpu.SemaphoreType.DMA((n_mpo,)),
            pltpu.SemaphoreType.DMA((3 * n_mpo,)),
            pltpu.SemaphoreType.DMA((2,)),
        ],
        compiler_params=PARAMS,
        cost_estimate=pl.CostEstimate(flops=COST_A, bytes_accessed=0, transcendentals=0),
        name="states_of_vector",
    )(mpo_charge, left_sizes, right_sizes, *psi_pieces, left_mine, *left_pieces, first_wide, second)

    right_pieces = [piece for far in right_far for piece in (far, from_near(far, 0, 1))]
    right_scratch = pltpu.VMEM((plan.far + 1, plan.w, width, width), BF16)
    image_shape = (PAIRS + 1,) + row_shape[1:]
    image_rows = pl.pallas_call(
        functools.partial(image_kernel, plan),
        out_shape=shape_of(image_shape, BF16),
        in_specs=[SMEM] * 2 + [ANY] * (3 + 2 * plan.far),
        out_specs=VMEM,
        scratch_shapes=[
            pltpu.VMEM(y_shape, F32),
            right_scratch,
            pltpu.VMEM(row_shape, BF16),
            pltpu.SemaphoreType.DMA((PAIRS,)),
            pltpu.SemaphoreType.DMA((1 + 2 * plan.far,)),
            pltpu.SemaphoreType.DMA,
        ],
        compiler_params=PARAMS,
        cost_estimate=pl.CostEstimate(flops=COST_B, bytes_accessed=0, transcendentals=0),
        name="image_rows",
    )(left_sizes, right_sizes, ys, vector, right_env, *right_pieces)

    by_sector = spread(image_rows, steps)
    image_pieces = [by_sector[step, r] for r in range(n_mpo) for step in steps]
    sums = summed_over_bond(merged([sums_of(by_sector[0, r]) for r in range(n_mpo)]))

    count_all = n_bond * PAIRS * width * width
    second_rows = pl.pallas_call(
        functools.partial(second_kernel, plan, float(count_all), len(sums)),
        out_shape=shape_of(row_shape, BF16),
        in_specs=[SMEM] * 2 + [VMEM] * len(sums) + [ANY] * (3 * n_mpo + 2) + [VMEM] * 2 + [ANY] * (1 + 2 * plan.far),
        out_specs=VMEM,
        scratch_shapes=[
            pltpu.VMEM(field_shape, BF16),
            pltpu.VMEM(x_shape, F32),
            pltpu.VMEM(y_shape, F32),
            pltpu.VMEM((3 * n_mpo,) + row_shape, BF16),
            pltpu.VMEM(field_shape, BF16),
            pltpu.VMEM(left_shape, BF16),
            right_scratch,
            pltpu.SemaphoreType.DMA((3 * n_mpo,)),
            pltpu.SemaphoreType.DMA((2,)),
            pltpu.SemaphoreType.DMA((1 + 2 * plan.far,)),
        ],
        compiler_params=PARAMS,
        cost_estimate=pl.CostEstimate(flops=COST_A, bytes_accessed=0, transcendentals=0),
        name="correction_image_rows",
    )(
        left_sizes, right_sizes, *sums, *image_pieces, vector, left_rows, first_whole, second, right_env,
        *right_pieces,
    )

    image = jnp.zeros((STATES, width, width), BF16)
    for r in range(n_mpo):
        rows_of = lax.bitwise_xor(me, r)
        block = lax.dynamic_slice_in_dim(by_sector[0, r], me * STATES, STATES, 0)
        image = lax.dynamic_update_slice_in_dim(image, block, rows_of * plan.rows, 1)
    result = lax.all_to_all(
        second_rows.reshape(n_mpo, STATES, plan.rows, width), "mpo", 0, 0, tiled=False
    )
    result = jnp.transpose(result, (1, 0, 2, 3)).reshape(STATES, width, width)
    return (image[None], result[None])


def solution(mesh):
    in_specs = (
        P(("groups", "bond"), "mpo", None, None),
        P("mpo", ("groups", "bond"), None, None),
        P(None, ("groups", "bond"), None, None),
        P("groups", None, None, None),
        P("groups", None, None, None),
        P(),
        P("groups"),
        P("groups"),
    )
    out_specs = (P(("groups", "bond"), "mpo", None, None), P(("groups", "bond"), "mpo", None, None))
    return jax.shard_map(shards, mesh=mesh, in_specs=in_specs, out_specs=out_specs, check_vma=False)
```

```python
import functools

import jax
import jax.numpy as jnp
from jax import lax
from jax.experimental import pallas as pl
from jax.experimental.pallas import tpu as pltpu
from jax.sharding import PartitionSpec as P

EPSILON = 1e-06
STATE_CHARGES = (0, 1, 1, 2)
STATES = len(STATE_CHARGES)
PAIRS = STATES * STATES
RIM = 4
F32 = jnp.float32
BF16 = jnp.bfloat16
NT = (((1,), (1,)), ((), ()))


def pair_charges():
    return [left + right for left in STATE_CHARGES for right in STATE_CHARGES]


def round_up(value, step):
    return -(-value // step) * step


def from_near(value, step, flip):
    n_bond, n_mpo = lax.axis_size("bond"), lax.axis_size("mpo")
    pairs = [
        ((i + step) * n_mpo + (j ^ flip), i * n_mpo + j)
        for i in range(n_bond)
        for j in range(n_mpo)
        if 0 <= i + step < n_bond
    ]
    return lax.ppermute(value, ("bond", "mpo"), pairs)


def mpo_bits():
    count = lax.axis_size("mpo")
    bits = []
    while count > 1:
        count //= 2
        bits.append(count)
    return bits


def exchange(own, direct):
    n_bond, n_mpo = lax.axis_size("bond"), lax.axis_size("mpo")
    here = {0: own, 1: from_near(own, 0, 1)}
    both = jnp.stack([here[0], here[1]])
    pairs = [
        (i * n_mpo + j, (i + 1 - 2 * (j % 2)) * n_mpo + j)
        for i in range(n_bond)
        for j in range(n_mpo)
        if 0 <= i + 1 - 2 * (j % 2) < n_bond
    ]
    mine = {0: lax.ppermute(both, ("bond", "mpo"), pairs)}
    for bit in mpo_bits()[:-1]:
        for r in range(0, n_mpo, 2):
            if r in mine and r ^ bit not in mine:
                here[r ^ bit] = from_near(here[r], 0, bit)
                if direct:
                    cross = [(i, (j // n_mpo) * n_mpo + ((j % n_mpo) ^ bit)) for i, j in pairs]
                    mine[r ^ bit] = lax.ppermute(both, ("bond", "mpo"), cross)
                else:
                    mine[r ^ bit] = from_near(mine[r], 0, bit)
    for r in range(2, n_mpo, 2):
        here[r ^ 1] = from_near(here[r], 0, 1)
    other = {r: from_near(pair, 0, 1) for r, pair in mine.items()}
    return here, mine, other


def by_place(here, mine, other):
    evens = sorted(mine)
    return [here[r] for r in sorted(here)] + [mine[r] for r in evens] + [other[r] for r in evens]


def block_places(n_mpo):
    places = [(r, None, r, 0) for r in range(n_mpo)]
    for kind in (1, 2):
        for r in range(0, n_mpo, 2):
            array = n_mpo + (kind - 1) * (n_mpo // 2) + r // 2
            order = (r, r ^ 1) if kind == 1 else (r ^ 1, r)
            places += [(array, index, member, kind) for index, member in enumerate(order)]
    return places


def sector_of(kind):
    odd = lax.rem(lax.axis_index("mpo"), 2)
    if kind == 0:
        return 0, 0
    above = odd if kind == 1 else 1 - odd
    return 1 + above, 2 * above - 1


def right_exchange(own, far):
    n_bond, n_mpo = lax.axis_size("bond"), lax.axis_size("mpo")
    arrays = []
    for first in range(1, far + 1, 2):
        pairs = [
            ((i + first + j % 2) * n_mpo + j, i * n_mpo + j)
            for i in range(n_bond)
            for j in range(n_mpo)
            if first + j % 2 <= far and i + first + j % 2 < n_bond
        ]
        arrays.append(lax.ppermute(own, ("bond", "mpo"), pairs))
    return arrays


def handed_over(arrays, far):
    n_bond, n_mpo = lax.axis_size("bond"), lax.axis_size("mpo")
    result = []
    for place, array in enumerate(arrays):
        pairs = [
            (i * n_mpo + j, i * n_mpo + (j ^ 1))
            for i in range(n_bond)
            for j in range(n_mpo)
            if 1 + 2 * place + j % 2 <= far
        ]
        result += [array, lax.ppermute(array, ("bond", "mpo"), pairs)]
    return result


def merged(parts):
    along = sum(part[0:1] for part in parts)
    norm = sum(part[1:2] for part in parts)
    ratio = jnp.where(norm > 0, along / jnp.where(norm > 0, norm, 1.0), 0.0)
    across = jnp.zeros_like(along)
    for part in parts:
        own = jnp.where(part[1:2] > 0, part[0:1] / jnp.where(part[1:2] > 0, part[1:2], 1.0), 0.0)
        gap = own - ratio
        across = across + part[2:3] + gap * gap * part[1:2]
    rest = jnp.zeros((parts[0].shape[0] - 3, parts[0].shape[1]), F32)
    return jnp.concatenate([along, norm, across, rest], 0)


def summed_over_bond(sums):
    n_bond = lax.axis_size("bond")
    reach, parts = 1, [sums]
    while reach < n_bond:
        if reach > 1:
            parts = [merged(parts)]
        radix = min(4, n_bond // reach)
        parts = parts + [
            lax.ppermute(parts[0], "bond", [(i ^ (reach * k), i) for i in range(n_bond)])
            for k in range(1, radix)
        ]
        reach *= radix
    return parts


def sector_limits(sizes_ref, sector, count):
    inside = (sector >= 0) & (sector < count)
    return jnp.where(inside, sizes_ref[jnp.clip(sector, 0, count - 1)], 0)


def state_charge(state):
    return (state + 1) // 2


class Plan:
    def __init__(self, n_mpo, n_bond, width, mpo_width):
        self.n_mpo = n_mpo
        self.n_bond = n_bond
        self.width = width
        self.w = mpo_width
        self.w_here = mpo_width // n_mpo
        self.w_pad = round_up(mpo_width, 8)
        self.rows = width // n_mpo
        self.k = STATES * self.w_pad
        self.y_step = self.rows + 8
        self.far = min(RIM, n_bond - 1)
        self.n_far = 2 * ((self.far + 1) // 2)


def fill_left(plan, charge_ref, left_near, wide, ls):
    me = lax.axis_index("mpo")
    wide[...] = jnp.zeros_like(wide)
    for r in range(plan.n_mpo):
        owner = lax.bitwise_xor(me, r)
        for t in range(plan.w_here):
            w = owner * plan.w_here + t
            block = left_near[r, t].astype(F32)
            for c, charge in enumerate((0, 1, -1)):
                factor = jnp.where(charge_ref[w] == charge, 1.0, 0.0).astype(F32)
                wide[c, pl.ds(w, plan.rows, stride=plan.w_pad), :] = block * factor
    for c in range(3):
        ls[:, c * plan.width : (c + 1) * plan.width] = wide[c].astype(BF16)


def fill_vector(plan, left_ref, right_ref, psi_near, fs):
    me = lax.axis_index("mpo")
    here = lax.axis_index("bond")
    row = lax.broadcasted_iota(jnp.int32, (plan.width, plan.width), 0)
    column = lax.broadcasted_iota(jnp.int32, (plan.width, plan.width), 1)
    for place, (_, _, r, kind) in enumerate(block_places(plan.n_mpo)):
        slot, step = sector_of(kind)
        sector = here + step
        first = lax.bitwise_xor(me, r)
        row_ok = row < sector_limits(left_ref, sector, plan.n_bond)
        where = pl.ds(pl.multiple_of(slot * plan.width, plan.width), plan.width)
        for second in range(STATES):
            target = sector + state_charge(first) + STATE_CHARGES[second]
            ok = row_ok & (column < sector_limits(right_ref, target, plan.n_bond))
            block = psi_near[place, second].astype(F32)
            fs[first * STATES + second, where, :] = jnp.where(ok, block, 0.0).astype(BF16)


def left_phase(plan, fs, ls, xs):
    def step(index, carry):
        p = index * 2
        both = jnp.concatenate([fs[p], fs[p + 1]], axis=1)
        done = jnp.dot(ls[...], both, preferred_element_type=F32)
        xs[p] = done[:, : plan.width]
        xs[p + 1] = done[:, plan.width :]
        return carry

    lax.fori_loop(0, PAIRS // 2, step, 0, unroll=4)


def middle_phase(plan, groups, xs, sites_ref, ys):
    pad = plan.w_pad
    first = sites_ref[0]
    second = sites_ref[1]
    if groups > 1:
        column = lax.broadcasted_iota(jnp.int32, first.shape, 1)
        wide = first.astype(F32)
        rows = []
        for g in range(groups):
            ok = jnp.zeros(first.shape, jnp.bool_)
            for a in range(STATES):
                start = a * pad + g * plan.w_here
                ok = ok | ((column >= start) & (column < start + plan.w_here))
            rows.append(jnp.where(ok, wide, 0.0))
        first = jnp.concatenate(rows, 0).astype(BF16)

    def step(index, carry):
        middle = []
        for b in range(STATES):
            columns = []
            for one in range(2):
                start = pl.multiple_of((index * 2 + one) * pad, pad)
                columns.append(
                    jnp.concatenate([xs[a * STATES + b, pl.ds(start, pad), :] for a in range(STATES)], 0)
                )
            column = jnp.concatenate(columns, 1).astype(BF16)
            middle.append(jnp.dot(first, column, preferred_element_type=F32))
        for s1 in range(STATES):
            total = None
            for g in range(groups):
                at = g * plan.k + s1 * pad
                column = jnp.concatenate([z[at : at + pad] for z in middle], 0).astype(BF16)
                term = jnp.dot(second, column, preferred_element_type=F32)
                if groups > 1:
                    term = term.astype(BF16).astype(F32)
                total = term if total is None else total + term
            for s2 in range(STATES):
                for one in range(2):
                    ys[s1 * STATES + s2, pl.ds(index * 2 + one, plan.w, stride=plan.y_step), :] = total[
                        s2 * pad : s2 * pad + plan.w, one * plan.width : (one + 1) * plan.width
                    ]
        return carry

    lax.fori_loop(0, plan.rows // 2, step, 0, unroll=4)


def right_phase(plan, split, ys, right_near, ready):
    result = [None] * PAIRS
    for n in range(plan.far + 1):
        ready(n)
        members = [p for p, charge in enumerate(pair_charges()) if charge == n]
        total = None
        for first in range(0, plan.w, plan.w_here):
            group = range(first, first + plan.w_here)
            right = jnp.concatenate([right_near[n, u] for u in group], 1)
            lines = []
            for p in members:
                parts = [ys[p, pl.ds(u * plan.y_step, plan.rows), :] for u in group]
                lines.append(jnp.concatenate(parts, 1))
            field = jnp.concatenate(lines, 0)
            high = field.astype(BF16)
            if split:
                low = (field - high.astype(F32)).astype(BF16)
                high = jnp.concatenate([high, low], 0)
            term = lax.dot_general(high, right, NT, preferred_element_type=F32)
            total = term if total is None else total + term
        if split:
            half = total.shape[0] // 2
            total = total[:half] + total[half:]
        for place, p in enumerate(members):
            result[p] = total[place * plan.rows : (place + 1) * plan.rows]
    return result


def right_copies(plan, own_ref, far_refs, right_near, sems):
    odd = lax.rem(lax.axis_index("mpo"), 2)
    copies = [[] for _ in range(plan.far + 1)]
    copies[0].append(pltpu.make_async_copy(own_ref.at[:, 0], right_near.at[0], sems.at[0]))
    for place, source in enumerate(far_refs):
        first, other = 1 + 2 * (place // 2), place % 2
        slot = first + (1 - odd if other else odd)
        copies[first].append(pltpu.make_async_copy(source.at[:, 0], right_near.at[slot], sems.at[1 + place]))
    return copies


def masked_rows(plan, left_ref, right_ref, result):
    me = lax.axis_index("mpo")
    here = lax.axis_index("bond")
    shape = (plan.rows, plan.width)
    row = lax.broadcasted_iota(jnp.int32, shape, 0) + me * plan.rows
    column = lax.broadcasted_iota(jnp.int32, shape, 1)
    row_ok = row < sector_limits(left_ref, here, plan.n_bond)
    blocks = []
    for p, charge in enumerate(pair_charges()):
        if result[p] is None:
            blocks.append(jnp.zeros(shape, BF16))
            continue
        ok = row_ok & (column < sector_limits(right_ref, here + charge, plan.n_bond))
        blocks.append(jnp.where(ok, result[p], 0.0).astype(BF16))
    return blocks


def whole_sum(values):
    return jnp.sum(jnp.sum(values, axis=1, keepdims=True), axis=0, keepdims=True)


def near_copies(plan, refs, near, sems, count):
    copies = []
    for place, (array, index, _, _) in enumerate(block_places(plan.n_mpo)):
        source = refs[array] if index is None else refs[array].at[index]
        copies.append(pltpu.make_async_copy(source.at[pl.ds(0, count)], near.at[place], sems.at[place]))
    return copies


def first_kernel(plan, *refs):
    charge_ref, left_ref, right_ref = refs[:3]
    psi_refs = refs[3 : 3 + 2 * plan.n_mpo]
    left_refs = refs[3 + 2 * plan.n_mpo : 3 + 3 * plan.n_mpo]
    sites_ref, ys, fs_out, ls_out, fs, ls, wide, xs, left_near, psi_near, left_sem, psi_sem, out_sem = refs[
        3 + 3 * plan.n_mpo :
    ]
    me = lax.axis_index("mpo")
    rows_here = pl.ds(pl.multiple_of(me * plan.rows, plan.rows), plan.rows)
    left_copies = [
        pltpu.make_async_copy(source.at[:, rows_here, :], left_near.at[r], left_sem.at[r])
        for r, source in enumerate(left_refs)
    ]
    psi_copies = near_copies(plan, psi_refs, psi_near, psi_sem, STATES)
    for copy in left_copies + psi_copies:
        copy.start()
    for copy in left_copies:
        copy.wait()
    fill_left(plan, charge_ref, left_near, wide, ls)
    ls_copy = pltpu.make_async_copy(ls, ls_out, out_sem.at[0])
    ls_copy.start()
    for copy in psi_copies:
        copy.wait()
    fill_vector(plan, left_ref, right_ref, psi_near, fs)
    fs_copy = pltpu.make_async_copy(fs, fs_out, out_sem.at[1])
    fs_copy.start()
    left_phase(plan, fs, ls, xs)
    middle_phase(plan, plan.n_mpo, xs, sites_ref, ys)
    ls_copy.wait()
    fs_copy.wait()


def image_kernel(plan, left_ref, right_ref, ys_ref, vector_ref, own_ref, *refs):
    far_refs, (image, ys, right_near, vector, y_sem, right_sem, v_sem) = refs[: plan.n_far], refs[plan.n_far :]
    me = lax.axis_index("mpo")
    rows_here = pl.ds(pl.multiple_of(me * plan.rows, plan.rows), plan.rows)
    charges = pair_charges()
    y_copies = {
        p: pltpu.make_async_copy(ys_ref.at[p], ys.at[p], y_sem.at[p]) for p in range(PAIRS) if charges[p] <= plan.far
    }
    r_copies = right_copies(plan, own_ref, far_refs, right_near, right_sem)
    v_copy = pltpu.make_async_copy(vector_ref.at[:, rows_here, :], vector, v_sem)
    for n in range(plan.far + 1):
        for copy in r_copies[n] + [y_copies[p] for p in range(PAIRS) if charges[p] == n]:
            copy.start()
    v_copy.start()

    def ready(n):
        for copy in r_copies[n] + [y_copies[p] for p in range(PAIRS) if charges[p] == n]:
            copy.wait()

    result = right_phase(plan, True, ys, right_near, ready)
    blocks = masked_rows(plan, left_ref, right_ref, result)
    v_copy.wait()
    along = jnp.zeros((plan.rows, plan.width), F32)
    norm = jnp.zeros((plan.rows, plan.width), F32)
    for p, block in enumerate(blocks):
        image[p] = block
        field = vector[p].astype(F32)
        along = along + field * block.astype(F32)
        norm = norm + field * field
    along = whole_sum(along)
    norm = whole_sum(norm)
    ratio = jnp.where(norm > 0, along / jnp.where(norm > 0, norm, 1.0), 0.0)
    across = jnp.zeros((plan.rows, plan.width), F32)
    for p, block in enumerate(blocks):
        left_over = block.astype(F32) - ratio * vector[p].astype(F32)
        across = across + left_over * left_over
    across = whole_sum(across)
    line = lax.broadcasted_iota(jnp.int32, (8, plan.width), 0)
    sums = jnp.where(line == 0, along, jnp.where(line == 1, norm, jnp.where(line == 2, across, 0.0)))
    parts = []
    for _ in range(3):
        parts.append(sums.astype(BF16).astype(F32))
        sums = sums - parts[-1]
    parts.append(jnp.zeros((plan.rows - 24, plan.width), F32))
    image[PAIRS] = jnp.concatenate(parts, 0).astype(BF16)


def sums_of(piece):
    block = piece[PAIRS].astype(F32)
    return block[0:8] + block[8:16] + block[16:24]


def second_kernel(plan, count_all, n_parts, *refs):
    left_ref, right_ref = refs[:2]
    parts, refs = refs[2 : 2 + n_parts], refs[2 + n_parts :]
    image_refs, refs = refs[: 2 * plan.n_mpo], refs[2 * plan.n_mpo :]
    vector_ref, ls_ref, sites_ref, own_ref = refs[:4]
    far_refs, refs = refs[4 : 4 + plan.n_far], refs[4 + plan.n_far :]
    outs, image_out = refs[: plan.n_mpo], refs[plan.n_mpo]
    fs, xs, ys, image_near, vector, ls, right_near, image_sem, field_sem, right_sem, out_sem = refs[plan.n_mpo + 1 :]
    me = lax.axis_index("mpo")
    image_copies = near_copies(plan, image_refs, image_near, image_sem, PAIRS)
    v_copy = pltpu.make_async_copy(vector_ref, vector, field_sem.at[0])
    l_copy = pltpu.make_async_copy(ls_ref, ls, field_sem.at[1])
    r_copies = right_copies(plan, own_ref, far_refs, right_near, right_sem)
    for copy in [v_copy] + image_copies + [l_copy] + [copy for some in r_copies for copy in some]:
        copy.start()
    sums = merged([part[...] for part in parts])
    rayleigh = sums[0:1, :] / sums[1:2, :]
    scale = lax.rsqrt(sums[2:3, :] / count_all + EPSILON)
    v_copy.wait()
    for place, (_, _, r, kind) in enumerate(block_places(plan.n_mpo)):
        image_copies[place].wait()
        slot, _ = sector_of(kind)
        start = slot * plan.width + lax.bitwise_xor(me, r) * plan.rows
        where = pl.ds(pl.multiple_of(start, plan.rows), plan.rows)
        for p in range(PAIRS):
            block = image_near[place, p].astype(F32)
            residual = block - rayleigh * vector[p, where, :].astype(F32)
            fs[p, where, :] = (residual * scale).astype(BF16)
    out_copies = []
    pairs_here = pl.ds(me * STATES, STATES)
    for place, (_, _, r, kind) in enumerate(block_places(plan.n_mpo)):
        if kind == 0:
            start = lax.bitwise_xor(me, r) * plan.rows
            rows = pl.ds(pl.multiple_of(start, plan.rows), plan.rows)
            out_copies.append(
                pltpu.make_async_copy(image_near.at[place, pairs_here], image_out.at[0, :, rows, :], out_sem.at[r])
            )
    for copy in out_copies:
        copy.start()
    l_copy.wait()
    left_phase(plan, fs, ls, xs)
    middle_phase(plan, 1, xs, sites_ref, ys)

    def ready(n):
        for copy in r_copies[n]:
            copy.wait()

    result = right_phase(plan, False, ys, right_near, ready)
    rows = masked_rows(plan, left_ref, right_ref, result)
    for p in range(PAIRS):
        ys[p, : plan.rows, :] = rows[p].astype(F32)
    for r, out in enumerate(outs):
        first = lax.bitwise_xor(me, r) * STATES
        for second in range(STATES):
            out[second] = ys[first + second, : plan.rows, :].astype(BF16)
    for copy in out_copies:
        copy.wait()


COST_A = 2_000_000_000
COST_B = 4_000_000_000
VMEM = pl.BlockSpec(memory_space=pltpu.VMEM)
ANY = pl.BlockSpec(memory_space=pl.ANY)
SMEM = pl.BlockSpec(memory_space=pltpu.SMEM)
PARAMS = pltpu.CompilerParams(vmem_limit_bytes=60 * 1024 * 1024)


def shape_of(shape, dtype):
    return jax.ShapeDtypeStruct(shape, dtype)


def shards(psi, left_env, right_env, site_one, site_two, mpo_charge, left_sizes, right_sizes):
    n_mpo = lax.axis_size("mpo")
    n_bond = lax.axis_size("bond")
    width = psi.shape[2]
    plan = Plan(n_mpo, n_bond, width, right_env.shape[0])
    me = lax.axis_index("mpo")

    psi_here, psi_mine, psi_other = exchange(psi[0], False)

    left_mine = left_env[:, 0]
    left_here = {0: left_mine}
    for bit in mpo_bits():
        left_here.update({r ^ bit: from_near(block, 0, bit) for r, block in list(left_here.items())})
    left_pieces = [left_here[r] for r in range(n_mpo)]

    right_far = right_exchange(right_env, plan.far)

    pad = plan.w_pad - plan.w
    charge_step = jnp.array(STATE_CHARGES, jnp.int32)
    charge_step = charge_step[:, None, None, None] - charge_step[None, None, :, None]
    bond_step = mpo_charge[None, :, None, None] - mpo_charge[None, None, None, :]
    sites = jnp.transpose(jnp.stack([site_one, site_two]), (0, 3, 2, 4, 1))
    sites = jnp.where((charge_step == bond_step)[None], sites, jnp.zeros_like(sites))
    sites = jnp.pad(sites, ((0, 0), (0, 0), (0, pad), (0, 0), (0, pad))).reshape(2, plan.k, plan.k)

    field_shape = (PAIRS, 3 * width, width)
    left_shape = (plan.rows * plan.w_pad, 3 * width)
    x_shape = (PAIRS, plan.rows * plan.w_pad, width)
    y_shape = (PAIRS, plan.y_step * plan.w, width)
    row_shape = (PAIRS, plan.rows, width)

    ys, vector, left_rows = pl.pallas_call(
        functools.partial(first_kernel, plan),
        out_shape=(shape_of(y_shape, F32), shape_of(field_shape, BF16), shape_of(left_shape, BF16)),
        in_specs=[SMEM] * 3 + [ANY] * (3 * n_mpo) + [VMEM],
        out_specs=(VMEM, ANY, ANY),
        scratch_shapes=[
            pltpu.VMEM(field_shape, BF16),
            pltpu.VMEM(left_shape, BF16),
            pltpu.VMEM((3, left_shape[0], width), F32),
            pltpu.VMEM(x_shape, F32),
            pltpu.VMEM((n_mpo, plan.w_here, plan.rows, width), BF16),
            pltpu.VMEM((3 * n_mpo,) + psi.shape[1:], BF16),
            pltpu.SemaphoreType.DMA((n_mpo,)),
            pltpu.SemaphoreType.DMA((3 * n_mpo,)),
            pltpu.SemaphoreType.DMA((2,)),
        ],
        compiler_params=PARAMS,
        cost_estimate=pl.CostEstimate(flops=COST_A, bytes_accessed=0, transcendentals=0),
        name="states_of_vector",
    )(
        mpo_charge, left_sizes, right_sizes, *by_place(psi_here, psi_mine, psi_other), *left_pieces, sites,
    )

    right_far, ys = lax.optimization_barrier((right_far, ys))
    right_pieces = handed_over(right_far, plan.far)
    right_scratch = pltpu.VMEM((plan.n_far + 1, plan.w, width, width), BF16)
    image_shape = (PAIRS + 1,) + row_shape[1:]
    image_rows = pl.pallas_call(
        functools.partial(image_kernel, plan),
        out_shape=shape_of(image_shape, BF16),
        in_specs=[SMEM] * 2 + [ANY] * (3 + plan.n_far),
        out_specs=VMEM,
        scratch_shapes=[
            pltpu.VMEM(y_shape, F32),
            right_scratch,
            pltpu.VMEM(row_shape, BF16),
            pltpu.SemaphoreType.DMA((PAIRS,)),
            pltpu.SemaphoreType.DMA((1 + plan.n_far,)),
            pltpu.SemaphoreType.DMA,
        ],
        compiler_params=PARAMS,
        cost_estimate=pl.CostEstimate(flops=COST_B, bytes_accessed=0, transcendentals=0),
        name="image_rows",
    )(left_sizes, right_sizes, ys, vector, right_env, *right_pieces)

    image_here, image_mine, image_other = exchange(image_rows, True)
    blocks, _ = lax.optimization_barrier((image_here, image_mine[0]))
    sums = summed_over_bond(merged([sums_of(blocks[r]) for r in range(n_mpo)]))

    count_all = n_bond * PAIRS * width * width
    *second_rows, image = pl.pallas_call(
        functools.partial(second_kernel, plan, float(count_all), len(sums)),
        out_shape=(shape_of((STATES,) + row_shape[1:], BF16),) * n_mpo + (shape_of(psi.shape, BF16),),
        in_specs=[SMEM] * 2 + [VMEM] * len(sums) + [ANY] * (2 * n_mpo + 2) + [VMEM] + [ANY] * (1 + plan.n_far),
        out_specs=(VMEM,) * n_mpo + (ANY,),
        scratch_shapes=[
            pltpu.VMEM(field_shape, BF16),
            pltpu.VMEM(x_shape, F32),
            pltpu.VMEM(y_shape, F32),
            pltpu.VMEM((3 * n_mpo,) + row_shape, BF16),
            pltpu.VMEM(field_shape, BF16),
            pltpu.VMEM(left_shape, BF16),
            right_scratch,
            pltpu.SemaphoreType.DMA((3 * n_mpo,)),
            pltpu.SemaphoreType.DMA((2,)),
            pltpu.SemaphoreType.DMA((1 + plan.n_far,)),
            pltpu.SemaphoreType.DMA((n_mpo,)),
        ],
        compiler_params=PARAMS,
        cost_estimate=pl.CostEstimate(flops=COST_A, bytes_accessed=0, transcendentals=0),
        name="correction_image_rows",
    )(
        left_sizes, right_sizes, *sums, *by_place(image_here, image_mine, image_other), vector, left_rows, sites,
        right_env, *right_pieces,
    )

    result = jnp.zeros((STATES, width, width), BF16)
    for r, block in enumerate(second_rows):
        block = from_near(block, 0, r) if r else block
        start = lax.bitwise_xor(me, r) * plan.rows
        result = lax.dynamic_update_slice_in_dim(result, block, start, 1)
    return (image, result[None])


def solution(mesh):
    in_specs = (
        P(("groups", "bond"), "mpo", None, None),
        P("mpo", ("groups", "bond"), None, None),
        P(None, ("groups", "bond"), None, None),
        P("groups", None, None, None),
        P("groups", None, None, None),
        P(),
        P("groups"),
        P("groups"),
    )
    out_specs = (P(("groups", "bond"), "mpo", None, None), P(("groups", "bond"), "mpo", None, None))
    return jax.shard_map(shards, mesh=mesh, in_specs=in_specs, out_specs=out_specs, check_vma=False)
```

```python
import functools

import jax
import jax.numpy as jnp
from jax import lax
from jax.experimental import pallas as pl
from jax.experimental.pallas import tpu as pltpu
from jax.sharding import PartitionSpec as P

EPSILON = 1e-06
STATE_CHARGES = (0, 1, 1, 2)
STATES = len(STATE_CHARGES)
PAIRS = STATES * STATES
RIM = 4
F32 = jnp.float32
BF16 = jnp.bfloat16
NT = (((1,), (1,)), ((), ()))


def pair_charges():
    return [left + right for left in STATE_CHARGES for right in STATE_CHARGES]


def round_up(value, step):
    return -(-value // step) * step


def from_near(value, step, flip):
    n_bond, n_mpo = lax.axis_size("bond"), lax.axis_size("mpo")
    pairs = [
        ((i + step) * n_mpo + (j ^ flip), i * n_mpo + j)
        for i in range(n_bond)
        for j in range(n_mpo)
        if 0 <= i + step < n_bond
    ]
    return lax.ppermute(value, ("bond", "mpo"), pairs)


def mpo_bits():
    count = lax.axis_size("mpo")
    bits = []
    while count > 1:
        count //= 2
        bits.append(count)
    return bits


def exchange(own, cross_last):
    n_bond, n_mpo = lax.axis_size("bond"), lax.axis_size("mpo")
    pairs = [
        (i * n_mpo + j, (i + 1 - 2 * (j % 2)) * n_mpo + j)
        for i in range(n_bond)
        for j in range(n_mpo)
        if 0 <= i + 1 - 2 * (j % 2) < n_bond
    ]
    here = {0: own, 1: from_near(own, 0, 1)}
    for bit in mpo_bits()[:-1]:
        here.update({r ^ bit: from_near(here[r], 0, bit) for r in sorted(here) if r % 2 == 0})
    for r in range(2, n_mpo, 2):
        here[r ^ 1] = from_near(here[r], 0, 1)
    mine = {}
    for r in range(0, n_mpo, 2):
        if r == 0 or not cross_last:
            mine[r] = lax.ppermute(jnp.stack([here[r], here[r ^ 1]]), ("bond", "mpo"), pairs)
    if cross_last:
        for bit in mpo_bits()[:-1]:
            mine.update({r ^ bit: from_near(pair, 0, bit) for r, pair in list(mine.items())})
    return here, mine


def handed_pairs(mine):
    return {r: from_near(pair, 0, 1) for r, pair in mine.items()}


def by_place(here, mine, other):
    evens = sorted(mine)
    return [here[r] for r in sorted(here)] + [mine[r] for r in evens] + [other[r] for r in evens]


def block_places(n_mpo):
    places = [(r, None, r, 0) for r in range(n_mpo)]
    for kind in (1, 2):
        for r in range(0, n_mpo, 2):
            array = n_mpo + (kind - 1) * (n_mpo // 2) + r // 2
            order = (r, r ^ 1) if kind == 1 else (r ^ 1, r)
            places += [(array, index, member, kind) for index, member in enumerate(order)]
    return places


def sector_of(kind):
    odd = lax.rem(lax.axis_index("mpo"), 2)
    if kind == 0:
        return 0, 0
    above = odd if kind == 1 else 1 - odd
    return 1 + above, 2 * above - 1


def right_exchange(own, far):
    n_bond, n_mpo = lax.axis_size("bond"), lax.axis_size("mpo")
    arrays = []
    for first in range(1, far + 1, 2):
        pairs = [
            ((i + first + j % 2) * n_mpo + j, i * n_mpo + j)
            for i in range(n_bond)
            for j in range(n_mpo)
            if first + j % 2 <= far and i + first + j % 2 < n_bond
        ]
        arrays.append(lax.ppermute(own, ("bond", "mpo"), pairs))
    return arrays


def handed_over(arrays, far):
    n_bond, n_mpo = lax.axis_size("bond"), lax.axis_size("mpo")
    result = []
    for place, array in enumerate(arrays):
        pairs = [
            (i * n_mpo + j, i * n_mpo + (j ^ 1))
            for i in range(n_bond)
            for j in range(n_mpo)
            if 1 + 2 * place + j % 2 <= far
        ]
        result += [array, lax.ppermute(array, ("bond", "mpo"), pairs)]
    return result


def merged(parts):
    along = sum(part[0:1] for part in parts)
    norm = sum(part[1:2] for part in parts)
    ratio = jnp.where(norm > 0, along / jnp.where(norm > 0, norm, 1.0), 0.0)
    across = jnp.zeros_like(along)
    for part in parts:
        own = jnp.where(part[1:2] > 0, part[0:1] / jnp.where(part[1:2] > 0, part[1:2], 1.0), 0.0)
        gap = own - ratio
        across = across + part[2:3] + gap * gap * part[1:2]
    rest = jnp.zeros((parts[0].shape[0] - 3, parts[0].shape[1]), F32)
    return jnp.concatenate([along, norm, across, rest], 0)


def summed_over_bond(sums):
    n_bond = lax.axis_size("bond")
    reach, parts = 1, [sums]
    while reach < n_bond:
        if reach > 1:
            parts = [merged(parts)]
        radix = min(4, n_bond // reach)
        parts = parts + [
            lax.ppermute(parts[0], "bond", [(i ^ (reach * k), i) for i in range(n_bond)])
            for k in range(1, radix)
        ]
        reach *= radix
    return parts


def sector_limits(sizes_ref, sector, count):
    inside = (sector >= 0) & (sector < count)
    return jnp.where(inside, sizes_ref[jnp.clip(sector, 0, count - 1)], 0)


def state_charge(state):
    return (state + 1) // 2


class Plan:
    def __init__(self, n_mpo, n_bond, width, mpo_width):
        self.n_mpo = n_mpo
        self.n_bond = n_bond
        self.width = width
        self.w = mpo_width
        self.w_here = mpo_width // n_mpo
        self.w_pad = round_up(mpo_width, 8)
        self.rows = width // n_mpo
        self.y_step = self.rows + 8
        self.far = min(RIM, n_bond - 1)
        self.n_far = 2 * ((self.far + 1) // 2)


def fill_left(plan, charge_ref, left_near, wide, ls):
    me = lax.axis_index("mpo")
    wide[...] = jnp.zeros_like(wide)
    for r in range(plan.n_mpo):
        owner = lax.bitwise_xor(me, r)
        for t in range(plan.w_here):
            w = owner * plan.w_here + t
            block = left_near[r, t].astype(F32)
            for c, charge in enumerate((0, 1, -1)):
                factor = jnp.where(charge_ref[w] == charge, 1.0, 0.0).astype(F32)
                wide[c, pl.ds(w, plan.rows, stride=plan.w_pad), :] = block * factor
    for c in range(3):
        ls[:, c * plan.width : (c + 1) * plan.width] = wide[c].astype(BF16)


def fill_vector(plan, left_ref, right_ref, psi_near, fs):
    me = lax.axis_index("mpo")
    here = lax.axis_index("bond")
    row = lax.broadcasted_iota(jnp.int32, (plan.width, plan.width), 0)
    column = lax.broadcasted_iota(jnp.int32, (plan.width, plan.width), 1)
    for place, (_, _, r, kind) in enumerate(block_places(plan.n_mpo)):
        slot, step = sector_of(kind)
        sector = here + step
        first = lax.bitwise_xor(me, r)
        row_ok = row < sector_limits(left_ref, sector, plan.n_bond)
        where = pl.ds(pl.multiple_of(slot * plan.width, plan.width), plan.width)
        for second in range(STATES):
            target = sector + state_charge(first) + STATE_CHARGES[second]
            ok = row_ok & (column < sector_limits(right_ref, target, plan.n_bond))
            block = psi_near[place, second].astype(F32)
            fs[first * STATES + second, where, :] = jnp.where(ok, block, 0.0).astype(BF16)


def left_phase(plan, fs, ls, xs):
    def step(index, carry):
        p = index * 2
        both = jnp.concatenate([fs[p], fs[p + 1]], axis=1)
        done = jnp.dot(ls[...], both, preferred_element_type=F32)
        xs[p] = done[:, : plan.width]
        xs[p + 1] = done[:, plan.width :]
        return carry

    lax.fori_loop(0, PAIRS // 2, step, 0, unroll=4)


def site_matrices(plan, charge_ref, sites_ref, first_out, second_out):
    w, pad = plan.w, plan.w_pad
    size = STATES * w

    def index(shape, axis):
        return lax.broadcasted_iota(jnp.int32, shape, axis)

    def charges(bond):
        total = jnp.zeros(bond.shape, jnp.int32)
        for v in range(w):
            total = jnp.where(bond == v, charge_ref[v], total)
        return total

    row, column = index((size, size), 0), index((size, size), 1)
    local_step = state_charge(row // w) - state_charge(column // w)
    allowed = local_step == charges(row % w) - charges(column % w)
    first = jnp.where(allowed, sites_ref[0].astype(F32), 0.0).astype(BF16)
    second = jnp.where(allowed, sites_ref[1].astype(F32), 0.0).astype(BF16)

    into = (size, STATES * pad)
    spread_w = (index(into, 0) // w == index(into, 1) // pad) & (index(into, 0) % w == index(into, 1) % pad)
    first = jnp.dot(first, jnp.where(spread_w, 1.0, 0.0).astype(BF16), preferred_element_type=F32)
    first_out[...] = first.astype(BF16)

    into = (size, 2 * size)
    of, to = index(into, 0), index(into, 1)
    halves = []
    for k in range(2):
        spread_v = to == (of // w) * 2 * w + k * w + of % w
        halves.append(jnp.dot(second, jnp.where(spread_v, 1.0, 0.0).astype(BF16), preferred_element_type=F32))
    second_out[...] = jnp.concatenate(halves, 0).astype(BF16)


def middle_phase(plan, groups, block, unroll, xs, first_ref, second_ref, ys, done):
    w, pad = plan.w, plan.w_pad
    first = first_ref[...]
    second = second_ref[...]
    size = STATES * w
    if groups > 1:
        column = lax.broadcasted_iota(jnp.int32, first.shape, 1) % pad
        wide = first.astype(F32)
        rows = []
        for g in range(groups):
            ok = (column >= g * plan.w_here) & (column < (g + 1) * plan.w_here)
            rows.append(jnp.where(ok, wide, 0.0))
        first = jnp.concatenate(rows, 0).astype(BF16)

    def step(index, carry):
        middle = []
        for b in range(STATES):
            columns = []
            for one in range(block):
                start = pl.multiple_of((index * block + one) * pad, pad)
                columns.append(
                    jnp.concatenate([xs[a * STATES + b, pl.ds(start, pad), :] for a in range(STATES)], 0)
                )
            column = jnp.concatenate(columns, 1).astype(BF16)
            middle.append(jnp.dot(first, column, preferred_element_type=F32))
        for half in range(STATES // 2):
            total = None
            for g in range(groups):
                at = g * size + half * 2 * w
                column = jnp.concatenate([z[at : at + 2 * w] for z in middle], 0).astype(BF16)
                term = jnp.dot(second, column, preferred_element_type=F32)
                if groups > 1:
                    term = term.astype(BF16).astype(F32)
                total = term if total is None else total + term
            for k in range(2):
                for s2 in range(STATES):
                    at = k * size + s2 * w
                    for one in range(block):
                        rows = pl.ds(index * block + one, w, stride=plan.y_step)
                        ys[(2 * half + k) * STATES + s2, rows, :] = total[
                            at : at + w, one * plan.width : (one + 1) * plan.width
                        ]
        done(index)
        return carry

    lax.fori_loop(0, plan.rows // block, step, 0, unroll=unroll)


def right_phase(plan, split, ys, y_step, right_near, ready):
    result = [None] * PAIRS
    for n in range(plan.far + 1):
        ready(n)
        members = [p for p, charge in enumerate(pair_charges()) if charge == n]
        total = None
        for first in range(0, plan.w, plan.w_here):
            group = range(first, first + plan.w_here)
            right = jnp.concatenate([right_near[n, u] for u in group], 1)
            lines = []
            for p in members:
                parts = [ys[p, pl.ds(u * y_step, plan.rows), :] for u in group]
                lines.append(jnp.concatenate(parts, 1))
            field = jnp.concatenate(lines, 0)
            high = field.astype(BF16)
            if split:
                low = (field - high.astype(F32)).astype(BF16)
                high = jnp.concatenate([high, low], 0)
            term = lax.dot_general(high, right, NT, preferred_element_type=F32)
            total = term if total is None else total + term
        if split:
            half = total.shape[0] // 2
            total = total[:half] + total[half:]
        for place, p in enumerate(members):
            result[p] = total[place * plan.rows : (place + 1) * plan.rows]
    return result


def right_copies(plan, own_ref, far_refs, right_near, sems):
    odd = lax.rem(lax.axis_index("mpo"), 2)
    copies = [[] for _ in range(plan.far + 1)]
    copies[0].append(pltpu.make_async_copy(own_ref.at[:, 0], right_near.at[0], sems.at[0]))
    for place, source in enumerate(far_refs):
        first, other = 1 + 2 * (place // 2), place % 2
        slot = first + (1 - odd if other else odd)
        copies[first].append(pltpu.make_async_copy(source.at[:, 0], right_near.at[slot], sems.at[1 + place]))
    return copies


def masked_rows(plan, left_ref, right_ref, result):
    me = lax.axis_index("mpo")
    here = lax.axis_index("bond")
    shape = (plan.rows, plan.width)
    row = lax.broadcasted_iota(jnp.int32, shape, 0) + me * plan.rows
    column = lax.broadcasted_iota(jnp.int32, shape, 1)
    row_ok = row < sector_limits(left_ref, here, plan.n_bond)
    blocks = []
    for p, charge in enumerate(pair_charges()):
        if result[p] is None:
            blocks.append(jnp.zeros(shape, BF16))
            continue
        ok = row_ok & (column < sector_limits(right_ref, here + charge, plan.n_bond))
        blocks.append(jnp.where(ok, result[p], 0.0).astype(BF16))
    return blocks


def whole_sum(values):
    return jnp.sum(jnp.sum(values, axis=1, keepdims=True), axis=0, keepdims=True)


def near_copies(plan, refs, near, sems, count):
    copies = []
    for place, (array, index, _, _) in enumerate(block_places(plan.n_mpo)):
        source = refs[array] if index is None else refs[array].at[index]
        copies.append(pltpu.make_async_copy(source.at[pl.ds(0, count)], near.at[place], sems.at[place]))
    return copies


def first_kernel(plan, *refs):
    charge_ref, left_ref, right_ref = refs[:3]
    psi_refs = refs[3 : 3 + 2 * plan.n_mpo]
    left_refs = refs[3 + 2 * plan.n_mpo : 3 + 3 * plan.n_mpo]
    refs = refs[3 + 3 * plan.n_mpo :]
    sites_ref, ys_out, fs_out, ls_out, first_out, second_out = refs[:6]
    fs, ls, wide, xs, ys, left_near, psi_near, left_sem, psi_sem, out_sem, y_sem = refs[6:]
    me = lax.axis_index("mpo")
    rows_here = pl.ds(pl.multiple_of(me * plan.rows, plan.rows), plan.rows)
    left_copies = [
        pltpu.make_async_copy(source.at[:, rows_here, :], left_near.at[r], left_sem.at[r])
        for r, source in enumerate(left_refs)
    ]
    psi_copies = near_copies(plan, psi_refs, psi_near, psi_sem, STATES)
    for copy in left_copies + psi_copies:
        copy.start()
    site_matrices(plan, charge_ref, sites_ref, first_out, second_out)
    for copy in left_copies:
        copy.wait()
    fill_left(plan, charge_ref, left_near, wide, ls)
    ls_copy = pltpu.make_async_copy(ls, ls_out, out_sem.at[0])
    ls_copy.start()
    for copy in psi_copies:
        copy.wait()
    fill_vector(plan, left_ref, right_ref, psi_near, fs)
    fs_copy = pltpu.make_async_copy(fs, fs_out, out_sem.at[1])
    fs_copy.start()
    left_phase(plan, fs, ls, xs)
    tiles = ys.reshape(PAIRS, plan.w, plan.y_step, plan.width)

    def out_copy(index):
        rows = pl.ds(pl.multiple_of(index * Y_BLOCK, Y_BLOCK), Y_BLOCK)
        return pltpu.make_async_copy(tiles.at[:, :, rows, :], ys_out.at[:, :, rows, :], y_sem.at[index])

    middle_phase(
        plan, plan.n_mpo, Y_BLOCK, 2, xs, first_out, second_out, ys, lambda index: out_copy(index).start()
    )
    for index in range(plan.rows // Y_BLOCK):
        out_copy(index).wait()
    ls_copy.wait()
    fs_copy.wait()


def image_kernel(plan, left_ref, right_ref, ys_ref, vector_ref, own_ref, *refs):
    far_refs, (image, ys, right_near, vector, y_sem, right_sem, v_sem) = refs[: plan.n_far], refs[plan.n_far :]
    me = lax.axis_index("mpo")
    rows_here = pl.ds(pl.multiple_of(me * plan.rows, plan.rows), plan.rows)
    charges = pair_charges()
    y_copies = {
        p: pltpu.make_async_copy(ys_ref.at[p], ys.at[p], y_sem.at[p]) for p in range(PAIRS) if charges[p] <= plan.far
    }
    r_copies = right_copies(plan, own_ref, far_refs, right_near, right_sem)
    v_copy = pltpu.make_async_copy(vector_ref.at[:, rows_here, :], vector, v_sem)
    for n in range(plan.far + 1):
        for copy in r_copies[n] + [y_copies[p] for p in range(PAIRS) if charges[p] == n]:
            copy.start()
    v_copy.start()

    def ready(n):
        for copy in r_copies[n] + [y_copies[p] for p in range(PAIRS) if charges[p] == n]:
            copy.wait()

    result = right_phase(plan, True, ys, plan.rows, right_near, ready)
    blocks = masked_rows(plan, left_ref, right_ref, result)
    v_copy.wait()
    along = jnp.zeros((plan.rows, plan.width), F32)
    norm = jnp.zeros((plan.rows, plan.width), F32)
    for p, block in enumerate(blocks):
        image[p] = block
        field = vector[p].astype(F32)
        along = along + field * block.astype(F32)
        norm = norm + field * field
    along = whole_sum(along)
    norm = whole_sum(norm)
    ratio = jnp.where(norm > 0, along / jnp.where(norm > 0, norm, 1.0), 0.0)
    across = jnp.zeros((plan.rows, plan.width), F32)
    for p, block in enumerate(blocks):
        left_over = block.astype(F32) - ratio * vector[p].astype(F32)
        across = across + left_over * left_over
    across = whole_sum(across)
    line = lax.broadcasted_iota(jnp.int32, (8, plan.width), 0)
    sums = jnp.where(line == 0, along, jnp.where(line == 1, norm, jnp.where(line == 2, across, 0.0)))
    parts = []
    for _ in range(3):
        parts.append(sums.astype(BF16).astype(F32))
        sums = sums - parts[-1]
    parts.append(jnp.zeros((plan.rows - 24, plan.width), F32))
    image[PAIRS] = jnp.concatenate(parts, 0).astype(BF16)


def sums_of(piece):
    block = piece[PAIRS].astype(F32)
    return block[0:8] + block[8:16] + block[16:24]


def second_kernel(plan, count_all, n_parts, *refs):
    left_ref, right_ref = refs[:2]
    parts, refs = refs[2 : 2 + n_parts], refs[2 + n_parts :]
    image_refs, refs = refs[: 2 * plan.n_mpo], refs[2 * plan.n_mpo :]
    vector_ref, ls_ref, first_ref, second_ref, own_ref = refs[:5]
    far_refs, refs = refs[5 : 5 + plan.n_far], refs[5 + plan.n_far :]
    outs, image_out = refs[: plan.n_mpo], refs[plan.n_mpo]
    fs, xs, ys, image_near, vector, ls, right_near, image_sem, field_sem, right_sem, out_sem = refs[plan.n_mpo + 1 :]
    me = lax.axis_index("mpo")
    image_copies = near_copies(plan, image_refs, image_near, image_sem, PAIRS)
    v_copy = pltpu.make_async_copy(vector_ref, vector, field_sem.at[0])
    l_copy = pltpu.make_async_copy(ls_ref, ls, field_sem.at[1])
    r_copies = right_copies(plan, own_ref, far_refs, right_near, right_sem)
    for copy in [v_copy] + image_copies + [l_copy] + [copy for some in r_copies for copy in some]:
        copy.start()
    sums = merged([part[...] for part in parts])
    rayleigh = sums[0:1, :] / sums[1:2, :]
    scale = lax.rsqrt(sums[2:3, :] / count_all + EPSILON)
    v_copy.wait()
    for place, (_, _, r, kind) in enumerate(block_places(plan.n_mpo)):
        image_copies[place].wait()
        slot, _ = sector_of(kind)
        start = slot * plan.width + lax.bitwise_xor(me, r) * plan.rows
        where = pl.ds(pl.multiple_of(start, plan.rows), plan.rows)
        for p in range(PAIRS):
            block = image_near[place, p].astype(F32)
            residual = block - rayleigh * vector[p, where, :].astype(F32)
            fs[p, where, :] = (residual * scale).astype(BF16)
    out_copies = []
    pairs_here = pl.ds(me * STATES, STATES)
    for place, (_, _, r, kind) in enumerate(block_places(plan.n_mpo)):
        if kind == 0:
            start = lax.bitwise_xor(me, r) * plan.rows
            rows = pl.ds(pl.multiple_of(start, plan.rows), plan.rows)
            out_copies.append(
                pltpu.make_async_copy(image_near.at[place, pairs_here], image_out.at[0, :, rows, :], out_sem.at[r])
            )
    for copy in out_copies:
        copy.start()
    l_copy.wait()
    left_phase(plan, fs, ls, xs)
    middle_phase(plan, 1, 2 * Y_BLOCK, 2, xs, first_ref, second_ref, ys, lambda index: None)

    def ready(n):
        for copy in r_copies[n]:
            copy.wait()

    result = right_phase(plan, False, ys, plan.y_step, right_near, ready)
    rows = masked_rows(plan, left_ref, right_ref, result)
    for p in range(PAIRS):
        ys[p, : plan.rows, :] = rows[p].astype(F32)
    for r, out in enumerate(outs):
        first = lax.bitwise_xor(me, r) * STATES
        for second in range(STATES):
            out[second] = ys[first + second, : plan.rows, :].astype(BF16)
    for copy in out_copies:
        copy.wait()


Y_BLOCK = 8
COST_A = 2_000_000_000
COST_B = 4_000_000_000
VMEM = pl.BlockSpec(memory_space=pltpu.VMEM)
ANY = pl.BlockSpec(memory_space=pl.ANY)
SMEM = pl.BlockSpec(memory_space=pltpu.SMEM)
PARAMS = pltpu.CompilerParams(vmem_limit_bytes=60 * 1024 * 1024)


def shape_of(shape, dtype):
    return jax.ShapeDtypeStruct(shape, dtype)


def shards(psi, left_env, right_env, site_one, site_two, mpo_charge, left_sizes, right_sizes):
    n_mpo = lax.axis_size("mpo")
    n_bond = lax.axis_size("bond")
    width = psi.shape[2]
    plan = Plan(n_mpo, n_bond, width, right_env.shape[0])
    me = lax.axis_index("mpo")

    psi_here, psi_mine = exchange(psi[0], True)
    psi_other = handed_pairs(psi_mine)

    left_mine = left_env[:, 0]
    left_here = {0: left_mine}
    for bit in mpo_bits():
        left_here.update({r ^ bit: from_near(block, 0, bit) for r, block in list(left_here.items())})
    left_pieces = [left_here[r] for r in range(n_mpo)]

    right_far = right_exchange(right_env, plan.far)

    sites = jnp.transpose(jnp.stack([site_one, site_two]), (0, 3, 2, 4, 1))
    sites = sites.reshape(2, STATES * plan.w, STATES * plan.w)

    field_shape = (PAIRS, 3 * width, width)
    left_shape = (plan.rows * plan.w_pad, 3 * width)
    x_shape = (PAIRS, plan.rows * plan.w_pad, width)
    y_shape = (PAIRS, plan.y_step * plan.w, width)
    row_shape = (PAIRS, plan.rows, width)

    first_shape = (STATES * plan.w, STATES * plan.w_pad)
    second_shape = (2 * STATES * plan.w,) * 2
    y_out_shape = (PAIRS, plan.w, plan.rows, width)
    ys, vector, left_rows, first, second = pl.pallas_call(
        functools.partial(first_kernel, plan),
        out_shape=(
            shape_of(y_out_shape, F32),
            shape_of(field_shape, BF16),
            shape_of(left_shape, BF16),
            shape_of(first_shape, BF16),
            shape_of(second_shape, BF16),
        ),
        in_specs=[SMEM] * 3 + [ANY] * (3 * n_mpo) + [VMEM],
        out_specs=(ANY, ANY, ANY, VMEM, VMEM),
        scratch_shapes=[
            pltpu.VMEM(field_shape, BF16),
            pltpu.VMEM(left_shape, BF16),
            pltpu.VMEM((3, left_shape[0], width), F32),
            pltpu.VMEM(x_shape, F32),
            pltpu.VMEM(y_shape, F32),
            pltpu.VMEM((n_mpo, plan.w_here, plan.rows, width), BF16),
            pltpu.VMEM((3 * n_mpo,) + psi.shape[1:], BF16),
            pltpu.SemaphoreType.DMA((n_mpo,)),
            pltpu.SemaphoreType.DMA((3 * n_mpo,)),
            pltpu.SemaphoreType.DMA((2,)),
            pltpu.SemaphoreType.DMA((plan.rows // Y_BLOCK,)),
        ],
        compiler_params=PARAMS,
        cost_estimate=pl.CostEstimate(flops=COST_A, bytes_accessed=0, transcendentals=0),
        name="states_of_vector",
    )(
        mpo_charge, left_sizes, right_sizes, *by_place(psi_here, psi_mine, psi_other), *left_pieces, sites,
    )

    right_far, ys = lax.optimization_barrier((right_far, ys))
    right_pieces = handed_over(right_far, plan.far)
    right_scratch = pltpu.VMEM((plan.n_far + 1, plan.w, width, width), BF16)
    image_shape = (PAIRS + 1,) + row_shape[1:]
    image_rows = pl.pallas_call(
        functools.partial(image_kernel, plan),
        out_shape=shape_of(image_shape, BF16),
        in_specs=[SMEM] * 2 + [ANY] * (3 + plan.n_far),
        out_specs=VMEM,
        scratch_shapes=[
            pltpu.VMEM((PAIRS, plan.w * plan.rows, width), F32),
            right_scratch,
            pltpu.VMEM(row_shape, BF16),
            pltpu.SemaphoreType.DMA((PAIRS,)),
            pltpu.SemaphoreType.DMA((1 + plan.n_far,)),
            pltpu.SemaphoreType.DMA,
        ],
        compiler_params=PARAMS,
        cost_estimate=pl.CostEstimate(flops=COST_B, bytes_accessed=0, transcendentals=0),
        name="image_rows",
    )(left_sizes, right_sizes, ys.reshape(PAIRS, plan.w * plan.rows, width), vector, right_env, *right_pieces)

    image_here, image_mine = exchange(image_rows, False)
    sums = summed_over_bond(merged([sums_of(image_here[r]) for r in range(n_mpo)]))
    image_mine, sums = lax.optimization_barrier((image_mine, sums))
    image_other = handed_pairs(image_mine)

    count_all = n_bond * PAIRS * width * width
    *second_rows, image = pl.pallas_call(
        functools.partial(second_kernel, plan, float(count_all), len(sums)),
        out_shape=(shape_of((STATES,) + row_shape[1:], BF16),) * n_mpo + (shape_of(psi.shape, BF16),),
        in_specs=[SMEM] * 2 + [VMEM] * len(sums) + [ANY] * (2 * n_mpo + 2) + [VMEM] * 2 + [ANY] * (1 + plan.n_far),
        out_specs=(VMEM,) * n_mpo + (ANY,),
        scratch_shapes=[
            pltpu.VMEM(field_shape, BF16),
            pltpu.VMEM(x_shape, F32),
            pltpu.VMEM(y_shape, F32),
            pltpu.VMEM((3 * n_mpo,) + row_shape, BF16),
            pltpu.VMEM(field_shape, BF16),
            pltpu.VMEM(left_shape, BF16),
            right_scratch,
            pltpu.SemaphoreType.DMA((3 * n_mpo,)),
            pltpu.SemaphoreType.DMA((2,)),
            pltpu.SemaphoreType.DMA((1 + plan.n_far,)),
            pltpu.SemaphoreType.DMA((n_mpo,)),
        ],
        compiler_params=PARAMS,
        cost_estimate=pl.CostEstimate(flops=COST_A, bytes_accessed=0, transcendentals=0),
        name="correction_image_rows",
    )(
        left_sizes, right_sizes, *sums, *by_place(image_here, image_mine, image_other), vector, left_rows,
        first, second, right_env, *right_pieces,
    )

    result = jnp.zeros((STATES, width, width), BF16)
    for r, block in enumerate(second_rows):
        block = from_near(block, 0, r) if r else block
        start = lax.bitwise_xor(me, r) * plan.rows
        result = lax.dynamic_update_slice_in_dim(result, block, start, 1)
    return (image, result[None])


def solution(mesh):
    in_specs = (
        P(("groups", "bond"), "mpo", None, None),
        P("mpo", ("groups", "bond"), None, None),
        P(None, ("groups", "bond"), None, None),
        P("groups", None, None, None),
        P("groups", None, None, None),
        P(),
        P("groups"),
        P("groups"),
    )
    out_specs = (P(("groups", "bond"), "mpo", None, None), P(("groups", "bond"), "mpo", None, None))
    return jax.shard_map(shards, mesh=mesh, in_specs=in_specs, out_specs=out_specs, check_vma=False)
```

```python
import functools

import jax
import jax.numpy as jnp
from jax import lax
from jax.experimental import pallas as pl
from jax.experimental.pallas import tpu as pltpu
from jax.sharding import PartitionSpec as P

EPSILON = 1e-06
STATE_CHARGES = (0, 1, 1, 2)
STATES = len(STATE_CHARGES)
PAIRS = STATES * STATES
RIM = 4
F32 = jnp.float32
BF16 = jnp.bfloat16
NT = (((1,), (1,)), ((), ()))


def pair_charges():
    return [left + right for left in STATE_CHARGES for right in STATE_CHARGES]


def round_up(value, step):
    return -(-value // step) * step


def from_near(value, step, flip):
    n_bond, n_mpo = lax.axis_size("bond"), lax.axis_size("mpo")
    pairs = [
        ((i + step) * n_mpo + (j ^ flip), i * n_mpo + j)
        for i in range(n_bond)
        for j in range(n_mpo)
        if 0 <= i + step < n_bond
    ]
    return lax.ppermute(value, ("bond", "mpo"), pairs)


def mpo_bits():
    count = lax.axis_size("mpo")
    bits = []
    while count > 1:
        count //= 2
        bits.append(count)
    return bits


def exchange(own, cross_last):
    n_bond, n_mpo = lax.axis_size("bond"), lax.axis_size("mpo")
    pairs = [
        (i * n_mpo + j, (i + 1 - 2 * (j % 2)) * n_mpo + j)
        for i in range(n_bond)
        for j in range(n_mpo)
        if 0 <= i + 1 - 2 * (j % 2) < n_bond
    ]
    here = {0: own, 1: from_near(own, 0, 1)}
    for bit in mpo_bits()[:-1]:
        here.update({r ^ bit: from_near(here[r], 0, bit) for r in sorted(here) if r % 2 == 0})
    for r in range(2, n_mpo, 2):
        here[r ^ 1] = from_near(here[r], 0, 1)
    mine = {}
    for r in range(0, n_mpo, 2):
        if r == 0 or not cross_last:
            mine[r] = lax.ppermute(jnp.stack([here[r], here[r ^ 1]]), ("bond", "mpo"), pairs)
    if cross_last:
        for bit in mpo_bits()[:-1]:
            mine.update({r ^ bit: from_near(pair, 0, bit) for r, pair in list(mine.items())})
    return here, mine


def handed_pairs(mine):
    return {r: from_near(pair, 0, 1) for r, pair in mine.items()}


def by_place(here, mine, other):
    evens = sorted(mine)
    return [here[r] for r in sorted(here)] + [mine[r] for r in evens] + [other[r] for r in evens]


def block_places(n_mpo):
    places = [(r, None, r, 0) for r in range(n_mpo)]
    for kind in (1, 2):
        for r in range(0, n_mpo, 2):
            array = n_mpo + (kind - 1) * (n_mpo // 2) + r // 2
            order = (r, r ^ 1) if kind == 1 else (r ^ 1, r)
            places += [(array, index, member, kind) for index, member in enumerate(order)]
    return places


def sector_of(kind):
    odd = lax.rem(lax.axis_index("mpo"), 2)
    if kind == 0:
        return 0, 0
    above = odd if kind == 1 else 1 - odd
    return 1 + above, 2 * above - 1


def right_exchange(own, far):
    n_bond, n_mpo = lax.axis_size("bond"), lax.axis_size("mpo")
    arrays = []
    for first in range(1, far + 1, 2):
        pairs = [
            ((i + first + j % 2) * n_mpo + j, i * n_mpo + j)
            for i in range(n_bond)
            for j in range(n_mpo)
            if first + j % 2 <= far and i + first + j % 2 < n_bond
        ]
        arrays.append(lax.ppermute(own, ("bond", "mpo"), pairs))
    return arrays


def handed_over(arrays, far):
    n_bond, n_mpo = lax.axis_size("bond"), lax.axis_size("mpo")
    result = []
    for place, array in enumerate(arrays):
        pairs = [
            (i * n_mpo + j, i * n_mpo + (j ^ 1))
            for i in range(n_bond)
            for j in range(n_mpo)
            if 1 + 2 * place + j % 2 <= far
        ]
        result += [array, lax.ppermute(array, ("bond", "mpo"), pairs)]
    return result


def merged(parts):
    along = sum(part[0:1] for part in parts)
    norm = sum(part[1:2] for part in parts)
    ratio = jnp.where(norm > 0, along / jnp.where(norm > 0, norm, 1.0), 0.0)
    across = jnp.zeros_like(along)
    for part in parts:
        own = jnp.where(part[1:2] > 0, part[0:1] / jnp.where(part[1:2] > 0, part[1:2], 1.0), 0.0)
        gap = own - ratio
        across = across + part[2:3] + gap * gap * part[1:2]
    rest = jnp.zeros((parts[0].shape[0] - 3, parts[0].shape[1]), F32)
    return jnp.concatenate([along, norm, across, rest], 0)


def summed_over_bond(sums):
    n_bond = lax.axis_size("bond")
    reach, parts = 1, [sums]
    while reach < n_bond:
        if reach > 1:
            parts = [merged(parts)]
        radix = min(4, n_bond // reach)
        parts = parts + [
            lax.ppermute(parts[0], "bond", [(i ^ (reach * k), i) for i in range(n_bond)])
            for k in range(1, radix)
        ]
        reach *= radix
    return parts


def sector_limits(sizes_ref, sector, count):
    inside = (sector >= 0) & (sector < count)
    return jnp.where(inside, sizes_ref[jnp.clip(sector, 0, count - 1)], 0)


def state_charge(state):
    return (state + 1) // 2


class Plan:
    def __init__(self, n_mpo, n_bond, width, mpo_width):
        self.n_mpo = n_mpo
        self.n_bond = n_bond
        self.width = width
        self.w = mpo_width
        self.w_here = mpo_width // n_mpo
        self.w_pad = round_up(mpo_width, 8)
        self.rows = width // n_mpo
        self.y_step = self.rows + 8
        self.far = min(RIM, n_bond - 1)
        self.n_far = 2 * ((self.far + 1) // 2)


def fill_left(plan, charge_ref, left_near, wide, ls):
    me = lax.axis_index("mpo")
    wide[...] = jnp.zeros_like(wide)
    for r in range(plan.n_mpo):
        owner = lax.bitwise_xor(me, r)
        for t in range(plan.w_here):
            w = owner * plan.w_here + t
            block = left_near[r, t].astype(F32)
            for c, charge in enumerate((0, 1, -1)):
                factor = jnp.where(charge_ref[w] == charge, 1.0, 0.0).astype(F32)
                wide[c, pl.ds(w, plan.rows, stride=plan.w_pad), :] = block * factor
    for c in range(3):
        ls[:, c * plan.width : (c + 1) * plan.width] = wide[c].astype(BF16)


def fill_vector(plan, left_ref, right_ref, psi_near, fs):
    me = lax.axis_index("mpo")
    here = lax.axis_index("bond")
    row = lax.broadcasted_iota(jnp.int32, (plan.width, plan.width), 0)
    column = lax.broadcasted_iota(jnp.int32, (plan.width, plan.width), 1)
    for place, (_, _, r, kind) in enumerate(block_places(plan.n_mpo)):
        slot, step = sector_of(kind)
        sector = here + step
        first = lax.bitwise_xor(me, r)
        row_ok = row < sector_limits(left_ref, sector, plan.n_bond)
        where = pl.ds(pl.multiple_of(slot * plan.width, plan.width), plan.width)
        for second in range(STATES):
            target = sector + state_charge(first) + STATE_CHARGES[second]
            ok = row_ok & (column < sector_limits(right_ref, target, plan.n_bond))
            block = psi_near[place, second].astype(F32)
            fs[first * STATES + second, where, :] = jnp.where(ok, block, 0.0).astype(BF16)


def left_phase(plan, fs, ls, xs):
    def step(index, carry):
        p = index * 2
        both = jnp.concatenate([fs[p], fs[p + 1]], axis=1)
        done = jnp.dot(ls[...], both, preferred_element_type=F32)
        xs[p] = done[:, : plan.width]
        xs[p + 1] = done[:, plan.width :]
        return carry

    lax.fori_loop(0, PAIRS // 2, step, 0, unroll=8)


def site_matrices(plan, charge_ref, sites_ref, first_out, second_out):
    w, pad = plan.w, plan.w_pad
    size = STATES * w

    def index(shape, axis):
        return lax.broadcasted_iota(jnp.int32, shape, axis)

    def charges(bond):
        total = jnp.zeros(bond.shape, jnp.int32)
        for v in range(w):
            total = jnp.where(bond == v, charge_ref[v], total)
        return total

    row, column = index((size, size), 0), index((size, size), 1)
    local_step = state_charge(row // w) - state_charge(column // w)
    allowed = local_step == charges(row % w) - charges(column % w)
    first = jnp.where(allowed, sites_ref[0].astype(F32), 0.0).astype(BF16)
    second = jnp.where(allowed, sites_ref[1].astype(F32), 0.0).astype(BF16)

    into = (size, STATES * pad)
    spread_w = (index(into, 0) // w == index(into, 1) // pad) & (index(into, 0) % w == index(into, 1) % pad)
    first = jnp.dot(first, jnp.where(spread_w, 1.0, 0.0).astype(BF16), preferred_element_type=F32)
    first_out[...] = first.astype(BF16)

    into = (size, 2 * size)
    of, to = index(into, 0), index(into, 1)
    halves = []
    for k in range(2):
        spread_v = to == (of // w) * 2 * w + k * w + of % w
        halves.append(jnp.dot(second, jnp.where(spread_v, 1.0, 0.0).astype(BF16), preferred_element_type=F32))
    second_out[...] = jnp.concatenate(halves, 0).astype(BF16)


def middle_phase(plan, groups, block, unroll, xs, first_ref, second_ref, ys, done):
    w, pad = plan.w, plan.w_pad
    first = first_ref[...]
    second = second_ref[...]
    size = STATES * w
    if groups > 1:
        column = lax.broadcasted_iota(jnp.int32, first.shape, 1) % pad
        wide = first.astype(F32)
        rows = []
        for g in range(groups):
            ok = (column >= g * plan.w_here) & (column < (g + 1) * plan.w_here)
            rows.append(jnp.where(ok, wide, 0.0))
        first = jnp.concatenate(rows, 0).astype(BF16)

    def step(index, carry):
        middle = []
        for b in range(STATES):
            columns = []
            for one in range(block):
                start = pl.multiple_of((index * block + one) * pad, pad)
                columns.append(
                    jnp.concatenate([xs[a * STATES + b, pl.ds(start, pad), :] for a in range(STATES)], 0)
                )
            column = jnp.concatenate(columns, 1).astype(BF16)
            middle.append(jnp.dot(first, column, preferred_element_type=F32))
        for half in range(STATES // 2):
            total = None
            for g in range(groups):
                at = g * size + half * 2 * w
                column = jnp.concatenate([z[at : at + 2 * w] for z in middle], 0).astype(BF16)
                term = jnp.dot(second, column, preferred_element_type=F32)
                if groups > 1:
                    term = term.astype(BF16).astype(F32)
                total = term if total is None else total + term
            for k in range(2):
                for s2 in range(STATES):
                    at = k * size + s2 * w
                    for one in range(block):
                        rows = pl.ds(index * block + one, w, stride=plan.y_step)
                        ys[(2 * half + k) * STATES + s2, rows, :] = total[
                            at : at + w, one * plan.width : (one + 1) * plan.width
                        ]
        done(index)
        return carry

    lax.fori_loop(0, plan.rows // block, step, 0, unroll=unroll)


def right_phase(plan, split, ys, y_step, right_near, ready):
    result = [None] * PAIRS
    for n in range(plan.far + 1):
        ready(n)
        members = [p for p, charge in enumerate(pair_charges()) if charge == n]
        total = None
        for first in range(0, plan.w, plan.w_here):
            group = range(first, first + plan.w_here)
            right = jnp.concatenate([right_near[n, u] for u in group], 1)
            lines = []
            for p in members:
                parts = [ys[p, pl.ds(u * y_step, plan.rows), :] for u in group]
                lines.append(jnp.concatenate(parts, 1))
            field = jnp.concatenate(lines, 0)
            high = field.astype(BF16)
            if split:
                low = (field - high.astype(F32)).astype(BF16)
                high = jnp.concatenate([high, low], 0)
            term = lax.dot_general(high, right, NT, preferred_element_type=F32)
            total = term if total is None else total + term
        if split:
            half = total.shape[0] // 2
            total = total[:half] + total[half:]
        for place, p in enumerate(members):
            result[p] = total[place * plan.rows : (place + 1) * plan.rows]
    return result


def right_copies(plan, own_ref, far_refs, right_near, sems):
    odd = lax.rem(lax.axis_index("mpo"), 2)
    copies = [[] for _ in range(plan.far + 1)]
    copies[0].append(pltpu.make_async_copy(own_ref.at[:, 0], right_near.at[0], sems.at[0]))
    for place, source in enumerate(far_refs):
        first, other = 1 + 2 * (place // 2), place % 2
        slot = first + (1 - odd if other else odd)
        copies[first].append(pltpu.make_async_copy(source.at[:, 0], right_near.at[slot], sems.at[1 + place]))
    return copies


def masked_rows(plan, left_ref, right_ref, result):
    me = lax.axis_index("mpo")
    here = lax.axis_index("bond")
    shape = (plan.rows, plan.width)
    row = lax.broadcasted_iota(jnp.int32, shape, 0) + me * plan.rows
    column = lax.broadcasted_iota(jnp.int32, shape, 1)
    row_ok = row < sector_limits(left_ref, here, plan.n_bond)
    blocks = []
    for p, charge in enumerate(pair_charges()):
        if result[p] is None:
            blocks.append(jnp.zeros(shape, BF16))
            continue
        ok = row_ok & (column < sector_limits(right_ref, here + charge, plan.n_bond))
        blocks.append(jnp.where(ok, result[p], 0.0).astype(BF16))
    return blocks


def whole_sum(values):
    return jnp.sum(jnp.sum(values, axis=1, keepdims=True), axis=0, keepdims=True)


def near_copies(plan, refs, near, sems, count):
    copies = []
    for place, (array, index, _, _) in enumerate(block_places(plan.n_mpo)):
        source = refs[array] if index is None else refs[array].at[index]
        copies.append(pltpu.make_async_copy(source.at[pl.ds(0, count)], near.at[place], sems.at[place]))
    return copies


def first_kernel(plan, *refs):
    charge_ref, left_ref, right_ref = refs[:3]
    psi_refs = refs[3 : 3 + 2 * plan.n_mpo]
    left_refs = refs[3 + 2 * plan.n_mpo : 3 + 3 * plan.n_mpo]
    refs = refs[3 + 3 * plan.n_mpo :]
    sites_ref, ys_out, fs_out, ls_out, first_out, second_out = refs[:6]
    fs, ls, wide, xs, ys, left_near, psi_near, left_sem, psi_sem, out_sem, y_sem = refs[6:]
    me = lax.axis_index("mpo")
    rows_here = pl.ds(pl.multiple_of(me * plan.rows, plan.rows), plan.rows)
    odd_rows = pl.ds(pl.multiple_of(lax.rem(me, 2) * plan.rows, plan.rows), plan.rows)
    left_copies = [
        pltpu.make_async_copy(source.at[:, odd_rows if r > 1 else rows_here, :], left_near.at[r], left_sem.at[r])
        for r, source in enumerate(left_refs)
    ]
    psi_copies = near_copies(plan, psi_refs, psi_near, psi_sem, STATES)
    for copy in left_copies + psi_copies:
        copy.start()
    site_matrices(plan, charge_ref, sites_ref, first_out, second_out)
    for copy in left_copies:
        copy.wait()
    fill_left(plan, charge_ref, left_near, wide, ls)
    ls_copy = pltpu.make_async_copy(ls, ls_out, out_sem.at[0])
    ls_copy.start()
    for copy in psi_copies:
        copy.wait()
    fill_vector(plan, left_ref, right_ref, psi_near, fs)
    fs_copy = pltpu.make_async_copy(fs, fs_out, out_sem.at[1])
    fs_copy.start()
    left_phase(plan, fs, ls, xs)
    tiles = ys.reshape(PAIRS, plan.w, plan.y_step, plan.width)

    def out_copy(index):
        rows = pl.ds(pl.multiple_of(index * Y_BLOCK, Y_BLOCK), Y_BLOCK)
        return pltpu.make_async_copy(tiles.at[:, :, rows, :], ys_out.at[:, :, rows, :], y_sem.at[index])

    middle_phase(
        plan, plan.n_mpo, Y_BLOCK, 2, xs, first_out, second_out, ys, lambda index: out_copy(index).start()
    )
    for index in range(plan.rows // Y_BLOCK):
        out_copy(index).wait()
    ls_copy.wait()
    fs_copy.wait()


def image_kernel(plan, left_ref, right_ref, ys_ref, vector_ref, own_ref, *refs):
    far_refs, (image, ys, right_near, vector, y_sem, right_sem, v_sem) = refs[: plan.n_far], refs[plan.n_far :]
    me = lax.axis_index("mpo")
    rows_here = pl.ds(pl.multiple_of(me * plan.rows, plan.rows), plan.rows)
    charges = pair_charges()
    y_copies = {
        p: pltpu.make_async_copy(ys_ref.at[p], ys.at[p], y_sem.at[p]) for p in range(PAIRS) if charges[p] <= plan.far
    }
    r_copies = right_copies(plan, own_ref, far_refs, right_near, right_sem)
    v_copy = pltpu.make_async_copy(vector_ref.at[:, rows_here, :], vector, v_sem)
    for n in range(plan.far + 1):
        for copy in r_copies[n] + [y_copies[p] for p in range(PAIRS) if charges[p] == n]:
            copy.start()
    v_copy.start()

    def ready(n):
        for copy in r_copies[n] + [y_copies[p] for p in range(PAIRS) if charges[p] == n]:
            copy.wait()

    result = right_phase(plan, True, ys, plan.rows, right_near, ready)
    blocks = masked_rows(plan, left_ref, right_ref, result)
    v_copy.wait()
    along = jnp.zeros((plan.rows, plan.width), F32)
    norm = jnp.zeros((plan.rows, plan.width), F32)
    for p, block in enumerate(blocks):
        image[p] = block
        field = vector[p].astype(F32)
        along = along + field * block.astype(F32)
        norm = norm + field * field
    along = whole_sum(along)
    norm = whole_sum(norm)
    ratio = jnp.where(norm > 0, along / jnp.where(norm > 0, norm, 1.0), 0.0)
    across = jnp.zeros((plan.rows, plan.width), F32)
    for p, block in enumerate(blocks):
        left_over = block.astype(F32) - ratio * vector[p].astype(F32)
        across = across + left_over * left_over
    across = whole_sum(across)
    line = lax.broadcasted_iota(jnp.int32, (8, plan.width), 0)
    sums = jnp.where(line == 0, along, jnp.where(line == 1, norm, jnp.where(line == 2, across, 0.0)))
    parts = []
    for _ in range(3):
        parts.append(sums.astype(BF16).astype(F32))
        sums = sums - parts[-1]
    parts.append(jnp.zeros((plan.rows - 24, plan.width), F32))
    image[PAIRS] = jnp.concatenate(parts, 0).astype(BF16)


def sums_of(piece):
    block = piece[PAIRS].astype(F32)
    return block[0:8] + block[8:16] + block[16:24]


def second_kernel(plan, count_all, n_parts, *refs):
    left_ref, right_ref = refs[:2]
    parts, refs = refs[2 : 2 + n_parts], refs[2 + n_parts :]
    image_refs, refs = refs[: 2 * plan.n_mpo], refs[2 * plan.n_mpo :]
    vector_ref, ls_ref, first_ref, second_ref, own_ref = refs[:5]
    far_refs, refs = refs[5 : 5 + plan.n_far], refs[5 + plan.n_far :]
    outs, image_out = refs[: plan.n_mpo], refs[plan.n_mpo]
    fs, xs, ys, image_near, vector, ls, right_near, image_sem, field_sem, right_sem, out_sem = refs[plan.n_mpo + 1 :]
    me = lax.axis_index("mpo")
    image_copies = near_copies(plan, image_refs, image_near, image_sem, PAIRS)
    v_copy = pltpu.make_async_copy(vector_ref, vector, field_sem.at[0])
    l_copy = pltpu.make_async_copy(ls_ref, ls, field_sem.at[1])
    r_copies = right_copies(plan, own_ref, far_refs, right_near, right_sem)
    for copy in [v_copy] + image_copies + [l_copy]:
        copy.start()
    sums = merged([part[...] for part in parts])
    rayleigh = sums[0:1, :] / sums[1:2, :]
    scale = lax.rsqrt(sums[2:3, :] / count_all + EPSILON)
    v_copy.wait()
    for place, (_, _, r, kind) in enumerate(block_places(plan.n_mpo)):
        image_copies[place].wait()
        slot, _ = sector_of(kind)
        start = slot * plan.width + lax.bitwise_xor(me, r) * plan.rows
        where = pl.ds(pl.multiple_of(start, plan.rows), plan.rows)
        for p in range(PAIRS):
            block = image_near[place, p].astype(F32)
            residual = block - rayleigh * vector[p, where, :].astype(F32)
            fs[p, where, :] = (residual * scale).astype(BF16)
    out_copies = []
    pairs_here = pl.ds(me * STATES, STATES)
    for place, (_, _, r, kind) in enumerate(block_places(plan.n_mpo)):
        if kind == 0:
            start = lax.bitwise_xor(me, r) * plan.rows
            rows = pl.ds(pl.multiple_of(start, plan.rows), plan.rows)
            out_copies.append(
                pltpu.make_async_copy(image_near.at[place, pairs_here], image_out.at[0, :, rows, :], out_sem.at[r])
            )
    for copy in out_copies + [copy for some in r_copies for copy in some]:
        copy.start()
    l_copy.wait()
    left_phase(plan, fs, ls, xs)
    middle_phase(plan, 1, 2 * Y_BLOCK, 2, xs, first_ref, second_ref, ys, lambda index: None)

    def ready(n):
        for copy in r_copies[n]:
            copy.wait()

    result = right_phase(plan, False, ys, plan.y_step, right_near, ready)
    rows = masked_rows(plan, left_ref, right_ref, result)
    for p in range(PAIRS):
        ys[p, : plan.rows, :] = rows[p].astype(F32)
    for r, out in enumerate(outs):
        first = lax.bitwise_xor(me, r) * STATES
        for second in range(STATES):
            out[second] = ys[first + second, : plan.rows, :].astype(BF16)
    for copy in out_copies:
        copy.wait()


Y_BLOCK = 8
COST_A = 1_000
COST_B = 4_000_000_000
VMEM = pl.BlockSpec(memory_space=pltpu.VMEM)
ANY = pl.BlockSpec(memory_space=pl.ANY)
SMEM = pl.BlockSpec(memory_space=pltpu.SMEM)
PARAMS = pltpu.CompilerParams(vmem_limit_bytes=59 * 1024 * 1024)


def shape_of(shape, dtype):
    return jax.ShapeDtypeStruct(shape, dtype)


def shards(psi, left_env, right_env, site_one, site_two, mpo_charge, left_sizes, right_sizes):
    n_mpo = lax.axis_size("mpo")
    n_bond = lax.axis_size("bond")
    width = psi.shape[2]
    plan = Plan(n_mpo, n_bond, width, right_env.shape[0])
    me = lax.axis_index("mpo")

    sites = jnp.transpose(jnp.stack([site_one, site_two]), (0, 3, 2, 4, 1))
    sites = sites.reshape(2, STATES * plan.w, STATES * plan.w)

    psi_here, psi_mine = exchange(psi[0], True)
    psi_mine, sites = lax.optimization_barrier((psi_mine, sites))
    psi_other = handed_pairs(psi_mine)

    left_mine = left_env[:, 0]
    left_pieces = [left_mine, from_near(left_mine, 0, 1)]
    for r in range(2, n_mpo, 2):
        start = lax.bitwise_xor(me - lax.rem(me, 2), r) * plan.rows
        both = from_near(lax.dynamic_slice_in_dim(left_mine, start, 2 * plan.rows, 1), 0, r)
        left_pieces += [both, from_near(both, 0, 1)]

    right_far = right_exchange(right_env, plan.far)

    field_shape = (PAIRS, 3 * width, width)
    left_shape = (plan.rows * plan.w_pad, 3 * width)
    x_shape = (PAIRS, plan.rows * plan.w_pad, width)
    y_shape = (PAIRS, plan.y_step * plan.w, width)
    row_shape = (PAIRS, plan.rows, width)

    first_shape = (STATES * plan.w, STATES * plan.w_pad)
    second_shape = (2 * STATES * plan.w,) * 2
    y_out_shape = (PAIRS, plan.w, plan.rows, width)
    ys, vector, left_rows, first, second = pl.pallas_call(
        functools.partial(first_kernel, plan),
        out_shape=(
            shape_of(y_out_shape, F32),
            shape_of(field_shape, BF16),
            shape_of(left_shape, BF16),
            shape_of(first_shape, BF16),
            shape_of(second_shape, BF16),
        ),
        in_specs=[SMEM] * 3 + [ANY] * (3 * n_mpo) + [VMEM],
        out_specs=(ANY, ANY, ANY, VMEM, VMEM),
        scratch_shapes=[
            pltpu.VMEM(field_shape, BF16),
            pltpu.VMEM(left_shape, BF16),
            pltpu.VMEM((3, left_shape[0], width), F32),
            pltpu.VMEM(x_shape, F32),
            pltpu.VMEM(y_shape, F32),
            pltpu.VMEM((n_mpo, plan.w_here, plan.rows, width), BF16),
            pltpu.VMEM((3 * n_mpo,) + psi.shape[1:], BF16),
            pltpu.SemaphoreType.DMA((n_mpo,)),
            pltpu.SemaphoreType.DMA((3 * n_mpo,)),
            pltpu.SemaphoreType.DMA((2,)),
            pltpu.SemaphoreType.DMA((plan.rows // Y_BLOCK,)),
        ],
        compiler_params=PARAMS,
        cost_estimate=pl.CostEstimate(flops=COST_A, bytes_accessed=0, transcendentals=0),
        name="states_of_vector",
    )(
        mpo_charge, left_sizes, right_sizes, *by_place(psi_here, psi_mine, psi_other), *left_pieces, sites,
    )

    right_far, ys = lax.optimization_barrier((right_far, ys))
    right_pieces = handed_over(right_far, plan.far)
    right_scratch = pltpu.VMEM((plan.n_far + 1, plan.w, width, width), BF16)
    image_shape = (PAIRS + 1,) + row_shape[1:]
    image_rows = pl.pallas_call(
        functools.partial(image_kernel, plan),
        out_shape=shape_of(image_shape, BF16),
        in_specs=[SMEM] * 2 + [ANY] * (3 + plan.n_far),
        out_specs=VMEM,
        scratch_shapes=[
            pltpu.VMEM((PAIRS, plan.w * plan.rows, width), F32),
            right_scratch,
            pltpu.VMEM(row_shape, BF16),
            pltpu.SemaphoreType.DMA((PAIRS,)),
            pltpu.SemaphoreType.DMA((1 + plan.n_far,)),
            pltpu.SemaphoreType.DMA,
        ],
        compiler_params=PARAMS,
        cost_estimate=pl.CostEstimate(flops=COST_B, bytes_accessed=0, transcendentals=0),
        name="image_rows",
    )(left_sizes, right_sizes, ys.reshape(PAIRS, plan.w * plan.rows, width), vector, right_env, *right_pieces)

    image_here, image_mine = exchange(image_rows, False)
    blocks, _ = lax.optimization_barrier((image_here, image_mine[0]))
    sums = summed_over_bond(merged([sums_of(blocks[r]) for r in range(n_mpo)]))
    last = max(image_mine)
    image_mine[last], sums = lax.optimization_barrier((image_mine[last], sums))
    image_other = handed_pairs(image_mine)

    count_all = n_bond * PAIRS * width * width
    *second_rows, image = pl.pallas_call(
        functools.partial(second_kernel, plan, float(count_all), len(sums)),
        out_shape=(shape_of((STATES,) + row_shape[1:], BF16),) * n_mpo + (shape_of(psi.shape, BF16),),
        in_specs=[SMEM] * 2 + [VMEM] * len(sums) + [ANY] * (2 * n_mpo + 2) + [VMEM] * 2 + [ANY] * (1 + plan.n_far),
        out_specs=(VMEM,) * n_mpo + (ANY,),
        scratch_shapes=[
            pltpu.VMEM(field_shape, BF16),
            pltpu.VMEM(x_shape, F32),
            pltpu.VMEM(y_shape, F32),
            pltpu.VMEM((3 * n_mpo,) + row_shape, BF16),
            pltpu.VMEM(field_shape, BF16),
            pltpu.VMEM(left_shape, BF16),
            right_scratch,
            pltpu.SemaphoreType.DMA((3 * n_mpo,)),
            pltpu.SemaphoreType.DMA((2,)),
            pltpu.SemaphoreType.DMA((1 + plan.n_far,)),
            pltpu.SemaphoreType.DMA((n_mpo,)),
        ],
        compiler_params=PARAMS,
        cost_estimate=pl.CostEstimate(flops=COST_A, bytes_accessed=0, transcendentals=0),
        name="correction_image_rows",
    )(
        left_sizes, right_sizes, *sums, *by_place(image_here, image_mine, image_other), vector, left_rows,
        first, second, right_env, *right_pieces,
    )

    result = jnp.zeros((STATES, width, width), BF16)
    for r, block in enumerate(second_rows):
        block = from_near(block, 0, r) if r else block
        start = lax.bitwise_xor(me, r) * plan.rows
        result = lax.dynamic_update_slice_in_dim(result, block, start, 1)
    return (image, result[None])


def solution(mesh):
    in_specs = (
        P(("groups", "bond"), "mpo", None, None),
        P("mpo", ("groups", "bond"), None, None),
        P(None, ("groups", "bond"), None, None),
        P("groups", None, None, None),
        P("groups", None, None, None),
        P(),
        P("groups"),
        P("groups"),
    )
    out_specs = (P(("groups", "bond"), "mpo", None, None), P(("groups", "bond"), "mpo", None, None))
    return jax.shard_map(shards, mesh=mesh, in_specs=in_specs, out_specs=out_specs, check_vma=False)
```

```python
import functools

import jax
import jax.numpy as jnp
from jax import lax
from jax.experimental import pallas as pl
from jax.experimental.pallas import tpu as pltpu
from jax.sharding import PartitionSpec as P

EPSILON = 1e-06
STATE_CHARGES = (0, 1, 1, 2)
STATES = len(STATE_CHARGES)
PAIRS = STATES * STATES
RIM = 4
F32 = jnp.float32
BF16 = jnp.bfloat16
NT = (((1,), (1,)), ((), ()))


def pair_charges():
    return [left + right for left in STATE_CHARGES for right in STATE_CHARGES]


def round_up(value, step):
    return -(-value // step) * step


def from_near(value, step, flip):
    n_bond, n_mpo = lax.axis_size("bond"), lax.axis_size("mpo")
    pairs = [
        ((i + step) * n_mpo + (j ^ flip), i * n_mpo + j)
        for i in range(n_bond)
        for j in range(n_mpo)
        if 0 <= i + step < n_bond
    ]
    return lax.ppermute(value, ("bond", "mpo"), pairs)


def mpo_bits():
    count = lax.axis_size("mpo")
    bits = []
    while count > 1:
        count //= 2
        bits.append(count)
    return bits


def exchange(own):
    n_bond, n_mpo = lax.axis_size("bond"), lax.axis_size("mpo")
    pairs = [
        (i * n_mpo + j, (i + 1 - 2 * (j % 2)) * n_mpo + j)
        for i in range(n_bond)
        for j in range(n_mpo)
        if 0 <= i + 1 - 2 * (j % 2) < n_bond
    ]
    here = own_sector(own)
    first = jnp.stack([here[0], here[1]])
    mine = {}
    for r in range(0, n_mpo, 2):
        pair = jnp.stack([here[r], here[r ^ 1]]) if r else first
        mine[r] = lax.ppermute(pair, ("bond", "mpo"), pairs)
    return here, first, mine


def own_sector(own):
    here = {0: own, 1: from_near(own, 0, 1)}
    for bit in mpo_bits()[:-1]:
        here.update({r ^ bit: from_near(here[r], 0, bit) for r in sorted(here) if r % 2 == 0})
    for r in range(2, len(here) * 2 - 2, 2):
        here[r ^ 1] = from_near(here[r], 0, 1)
    return here


def exchange_all(own, before):
    n_mpo = lax.axis_size("mpo")
    low, high = from_near(own, -1, 0), from_near(own, 1, 0)
    here = own_sector(own)
    (low, high), _, before = lax.optimization_barrier(((low, high), here[n_mpo // 2], before))
    both = {0: jnp.stack([low, high])}
    for bit in mpo_bits():
        both.update({r ^ bit: from_near(pair, 0, bit) for r, pair in list(both.items())})
    rest = [here[r] for r in range(2, n_mpo)]
    return [jnp.stack([here[0], here[1]])] + rest + [both[r] for r in range(n_mpo)], before


def all_places(n_mpo):
    places = [(0, 0, 0, 0), (0, 1, 1, 0)] + [(r - 1, None, r, 0) for r in range(2, n_mpo)]
    return places + [(n_mpo - 1 + r, side, r, 3 + side) for r in range(n_mpo) for side in range(2)]


def handed_pairs(mine):
    return {r: from_near(pair, 0, 1) for r, pair in mine.items()}


def by_place(here, first, mine, other):
    evens = sorted(mine)
    rest = [here[r] for r in sorted(here) if r > 1]
    return [first] + rest + [mine[r] for r in evens] + [other[r] for r in evens]


def block_places(n_mpo):
    places = [(0, 0, 0, 0), (0, 1, 1, 0)] + [(r - 1, None, r, 0) for r in range(2, n_mpo)]
    for kind in (1, 2):
        for r in range(0, n_mpo, 2):
            array = n_mpo - 1 + (kind - 1) * (n_mpo // 2) + r // 2
            order = (r, r ^ 1) if kind == 1 else (r ^ 1, r)
            places += [(array, index, member, kind) for index, member in enumerate(order)]
    return places


def sector_of(kind):
    odd = lax.rem(lax.axis_index("mpo"), 2)
    if kind == 0:
        return 0, 0
    if kind > 2:
        return kind - 2, 2 * kind - 7
    above = odd if kind == 1 else 1 - odd
    return 1 + above, 2 * above - 1


def right_exchange(own, far):
    n_bond, n_mpo = lax.axis_size("bond"), lax.axis_size("mpo")
    arrays = []
    for first in range(1, far + 1, 2):
        pairs = [
            ((i + first + j % 2) * n_mpo + j, i * n_mpo + j)
            for i in range(n_bond)
            for j in range(n_mpo)
            if first + j % 2 <= far and i + first + j % 2 < n_bond
        ]
        arrays.append(lax.ppermute(own, ("bond", "mpo"), pairs))
    return arrays


def handed_over(arrays, far):
    n_bond, n_mpo = lax.axis_size("bond"), lax.axis_size("mpo")
    result = []
    for place, array in enumerate(arrays):
        pairs = [
            (i * n_mpo + j, i * n_mpo + (j ^ 1))
            for i in range(n_bond)
            for j in range(n_mpo)
            if 1 + 2 * place + j % 2 <= far
        ]
        result += [array, lax.ppermute(array, ("bond", "mpo"), pairs)]
    return result


def merged(parts):
    along = sum(part[0:1] for part in parts)
    norm = sum(part[1:2] for part in parts)
    ratio = jnp.where(norm > 0, along / jnp.where(norm > 0, norm, 1.0), 0.0)
    across = jnp.zeros_like(along)
    for part in parts:
        own = jnp.where(part[1:2] > 0, part[0:1] / jnp.where(part[1:2] > 0, part[1:2], 1.0), 0.0)
        gap = own - ratio
        across = across + part[2:3] + gap * gap * part[1:2]
    rest = jnp.zeros((parts[0].shape[0] - 3, parts[0].shape[1]), F32)
    return jnp.concatenate([along, norm, across, rest], 0)


def summed_over_bond(sums):
    n_bond = lax.axis_size("bond")
    reach, parts = 1, [sums]
    while reach < n_bond:
        if reach > 1:
            parts = [merged(parts)]
        radix = min(4, n_bond // reach)
        parts = parts + [
            lax.ppermute(parts[0], "bond", [(i ^ (reach * k), i) for i in range(n_bond)])
            for k in range(1, radix)
        ]
        reach *= radix
    return parts


def far_sums(sums):
    n_bond, n_mpo = lax.axis_size("bond"), lax.axis_size("mpo")
    pairs = [((i ^ (2 + j % 2)) * n_mpo + j, i * n_mpo + j) for i in range(n_bond) for j in range(n_mpo)]
    return [sums, lax.ppermute(sums, ("bond", "mpo"), pairs)]


def near_sums(plan, image_near):
    here = lax.axis_index("bond")
    parts = []
    for place, (_, _, _, kind) in enumerate(block_places(plan.n_mpo)):
        if kind > 0:
            wanted = here + sector_of(kind)[1] == lax.bitwise_xor(here, 1)
            parts.append(sums_of(image_near[place]) * jnp.where(wanted, 1.0, 0.0).astype(F32))
    return parts


def sector_limits(sizes_ref, first, sector, count):
    inside = (sector >= 0) & (sector < count)
    return jnp.where(inside, sizes_ref[first + jnp.clip(sector, 0, count - 1)], 0)


def state_charge(state):
    return (state + 1) // 2


class Plan:
    def __init__(self, n_mpo, n_bond, width, mpo_width):
        self.n_mpo = n_mpo
        self.n_bond = n_bond
        self.width = width
        self.w = mpo_width
        self.w_here = mpo_width // n_mpo
        self.w_pad = round_up(mpo_width, 8)
        self.rows = width // n_mpo
        self.y_step = self.rows + 8
        self.far = min(RIM, n_bond - 1)
        self.n_near = 2 * n_mpo - 1
        self.n_far = 2 * ((self.far + 1) // 2)


def fill_left(plan, sizes_ref, left_near, wide, ls):
    me = lax.axis_index("mpo")
    wide[...] = jnp.zeros_like(wide)
    for r in range(plan.n_mpo):
        owner = lax.bitwise_xor(me, r)
        for t in range(plan.w_here):
            w = owner * plan.w_here + t
            block = left_near[r, t].astype(F32)
            for c, charge in enumerate((0, 1, -1)):
                factor = jnp.where(sizes_ref[w] == charge, 1.0, 0.0).astype(F32)
                wide[c, pl.ds(w, plan.rows, stride=plan.w_pad), :] = block * factor
    for c in range(3):
        ls[:, c * plan.width : (c + 1) * plan.width] = wide[c].astype(BF16)


def fill_vector(plan, sizes_ref, psi_near, fs):
    me = lax.axis_index("mpo")
    here = lax.axis_index("bond")
    row = lax.broadcasted_iota(jnp.int32, (plan.width, plan.width), 0)
    column = lax.broadcasted_iota(jnp.int32, (plan.width, plan.width), 1)
    for place, (_, _, r, kind) in enumerate(all_places(plan.n_mpo)):
        slot, step = sector_of(kind)
        sector = here + step
        first = lax.bitwise_xor(me, r)
        row_ok = row < sector_limits(sizes_ref, plan.w, sector, plan.n_bond)
        where = pl.ds(pl.multiple_of(slot * plan.width, plan.width), plan.width)
        for second in range(STATES):
            target = sector + state_charge(first) + STATE_CHARGES[second]
            ok = row_ok & (column < sector_limits(sizes_ref, plan.w + plan.n_bond, target, plan.n_bond))
            block = psi_near[place, second].astype(F32)
            fs[first * STATES + second, where, :] = jnp.where(ok, block, 0.0).astype(BF16)


def left_phase(plan, fs, ls, xs):
    def step(index, carry):
        p = index * 2
        both = jnp.concatenate([fs[p], fs[p + 1]], axis=1)
        done = jnp.dot(ls[...], both, preferred_element_type=F32)
        xs[p] = done[:, : plan.width]
        xs[p + 1] = done[:, plan.width :]
        return carry

    lax.fori_loop(0, PAIRS // 2, step, 0, unroll=8)


def site_matrices(plan, sizes_ref, sites_ref, first_out, second_out):
    w, pad = plan.w, plan.w_pad
    size = STATES * w

    def index(shape, axis):
        return lax.broadcasted_iota(jnp.int32, shape, axis)

    def charges(bond):
        total = jnp.zeros(bond.shape, jnp.int32)
        for v in range(w):
            total = jnp.where(bond == v, sizes_ref[v], total)
        return total

    row, column = index((size, size), 0), index((size, size), 1)
    local_step = state_charge(row // w) - state_charge(column // w)
    allowed = local_step == charges(row % w) - charges(column % w)
    first = jnp.where(allowed, sites_ref[0].astype(F32), 0.0).astype(BF16)
    second = jnp.where(allowed, sites_ref[1].astype(F32), 0.0).astype(BF16)

    into = (size, STATES * pad)
    spread_w = (index(into, 0) // w == index(into, 1) // pad) & (index(into, 0) % w == index(into, 1) % pad)
    first = jnp.dot(first, jnp.where(spread_w, 1.0, 0.0).astype(BF16), preferred_element_type=F32)
    first_out[...] = first.astype(BF16)

    into = (size, 2 * size)
    of, to = index(into, 0), index(into, 1)
    halves = []
    for k in range(2):
        spread_v = to == (of // w) * 2 * w + k * w + of % w
        halves.append(jnp.dot(second, jnp.where(spread_v, 1.0, 0.0).astype(BF16), preferred_element_type=F32))
    second_out[...] = jnp.concatenate(halves, 0).astype(BF16)


def middle_phase(plan, groups, block, unroll, xs, first_ref, second_ref, ys, done):
    w, pad = plan.w, plan.w_pad
    first = first_ref[...]
    second = second_ref[...]
    size = STATES * w
    if groups > 1:
        column = lax.broadcasted_iota(jnp.int32, first.shape, 1) % pad
        wide = first.astype(F32)
        rows = []
        for g in range(groups):
            ok = (column >= g * plan.w_here) & (column < (g + 1) * plan.w_here)
            rows.append(jnp.where(ok, wide, 0.0))
        first = jnp.concatenate(rows, 0).astype(BF16)

    def step(index, carry):
        middle = []
        for b in range(STATES):
            columns = []
            for one in range(block):
                start = pl.multiple_of((index * block + one) * pad, pad)
                columns.append(
                    jnp.concatenate([xs[a * STATES + b, pl.ds(start, pad), :] for a in range(STATES)], 0)
                )
            column = jnp.concatenate(columns, 1).astype(BF16)
            middle.append(jnp.dot(first, column, preferred_element_type=F32))
        for half in range(STATES // 2):
            total = None
            for g in range(groups):
                at = g * size + half * 2 * w
                column = jnp.concatenate([z[at : at + 2 * w] for z in middle], 0).astype(BF16)
                term = jnp.dot(second, column, preferred_element_type=F32)
                if groups > 1:
                    term = term.astype(BF16).astype(F32)
                total = term if total is None else total + term
            for k in range(2):
                for s2 in range(STATES):
                    at = k * size + s2 * w
                    for one in range(block):
                        rows = pl.ds(index * block + one, w, stride=plan.y_step)
                        ys[(2 * half + k) * STATES + s2, rows, :] = total[
                            at : at + w, one * plan.width : (one + 1) * plan.width
                        ]
        done(index)
        return carry

    lax.fori_loop(0, plan.rows // block, step, 0, unroll=unroll)


def right_phase(plan, split, ys, y_step, right_near, ready):
    result = [None] * PAIRS
    for n in range(plan.far + 1):
        ready(n)
        members = [p for p, charge in enumerate(pair_charges()) if charge == n]
        total = None
        for first in range(0, plan.w, plan.w_here):
            group = range(first, first + plan.w_here)
            right = jnp.concatenate([right_near[n, u] for u in group], 1)
            lines = []
            for p in members:
                parts = [ys[p, pl.ds(u * y_step, plan.rows), :] for u in group]
                lines.append(jnp.concatenate(parts, 1))
            field = jnp.concatenate(lines, 0)
            high = field.astype(BF16)
            if split:
                low = (field - high.astype(F32)).astype(BF16)
                high = jnp.concatenate([high, low], 0)
            term = lax.dot_general(high, right, NT, preferred_element_type=F32)
            total = term if total is None else total + term
        if split:
            half = total.shape[0] // 2
            total = total[:half] + total[half:]
        for place, p in enumerate(members):
            result[p] = total[place * plan.rows : (place + 1) * plan.rows]
    return result


class RightCopy:
    def __init__(self, plan, source, right_near, slot, sem):
        self.copy = pltpu.make_async_copy(source.at[:, 0], right_near.at[slot], sem)
        self.there = None if isinstance(slot, int) else slot <= plan.far

    def start(self):
        self.do(self.copy.start)

    def wait(self):
        self.do(self.copy.wait)

    def do(self, action):
        if self.there is None:
            action()
        else:
            pl.when(self.there)(action)


def right_copies(plan, own_ref, far_refs, right_near, sems):
    odd = lax.rem(lax.axis_index("mpo"), 2)
    copies = [[] for _ in range(plan.far + 1)]
    copies[0].append(RightCopy(plan, own_ref, right_near, 0, sems.at[0]))
    for place, source in enumerate(far_refs):
        first, other = 1 + 2 * (place // 2), place % 2
        slot = first + (1 - odd if other else odd)
        copies[first].append(RightCopy(plan, source, right_near, slot, sems.at[1 + place]))
    return copies


def masked_rows(plan, sizes_ref, result):
    me = lax.axis_index("mpo")
    here = lax.axis_index("bond")
    shape = (plan.rows, plan.width)
    row = lax.broadcasted_iota(jnp.int32, shape, 0) + me * plan.rows
    column = lax.broadcasted_iota(jnp.int32, shape, 1)
    row_ok = row < sector_limits(sizes_ref, plan.w, here, plan.n_bond)
    blocks = []
    for p, charge in enumerate(pair_charges()):
        if result[p] is None:
            blocks.append(jnp.zeros(shape, BF16))
            continue
        ok = row_ok & (column < sector_limits(sizes_ref, plan.w + plan.n_bond, here + charge, plan.n_bond))
        blocks.append(jnp.where(ok, result[p], 0.0).astype(BF16))
    return blocks


def whole_sum(values):
    return jnp.sum(jnp.sum(values, axis=1, keepdims=True), axis=0, keepdims=True)


def near_copies(places, refs, near, sems, count):
    copies = []
    for place, (array, index, _, _) in enumerate(places):
        source = refs[array] if index is None else refs[array].at[index]
        copies.append(pltpu.make_async_copy(source.at[pl.ds(0, count)], near.at[place], sems.at[place]))
    return copies


def first_kernel(plan, *refs):
    sizes_ref, refs = refs[0], refs[1:]
    psi_refs, refs = refs[: plan.n_near], refs[plan.n_near :]
    left_refs, refs = refs[: plan.n_mpo], refs[plan.n_mpo :]
    sites_ref, ys_out, fs_out, ls_out, first_out, second_out = refs[:6]
    fs, ls, wide, xs, ys, left_near, psi_near, left_sem, psi_sem, out_sem, y_sem = refs[6:]
    me = lax.axis_index("mpo")
    odd_rows = pl.ds(pl.multiple_of(lax.rem(me, 2) * plan.rows, plan.rows), plan.rows)
    left_copies = [
        pltpu.make_async_copy(source.at[:, odd_rows, :], left_near.at[r], left_sem.at[r])
        for r, source in enumerate(left_refs)
    ]
    psi_copies = near_copies(all_places(plan.n_mpo), psi_refs, psi_near, psi_sem, STATES)
    for copy in left_copies + psi_copies:
        copy.start()
    site_matrices(plan, sizes_ref, sites_ref, first_out, second_out)
    for copy in left_copies:
        copy.wait()
    fill_left(plan, sizes_ref, left_near, wide, ls)
    ls_copy = pltpu.make_async_copy(ls, ls_out, out_sem.at[0])
    ls_copy.start()
    for copy in psi_copies:
        copy.wait()
    fill_vector(plan, sizes_ref, psi_near, fs)
    fs_copy = pltpu.make_async_copy(fs, fs_out, out_sem.at[1])
    fs_copy.start()
    left_phase(plan, fs, ls, xs)
    tiles = ys.reshape(PAIRS, plan.w, plan.y_step, plan.width)

    def out_copy(index):
        rows = pl.ds(pl.multiple_of(index * Y_BLOCK, Y_BLOCK), Y_BLOCK)
        return pltpu.make_async_copy(tiles.at[:, :, rows, :], ys_out.at[:, :, rows, :], y_sem.at[index])

    middle_phase(
        plan, plan.n_mpo, Y_BLOCK, 2, xs, first_out, second_out, ys, lambda index: out_copy(index).start()
    )
    for index in range(plan.rows // Y_BLOCK):
        out_copy(index).wait()
    ls_copy.wait()
    fs_copy.wait()


def image_kernel(plan, sizes_ref, ys_ref, vector_ref, own_ref, *refs):
    far_refs, (image, ys, right_near, vector, y_sem, right_sem, v_sem) = refs[: plan.n_far], refs[plan.n_far :]
    me = lax.axis_index("mpo")
    rows_here = pl.ds(pl.multiple_of(me * plan.rows, plan.rows), plan.rows)
    charges = pair_charges()
    y_copies = {
        p: pltpu.make_async_copy(ys_ref.at[p], ys.at[p], y_sem.at[p]) for p in range(PAIRS) if charges[p] <= plan.far
    }
    r_copies = right_copies(plan, own_ref, far_refs, right_near, right_sem)
    v_copy = pltpu.make_async_copy(vector_ref.at[:, rows_here, :], vector, v_sem)
    stages = [r_copies[n] + [y_copies[p] for p in range(PAIRS) if charges[p] == n] for n in range(plan.far + 1)]
    for copy in [copy for some in stages[:AHEAD] for copy in some] + [v_copy]:
        copy.start()

    def ready(n):
        for copy in [copy for some in stages[n + AHEAD : n + AHEAD + 1] for copy in some]:
            copy.start()
        for copy in stages[n]:
            copy.wait()

    result = right_phase(plan, True, ys, plan.rows, right_near, ready)
    blocks = masked_rows(plan, sizes_ref, result)
    v_copy.wait()
    along = jnp.zeros((plan.rows, plan.width), F32)
    norm = jnp.zeros((plan.rows, plan.width), F32)
    for p, block in enumerate(blocks):
        image[p] = block
        field = vector[p].astype(F32)
        along = along + field * block.astype(F32)
        norm = norm + field * field
    along = whole_sum(along)
    norm = whole_sum(norm)
    ratio = jnp.where(norm > 0, along / jnp.where(norm > 0, norm, 1.0), 0.0)
    across = jnp.zeros((plan.rows, plan.width), F32)
    for p, block in enumerate(blocks):
        left_over = block.astype(F32) - ratio * vector[p].astype(F32)
        across = across + left_over * left_over
    across = whole_sum(across)
    line = lax.broadcasted_iota(jnp.int32, (8, plan.width), 0)
    sums = jnp.where(line == 0, along, jnp.where(line == 1, norm, jnp.where(line == 2, across, 0.0)))
    parts = []
    for _ in range(3):
        parts.append(sums.astype(BF16).astype(F32))
        sums = sums - parts[-1]
    parts.append(jnp.zeros((plan.rows - 24, plan.width), F32))
    image[PAIRS] = jnp.concatenate(parts, 0).astype(BF16)


def sums_of(piece):
    block = piece[PAIRS].astype(F32)
    return block[0:8] + block[8:16] + block[16:24]


def second_kernel(plan, count_all, n_parts, near, *refs):
    sizes_ref = refs[0]
    parts, refs = refs[1 : 1 + n_parts], refs[1 + n_parts :]
    image_refs, refs = refs[: plan.n_near], refs[plan.n_near :]
    vector_ref, ls_ref, first_ref, second_ref, own_ref = refs[:5]
    far_refs, refs = refs[5 : 5 + plan.n_far], refs[5 + plan.n_far :]
    outs, image_out = refs[: plan.n_mpo], refs[plan.n_mpo]
    fs, xs, ys, image_near, vector, ls, right_near, image_sem, field_sem, right_sem, out_sem = refs[plan.n_mpo + 1 :]
    me = lax.axis_index("mpo")
    image_copies = near_copies(block_places(plan.n_mpo), image_refs, image_near, image_sem, PAIRS + 1)
    v_copy = pltpu.make_async_copy(vector_ref, vector, field_sem.at[0])
    l_copy = pltpu.make_async_copy(ls_ref, ls, field_sem.at[1])
    r_copies = right_copies(plan, own_ref, far_refs, right_near, right_sem)
    for copy in [v_copy] + image_copies + [l_copy]:
        copy.start()
    for copy in image_copies:
        copy.wait()
    sums = merged([part[...] for part in parts] + (near_sums(plan, image_near) if near else []))
    rayleigh = sums[0:1, :] / sums[1:2, :]
    scale = lax.rsqrt(sums[2:3, :] / count_all + EPSILON)
    v_copy.wait()
    for place, (_, _, r, kind) in enumerate(block_places(plan.n_mpo)):
        slot, _ = sector_of(kind)
        start = slot * plan.width + lax.bitwise_xor(me, r) * plan.rows
        where = pl.ds(pl.multiple_of(start, plan.rows), plan.rows)
        for p in range(PAIRS):
            block = image_near[place, p].astype(F32)
            residual = block - rayleigh * vector[p, where, :].astype(F32)
            fs[p, where, :] = (residual * scale).astype(BF16)
    out_copies = []
    pairs_here = pl.ds(me * STATES, STATES)
    for place, (_, _, r, kind) in enumerate(block_places(plan.n_mpo)):
        if kind == 0:
            start = lax.bitwise_xor(me, r) * plan.rows
            rows = pl.ds(pl.multiple_of(start, plan.rows), plan.rows)
            out_copies.append(
                pltpu.make_async_copy(image_near.at[place, pairs_here], image_out.at[0, :, rows, :], out_sem.at[r])
            )
    for copy in out_copies + [copy for some in r_copies for copy in some]:
        copy.start()
    l_copy.wait()
    left_phase(plan, fs, ls, xs)
    middle_phase(plan, 1, 2 * Y_BLOCK, 2, xs, first_ref, second_ref, ys, lambda index: None)

    def ready(n):
        for copy in r_copies[n]:
            copy.wait()

    result = right_phase(plan, False, ys, plan.y_step, right_near, ready)
    rows = masked_rows(plan, sizes_ref, result)
    for p in range(PAIRS):
        ys[p, : plan.rows, :] = rows[p].astype(F32)
    for r, out in enumerate(outs):
        first = lax.bitwise_xor(me, r) * STATES
        for second in range(STATES):
            out[second] = ys[first + second, : plan.rows, :].astype(BF16)
    for copy in out_copies:
        copy.wait()


Y_BLOCK = 8
AHEAD = 2
COST_A = 1_000
COST_B = 4_000_000_000
VMEM = pl.BlockSpec(memory_space=pltpu.VMEM)
ANY = pl.BlockSpec(memory_space=pl.ANY)
SMEM = pl.BlockSpec(memory_space=pltpu.SMEM)
PARAMS = pltpu.CompilerParams(vmem_limit_bytes=52 * 1024 * 1024)
PARAMS_B = pltpu.CompilerParams(vmem_limit_bytes=52 * 1024 * 1024)


def shape_of(shape, dtype):
    return jax.ShapeDtypeStruct(shape, dtype)


def shards(psi, left_env, right_env, site_one, site_two, mpo_charge, left_sizes, right_sizes):
    n_mpo = lax.axis_size("mpo")
    n_bond = lax.axis_size("bond")
    width = psi.shape[2]
    plan = Plan(n_mpo, n_bond, width, right_env.shape[0])
    me = lax.axis_index("mpo")

    sites = jnp.transpose(jnp.stack([site_one, site_two]), (0, 3, 2, 4, 1))
    sites = sites.reshape(2, STATES * plan.w, STATES * plan.w)

    sizes = jnp.concatenate([mpo_charge, left_sizes, right_sizes])

    left_mine = left_env[:, 0]
    left_halves = []
    for r in range(0, n_mpo, 2):
        start = lax.bitwise_xor(me - lax.rem(me, 2), r) * plan.rows
        left_halves.append(lax.dynamic_slice_in_dim(left_mine, start, 2 * plan.rows, 1))
    right_here, left_halves[0] = lax.optimization_barrier((right_env, left_halves[0]))
    left_halves = [from_near(both, 0, 2 * r) if r else both for r, both in enumerate(left_halves)]
    psi_arrays, before = exchange_all(psi[0], (left_halves, sites, sizes))
    left_halves, sites, sizes = before
    left_pieces = [piece for both in left_halves for piece in (both, from_near(both, 0, 1))]

    right_far = right_exchange(right_here, plan.far)

    field_shape = (PAIRS, 3 * width, width)
    left_shape = (plan.rows * plan.w_pad, 3 * width)
    x_shape = (PAIRS, plan.rows * plan.w_pad, width)
    y_shape = (PAIRS, plan.y_step * plan.w, width)
    row_shape = (PAIRS, plan.rows, width)

    first_shape = (STATES * plan.w, STATES * plan.w_pad)
    second_shape = (2 * STATES * plan.w,) * 2
    y_out_shape = (PAIRS, plan.w, plan.rows, width)
    ys, vector, left_rows, first, second = pl.pallas_call(
        functools.partial(first_kernel, plan),
        out_shape=(
            shape_of(y_out_shape, F32),
            shape_of(field_shape, BF16),
            shape_of(left_shape, BF16),
            shape_of(first_shape, BF16),
            shape_of(second_shape, BF16),
        ),
        in_specs=[SMEM] + [ANY] * (plan.n_near + n_mpo) + [VMEM],
        out_specs=(ANY, ANY, ANY, VMEM, VMEM),
        scratch_shapes=[
            pltpu.VMEM(field_shape, BF16),
            pltpu.VMEM(left_shape, BF16),
            pltpu.VMEM((3, left_shape[0], width), F32),
            pltpu.VMEM(x_shape, F32),
            pltpu.VMEM(y_shape, F32),
            pltpu.VMEM((n_mpo, plan.w_here, plan.rows, width), BF16),
            pltpu.VMEM((3 * n_mpo,) + psi.shape[1:], BF16),
            pltpu.SemaphoreType.DMA((n_mpo,)),
            pltpu.SemaphoreType.DMA((3 * n_mpo,)),
            pltpu.SemaphoreType.DMA((2,)),
            pltpu.SemaphoreType.DMA((plan.rows // Y_BLOCK,)),
        ],
        compiler_params=PARAMS,
        cost_estimate=pl.CostEstimate(flops=COST_A, bytes_accessed=0, transcendentals=0),
        name="states_of_vector",
    )(
        sizes, *psi_arrays, *left_pieces, sites,
    )

    right_far, ys = lax.optimization_barrier((right_far, ys))
    right_pieces = handed_over(right_far, plan.far)
    right_scratch = pltpu.VMEM((plan.n_far + 1, plan.w, width, width), BF16)
    image_shape = (PAIRS + 1,) + row_shape[1:]
    image_rows = pl.pallas_call(
        functools.partial(image_kernel, plan),
        out_shape=shape_of(image_shape, BF16),
        in_specs=[SMEM] + [ANY] * (3 + plan.n_far),
        out_specs=VMEM,
        scratch_shapes=[
            pltpu.VMEM((PAIRS, plan.w * plan.rows, width), F32),
            right_scratch,
            pltpu.VMEM(row_shape, BF16),
            pltpu.SemaphoreType.DMA((PAIRS,)),
            pltpu.SemaphoreType.DMA((1 + plan.n_far,)),
            pltpu.SemaphoreType.DMA,
        ],
        compiler_params=PARAMS_B,
        cost_estimate=pl.CostEstimate(flops=COST_B, bytes_accessed=0, transcendentals=0),
        name="image_rows",
    )(sizes, ys.reshape(PAIRS, plan.w * plan.rows, width), vector, right_env, *right_pieces)

    image_here, image_first, image_mine = exchange(image_rows)
    blocks, _ = lax.optimization_barrier((image_here, image_mine[0]))
    sums = merged([sums_of(blocks[r]) for r in range(n_mpo)])
    near = n_bond == 4
    sums = far_sums(sums) if near else summed_over_bond(sums)
    last = max(image_mine)
    image_mine[last], sums = lax.optimization_barrier((image_mine[last], sums))
    image_other = handed_pairs(image_mine)
    if near:
        sums = sums + [from_near(sums[1], 0, 1)]

    count_all = n_bond * PAIRS * width * width
    *second_rows, image = pl.pallas_call(
        functools.partial(second_kernel, plan, float(count_all), len(sums), near),
        out_shape=(shape_of((STATES,) + row_shape[1:], BF16),) * n_mpo + (shape_of(psi.shape, BF16),),
        in_specs=[SMEM] + [VMEM] * len(sums) + [ANY] * (plan.n_near + 2) + [VMEM] * 2 + [ANY] * (1 + plan.n_far),
        out_specs=(VMEM,) * n_mpo + (ANY,),
        scratch_shapes=[
            pltpu.VMEM(field_shape, BF16),
            pltpu.VMEM(x_shape, F32),
            pltpu.VMEM(y_shape, F32),
            pltpu.VMEM((3 * n_mpo,) + image_shape, BF16),
            pltpu.VMEM(field_shape, BF16),
            pltpu.VMEM(left_shape, BF16),
            right_scratch,
            pltpu.SemaphoreType.DMA((3 * n_mpo,)),
            pltpu.SemaphoreType.DMA((2,)),
            pltpu.SemaphoreType.DMA((1 + plan.n_far,)),
            pltpu.SemaphoreType.DMA((n_mpo,)),
        ],
        compiler_params=PARAMS,
        cost_estimate=pl.CostEstimate(flops=COST_A, bytes_accessed=0, transcendentals=0),
        name="correction_image_rows",
    )(
        sizes, *sums, *by_place(image_here, image_first, image_mine, image_other), vector, left_rows,
        first, second, right_env, *right_pieces,
    )

    result = jnp.zeros((STATES, width, width), BF16)
    for r, block in enumerate(second_rows):
        block = from_near(block, 0, r) if r else block
        start = lax.bitwise_xor(me, r) * plan.rows
        result = lax.dynamic_update_slice_in_dim(result, block, start, 1)
    return (image, result[None])


def solution(mesh):
    in_specs = (
        P(("groups", "bond"), "mpo", None, None),
        P("mpo", ("groups", "bond"), None, None),
        P(None, ("groups", "bond"), None, None),
        P("groups", None, None, None),
        P("groups", None, None, None),
        P(),
        P("groups"),
        P("groups"),
    )
    out_specs = (P(("groups", "bond"), "mpo", None, None), P(("groups", "bond"), "mpo", None, None))
    return jax.shard_map(shards, mesh=mesh, in_specs=in_specs, out_specs=out_specs, check_vma=False)
```

```python
import functools

import jax
import jax.numpy as jnp
from jax import lax
from jax.experimental import pallas as pl
from jax.experimental.pallas import tpu as pltpu
from jax.sharding import PartitionSpec as P

EPSILON = 1e-06
STATE_CHARGES = (0, 1, 1, 2)
STATES = len(STATE_CHARGES)
PAIRS = STATES * STATES
RIM = 4
F32 = jnp.float32
BF16 = jnp.bfloat16
NT = (((1,), (1,)), ((), ()))


def pair_charges():
    return [left + right for left in STATE_CHARGES for right in STATE_CHARGES]


def round_up(value, step):
    return -(-value // step) * step


def from_near(value, step, flip):
    n_bond, n_mpo = lax.axis_size("bond"), lax.axis_size("mpo")
    pairs = [
        ((i + step) * n_mpo + (j ^ flip), i * n_mpo + j)
        for i in range(n_bond)
        for j in range(n_mpo)
        if 0 <= i + step < n_bond
    ]
    return lax.ppermute(value, ("bond", "mpo"), pairs)


def mpo_bits():
    count = lax.axis_size("mpo")
    bits = []
    while count > 1:
        count //= 2
        bits.append(count)
    return bits


def exchange(own):
    n_bond, n_mpo = lax.axis_size("bond"), lax.axis_size("mpo")
    pairs = [
        (i * n_mpo + j, (i + 1 - 2 * (j % 2)) * n_mpo + j)
        for i in range(n_bond)
        for j in range(n_mpo)
        if 0 <= i + 1 - 2 * (j % 2) < n_bond
    ]
    here = own_sector(own)
    first = jnp.stack([here[0], here[1]])
    mine = {}
    for r in range(0, n_mpo, 2):
        pair = jnp.stack([here[r], here[r ^ 1]]) if r else first
        mine[r] = lax.ppermute(pair, ("bond", "mpo"), pairs)
    return here, first, mine


def own_sector(own):
    here = {0: own, 1: from_near(own, 0, 1)}
    for bit in mpo_bits()[:-1]:
        here.update({r ^ bit: from_near(here[r], 0, bit) for r in sorted(here) if r % 2 == 0})
    for r in range(2, len(here) * 2 - 2, 2):
        here[r ^ 1] = from_near(here[r], 0, 1)
    return here


def exchange_all(own, before):
    n_mpo = lax.axis_size("mpo")
    low, high = from_near(own, -1, 0), from_near(own, 1, 0)
    here = own_sector(own)
    (low, high), _, before = lax.optimization_barrier(((low, high), here[n_mpo // 2], before))
    both = {0: jnp.stack([low, high])}
    for bit in mpo_bits():
        both.update({r ^ bit: from_near(pair, 0, bit) for r, pair in list(both.items())})
    rest = [here[r] for r in range(2, n_mpo)]
    return [jnp.stack([here[0], here[1]])] + rest + [both[r] for r in range(n_mpo)], before


def all_places(n_mpo):
    places = [(0, 0, 0, 0), (0, 1, 1, 0)] + [(r - 1, None, r, 0) for r in range(2, n_mpo)]
    return places + [(n_mpo - 1 + r, side, r, 3 + side) for r in range(n_mpo) for side in range(2)]


def handed_pairs(mine):
    return {r: from_near(pair, 0, 1) for r, pair in mine.items()}


def by_place(here, first, mine, other):
    evens = sorted(mine)
    rest = [here[r] for r in sorted(here) if r > 1]
    return [first] + rest + [mine[r] for r in evens] + [other[r] for r in evens]


def block_places(n_mpo):
    places = [(0, 0, 0, 0), (0, 1, 1, 0)] + [(r - 1, None, r, 0) for r in range(2, n_mpo)]
    for kind in (1, 2):
        for r in range(0, n_mpo, 2):
            array = n_mpo - 1 + (kind - 1) * (n_mpo // 2) + r // 2
            order = (r, r ^ 1) if kind == 1 else (r ^ 1, r)
            places += [(array, index, member, kind) for index, member in enumerate(order)]
    return places


def sector_of(kind):
    odd = lax.rem(lax.axis_index("mpo"), 2)
    if kind == 0:
        return 0, 0
    if kind > 2:
        return kind - 2, 2 * kind - 7
    above = odd if kind == 1 else 1 - odd
    return 1 + above, 2 * above - 1


def right_exchange(own, far):
    n_bond, n_mpo = lax.axis_size("bond"), lax.axis_size("mpo")
    arrays = []
    for first in range(1, far + 1, 2):
        pairs = [
            ((i + first + j % 2) * n_mpo + j, i * n_mpo + j)
            for i in range(n_bond)
            for j in range(n_mpo)
            if first + j % 2 <= far and i + first + j % 2 < n_bond
        ]
        arrays.append(lax.ppermute(own, ("bond", "mpo"), pairs))
    return arrays


def handed_over(arrays, far):
    n_bond, n_mpo = lax.axis_size("bond"), lax.axis_size("mpo")
    result = []
    for place, array in enumerate(arrays):
        pairs = [
            (i * n_mpo + j, i * n_mpo + (j ^ 1))
            for i in range(n_bond)
            for j in range(n_mpo)
            if 1 + 2 * place + j % 2 <= far
        ]
        result += [array, lax.ppermute(array, ("bond", "mpo"), pairs)]
    return result


def merged(parts):
    along = sum(part[0:1] for part in parts)
    norm = sum(part[1:2] for part in parts)
    ratio = jnp.where(norm > 0, along / jnp.where(norm > 0, norm, 1.0), 0.0)
    across = jnp.zeros_like(along)
    for part in parts:
        own = jnp.where(part[1:2] > 0, part[0:1] / jnp.where(part[1:2] > 0, part[1:2], 1.0), 0.0)
        gap = own - ratio
        across = across + part[2:3] + gap * gap * part[1:2]
    rest = jnp.zeros((parts[0].shape[0] - 3, parts[0].shape[1]), F32)
    return jnp.concatenate([along, norm, across, rest], 0)


def summed_over_bond(sums):
    n_bond = lax.axis_size("bond")
    reach, parts = 1, [sums]
    while reach < n_bond:
        if reach > 1:
            parts = [merged(parts)]
        radix = min(4, n_bond // reach)
        parts = parts + [
            lax.ppermute(parts[0], "bond", [(i ^ (reach * k), i) for i in range(n_bond)])
            for k in range(1, radix)
        ]
        reach *= radix
    return parts


def far_sums(sums):
    n_bond, n_mpo = lax.axis_size("bond"), lax.axis_size("mpo")
    pairs = [((i ^ (2 + j % 2)) * n_mpo + j, i * n_mpo + j) for i in range(n_bond) for j in range(n_mpo)]
    return [sums, lax.ppermute(sums, ("bond", "mpo"), pairs)]


def near_sums(plan, blocks):
    here = lax.axis_index("bond")
    parts = []
    for place, (_, _, _, kind) in enumerate(block_places(plan.n_mpo)):
        if kind > 0:
            wanted = here + sector_of(kind)[1] == lax.bitwise_xor(here, 1)
            parts.append(sums_of(blocks[place]) * jnp.where(wanted, 1.0, 0.0).astype(F32))
    return parts


def sector_limits(sizes_ref, first, sector, count):
    inside = (sector >= 0) & (sector < count)
    return jnp.where(inside, sizes_ref[first + jnp.clip(sector, 0, count - 1)], 0)


def state_charge(state):
    return (state + 1) // 2


class Plan:
    def __init__(self, n_mpo, n_bond, width, mpo_width):
        self.n_mpo = n_mpo
        self.n_bond = n_bond
        self.width = width
        self.w = mpo_width
        self.w_here = mpo_width // n_mpo
        self.w_pad = round_up(mpo_width, 8)
        self.rows = width // n_mpo
        self.y_step = self.rows + 8
        self.far = min(RIM, n_bond - 1)
        self.n_near = 2 * n_mpo - 1
        self.n_far = 2 * ((self.far + 1) // 2)


def fill_left(plan, sizes_ref, left_refs, wide, ls):
    me = lax.axis_index("mpo")
    odd_rows = pl.ds(pl.multiple_of(lax.rem(me, 2) * plan.rows, plan.rows), plan.rows)
    wide[...] = jnp.zeros_like(wide)
    for r in range(plan.n_mpo):
        owner = lax.bitwise_xor(me, r)
        for t in range(plan.w_here):
            w = owner * plan.w_here + t
            block = left_refs[r][t, odd_rows, :].astype(F32)
            for c, charge in enumerate((0, 1, -1)):
                factor = jnp.where(sizes_ref[w] == charge, 1.0, 0.0).astype(F32)
                wide[c, pl.ds(w, plan.rows, stride=plan.w_pad), :] = block * factor
    for c in range(3):
        ls[:, c * plan.width : (c + 1) * plan.width] = wide[c].astype(BF16)


def fill_vector(plan, sizes_ref, psi_blocks, fs):
    me = lax.axis_index("mpo")
    here = lax.axis_index("bond")
    row = lax.broadcasted_iota(jnp.int32, (plan.width, plan.width), 0)
    column = lax.broadcasted_iota(jnp.int32, (plan.width, plan.width), 1)
    for place, (_, _, r, kind) in enumerate(all_places(plan.n_mpo)):
        slot, step = sector_of(kind)
        sector = here + step
        first = lax.bitwise_xor(me, r)
        row_ok = row < sector_limits(sizes_ref, plan.w, sector, plan.n_bond)
        where = pl.ds(pl.multiple_of(slot * plan.width, plan.width), plan.width)
        for second in range(STATES):
            target = sector + state_charge(first) + STATE_CHARGES[second]
            ok = row_ok & (column < sector_limits(sizes_ref, plan.w + plan.n_bond, target, plan.n_bond))
            block = psi_blocks[place][second].astype(F32)
            fs[first * STATES + second, where, :] = jnp.where(ok, block, 0.0).astype(BF16)


def left_phase(plan, fs, ls, xs):
    def step(index, carry):
        p = index * 2
        both = jnp.concatenate([fs[p], fs[p + 1]], axis=1)
        done = jnp.dot(ls[...], both, preferred_element_type=F32)
        xs[p] = done[:, : plan.width]
        xs[p + 1] = done[:, plan.width :]
        return carry

    lax.fori_loop(0, PAIRS // 2, step, 0, unroll=8)


def site_matrices(plan, sizes_ref, sites_ref, first_out, second_out):
    w, pad = plan.w, plan.w_pad
    size = STATES * w

    def index(shape, axis):
        return lax.broadcasted_iota(jnp.int32, shape, axis)

    def charges(bond):
        total = jnp.zeros(bond.shape, jnp.int32)
        for v in range(w):
            total = jnp.where(bond == v, sizes_ref[v], total)
        return total

    row, column = index((size, size), 0), index((size, size), 1)
    local_step = state_charge(row // w) - state_charge(column // w)
    allowed = local_step == charges(row % w) - charges(column % w)
    first = jnp.where(allowed, sites_ref[0].astype(F32), 0.0).astype(BF16)
    second = jnp.where(allowed, sites_ref[1].astype(F32), 0.0).astype(BF16)

    into = (size, STATES * pad)
    spread_w = (index(into, 0) // w == index(into, 1) // pad) & (index(into, 0) % w == index(into, 1) % pad)
    first = jnp.dot(first, jnp.where(spread_w, 1.0, 0.0).astype(BF16), preferred_element_type=F32)
    first_out[...] = first.astype(BF16)

    into = (size, 2 * size)
    of, to = index(into, 0), index(into, 1)
    halves = []
    for k in range(2):
        spread_v = to == (of // w) * 2 * w + k * w + of % w
        halves.append(jnp.dot(second, jnp.where(spread_v, 1.0, 0.0).astype(BF16), preferred_element_type=F32))
    second_out[...] = jnp.concatenate(halves, 0).astype(BF16)


def middle_phase(plan, groups, block, unroll, xs, first_ref, second_ref, ys, done):
    w, pad = plan.w, plan.w_pad
    first = first_ref[...]
    second = second_ref[...]
    size = STATES * w
    if groups > 1:
        column = lax.broadcasted_iota(jnp.int32, first.shape, 1) % pad
        wide = first.astype(F32)
        rows = []
        for g in range(groups):
            ok = (column >= g * plan.w_here) & (column < (g + 1) * plan.w_here)
            rows.append(jnp.where(ok, wide, 0.0))
        first = jnp.concatenate(rows, 0).astype(BF16)

    def step(index, carry):
        middle = []
        for b in range(STATES):
            columns = []
            for one in range(block):
                start = pl.multiple_of((index * block + one) * pad, pad)
                columns.append(
                    jnp.concatenate([xs[a * STATES + b, pl.ds(start, pad), :] for a in range(STATES)], 0)
                )
            column = jnp.concatenate(columns, 1).astype(BF16)
            middle.append(jnp.dot(first, column, preferred_element_type=F32))
        for half in range(STATES // 2):
            total = None
            for g in range(groups):
                at = g * size + half * 2 * w
                column = jnp.concatenate([z[at : at + 2 * w] for z in middle], 0).astype(BF16)
                term = jnp.dot(second, column, preferred_element_type=F32)
                if groups > 1:
                    term = term.astype(BF16).astype(F32)
                total = term if total is None else total + term
            for k in range(2):
                for s2 in range(STATES):
                    at = k * size + s2 * w
                    for one in range(block):
                        rows = pl.ds(index * block + one, w, stride=plan.y_step)
                        ys[(2 * half + k) * STATES + s2, rows, :] = total[
                            at : at + w, one * plan.width : (one + 1) * plan.width
                        ]
        done(index)
        return carry

    lax.fori_loop(0, plan.rows // block, step, 0, unroll=unroll)


def right_phase(plan, split, ys, y_step, right_near, ready):
    result = [None] * PAIRS
    for n in range(plan.far + 1):
        ready(n)
        members = [p for p, charge in enumerate(pair_charges()) if charge == n]
        total = None
        for first in range(0, plan.w, plan.w_here):
            group = range(first, first + plan.w_here)
            right = jnp.concatenate([right_near[n, u] for u in group], 1)
            lines = []
            for p in members:
                parts = [ys[p, pl.ds(u * y_step, plan.rows), :] for u in group]
                lines.append(jnp.concatenate(parts, 1))
            field = jnp.concatenate(lines, 0)
            high = field.astype(BF16)
            if split:
                low = (field - high.astype(F32)).astype(BF16)
                high = jnp.concatenate([high, low], 0)
            term = lax.dot_general(high, right, NT, preferred_element_type=F32)
            total = term if total is None else total + term
        if split:
            half = total.shape[0] // 2
            total = total[:half] + total[half:]
        for place, p in enumerate(members):
            result[p] = total[place * plan.rows : (place + 1) * plan.rows]
    return result


class RightCopy:
    def __init__(self, plan, source, right_near, slot, sem):
        self.copy = pltpu.make_async_copy(source.at[:, 0], right_near.at[slot], sem)
        self.there = None if isinstance(slot, int) else slot <= plan.far

    def start(self):
        self.do(self.copy.start)

    def wait(self):
        self.do(self.copy.wait)

    def do(self, action):
        if self.there is None:
            action()
        else:
            pl.when(self.there)(action)


def right_copies(plan, own_ref, far_refs, right_near, sems):
    odd = lax.rem(lax.axis_index("mpo"), 2)
    copies = [[] for _ in range(plan.far + 1)]
    copies[0].append(RightCopy(plan, own_ref, right_near, 0, sems.at[0]))
    for place, source in enumerate(far_refs):
        first, other = 1 + 2 * (place // 2), place % 2
        slot = first + (1 - odd if other else odd)
        copies[first].append(RightCopy(plan, source, right_near, slot, sems.at[1 + place]))
    return copies


def masked_rows(plan, sizes_ref, result):
    me = lax.axis_index("mpo")
    here = lax.axis_index("bond")
    shape = (plan.rows, plan.width)
    row = lax.broadcasted_iota(jnp.int32, shape, 0) + me * plan.rows
    column = lax.broadcasted_iota(jnp.int32, shape, 1)
    row_ok = row < sector_limits(sizes_ref, plan.w, here, plan.n_bond)
    blocks = []
    for p, charge in enumerate(pair_charges()):
        if result[p] is None:
            blocks.append(jnp.zeros(shape, BF16))
            continue
        ok = row_ok & (column < sector_limits(sizes_ref, plan.w + plan.n_bond, here + charge, plan.n_bond))
        blocks.append(jnp.where(ok, result[p], 0.0).astype(BF16))
    return blocks


def whole_sum(values):
    return jnp.sum(jnp.sum(values, axis=1, keepdims=True), axis=0, keepdims=True)


def near_blocks(places, refs):
    return [refs[array] if index is None else refs[array].at[index] for array, index, _, _ in places]


def first_kernel(plan, *refs):
    sizes_ref, refs = refs[0], refs[1:]
    psi_refs, refs = refs[: plan.n_near], refs[plan.n_near :]
    left_refs, refs = refs[: plan.n_mpo], refs[plan.n_mpo :]
    sites_ref, ys_out, fs_out, ls_out, first_out, second_out = refs[:6]
    fs, ls, wide, xs, ys, out_sem, y_sem = refs[6:]
    site_matrices(plan, sizes_ref, sites_ref, first_out, second_out)
    fill_left(plan, sizes_ref, left_refs, wide, ls)
    ls_copy = pltpu.make_async_copy(ls, ls_out, out_sem.at[0])
    ls_copy.start()
    fill_vector(plan, sizes_ref, near_blocks(all_places(plan.n_mpo), psi_refs), fs)
    fs_copy = pltpu.make_async_copy(fs, fs_out, out_sem.at[1])
    fs_copy.start()
    left_phase(plan, fs, ls, xs)
    tiles = ys.reshape(PAIRS, plan.w, plan.y_step, plan.width)

    def out_copy(index):
        rows = pl.ds(pl.multiple_of(index * Y_BLOCK, Y_BLOCK), Y_BLOCK)
        return pltpu.make_async_copy(tiles.at[:, :, rows, :], ys_out.at[:, :, rows, :], y_sem.at[index])

    middle_phase(
        plan, plan.n_mpo, Y_BLOCK, 2, xs, first_out, second_out, ys, lambda index: out_copy(index).start()
    )
    for index in range(plan.rows // Y_BLOCK):
        out_copy(index).wait()
    ls_copy.wait()
    fs_copy.wait()


def image_kernel(plan, sizes_ref, ys_ref, vector_ref, own_ref, *refs):
    far_refs, (image, ys, right_near, vector, y_sem, right_sem, v_sem) = refs[: plan.n_far], refs[plan.n_far :]
    me = lax.axis_index("mpo")
    rows_here = pl.ds(pl.multiple_of(me * plan.rows, plan.rows), plan.rows)
    charges = pair_charges()
    y_copies = {
        p: pltpu.make_async_copy(ys_ref.at[p], ys.at[p], y_sem.at[p]) for p in range(PAIRS) if charges[p] <= plan.far
    }
    r_copies = right_copies(plan, own_ref, far_refs, right_near, right_sem)
    v_copy = pltpu.make_async_copy(vector_ref.at[:, rows_here, :], vector, v_sem)
    stages = [r_copies[n] + [y_copies[p] for p in range(PAIRS) if charges[p] == n] for n in range(plan.far + 1)]
    for copy in [copy for some in stages[:AHEAD] for copy in some] + [v_copy]:
        copy.start()

    def ready(n):
        for copy in [copy for some in stages[n + AHEAD : n + AHEAD + 1] for copy in some]:
            copy.start()
        for copy in stages[n]:
            copy.wait()

    result = right_phase(plan, True, ys, plan.rows, right_near, ready)
    blocks = masked_rows(plan, sizes_ref, result)
    v_copy.wait()
    along = jnp.zeros((plan.rows, plan.width), F32)
    norm = jnp.zeros((plan.rows, plan.width), F32)
    for p, block in enumerate(blocks):
        image[p] = block
        field = vector[p].astype(F32)
        along = along + field * block.astype(F32)
        norm = norm + field * field
    along = whole_sum(along)
    norm = whole_sum(norm)
    ratio = jnp.where(norm > 0, along / jnp.where(norm > 0, norm, 1.0), 0.0)
    across = jnp.zeros((plan.rows, plan.width), F32)
    for p, block in enumerate(blocks):
        left_over = block.astype(F32) - ratio * vector[p].astype(F32)
        across = across + left_over * left_over
    across = whole_sum(across)
    line = lax.broadcasted_iota(jnp.int32, (8, plan.width), 0)
    sums = jnp.where(line == 0, along, jnp.where(line == 1, norm, jnp.where(line == 2, across, 0.0)))
    parts = []
    for _ in range(3):
        parts.append(sums.astype(BF16).astype(F32))
        sums = sums - parts[-1]
    parts.append(jnp.zeros((plan.rows - 24, plan.width), F32))
    image[PAIRS] = jnp.concatenate(parts, 0).astype(BF16)


def sums_of(piece):
    block = piece[PAIRS].astype(F32)
    return block[0:8] + block[8:16] + block[16:24]


def second_kernel(plan, count_all, n_parts, near, *refs):
    sizes_ref = refs[0]
    parts, refs = refs[1 : 1 + n_parts], refs[1 + n_parts :]
    image_refs, refs = refs[: plan.n_near], refs[plan.n_near :]
    vector_ref, ls_ref, first_ref, second_ref, own_ref = refs[:5]
    far_refs, refs = refs[5 : 5 + plan.n_far], refs[5 + plan.n_far :]
    outs, image_out = refs[: plan.n_mpo], refs[plan.n_mpo]
    fs, xs, ys, vector, ls, right_near, field_sem, right_sem, out_sem = refs[plan.n_mpo + 1 :]
    me = lax.axis_index("mpo")
    blocks = near_blocks(block_places(plan.n_mpo), image_refs)
    v_copy = pltpu.make_async_copy(vector_ref, vector, field_sem.at[0])
    l_copy = pltpu.make_async_copy(ls_ref, ls, field_sem.at[1])
    r_copies = right_copies(plan, own_ref, far_refs, right_near, right_sem)
    for copy in [v_copy, l_copy]:
        copy.start()
    sums = merged([part[...] for part in parts] + (near_sums(plan, blocks) if near else []))
    rayleigh = sums[0:1, :] / sums[1:2, :]
    scale = lax.rsqrt(sums[2:3, :] / count_all + EPSILON)
    v_copy.wait()
    for place, (_, _, r, kind) in enumerate(block_places(plan.n_mpo)):
        slot, _ = sector_of(kind)
        start = slot * plan.width + lax.bitwise_xor(me, r) * plan.rows
        where = pl.ds(pl.multiple_of(start, plan.rows), plan.rows)
        for p in range(PAIRS):
            block = blocks[place][p].astype(F32)
            residual = block - rayleigh * vector[p, where, :].astype(F32)
            fs[p, where, :] = (residual * scale).astype(BF16)
    out_copies = []
    pairs_here = pl.ds(me * STATES, STATES)
    for place, (_, _, r, kind) in enumerate(block_places(plan.n_mpo)):
        if kind == 0:
            start = lax.bitwise_xor(me, r) * plan.rows
            rows = pl.ds(pl.multiple_of(start, plan.rows), plan.rows)
            out_copies.append(
                pltpu.make_async_copy(blocks[place].at[pairs_here], image_out.at[0, :, rows, :], out_sem.at[r])
            )
    for copy in out_copies + [copy for some in r_copies for copy in some]:
        copy.start()
    l_copy.wait()
    left_phase(plan, fs, ls, xs)
    middle_phase(plan, 1, 2 * Y_BLOCK, 2, xs, first_ref, second_ref, ys, lambda index: None)

    def ready(n):
        for copy in r_copies[n]:
            copy.wait()

    result = right_phase(plan, False, ys, plan.y_step, right_near, ready)
    rows = masked_rows(plan, sizes_ref, result)
    for p in range(PAIRS):
        ys[p, : plan.rows, :] = rows[p].astype(F32)
    for r, out in enumerate(outs):
        first = lax.bitwise_xor(me, r) * STATES
        for second in range(STATES):
            out[second] = ys[first + second, : plan.rows, :].astype(BF16)
    for copy in out_copies:
        copy.wait()


Y_BLOCK = 8
AHEAD = 2
COST_A = 1_000
COST_B = 4_000_000_000
VMEM = pl.BlockSpec(memory_space=pltpu.VMEM)
ANY = pl.BlockSpec(memory_space=pl.ANY)
SMEM = pl.BlockSpec(memory_space=pltpu.SMEM)
PARAMS = pltpu.CompilerParams(vmem_limit_bytes=52 * 1024 * 1024)
PARAMS_B = pltpu.CompilerParams(vmem_limit_bytes=52 * 1024 * 1024)


def shape_of(shape, dtype):
    return jax.ShapeDtypeStruct(shape, dtype)


def shards(psi, left_env, right_env, site_one, site_two, mpo_charge, left_sizes, right_sizes):
    n_mpo = lax.axis_size("mpo")
    n_bond = lax.axis_size("bond")
    width = psi.shape[2]
    plan = Plan(n_mpo, n_bond, width, right_env.shape[0])
    me = lax.axis_index("mpo")

    sites = jnp.transpose(jnp.stack([site_one, site_two]), (0, 3, 2, 4, 1))
    sites = sites.reshape(2, STATES * plan.w, STATES * plan.w)

    sizes = jnp.concatenate([mpo_charge, left_sizes, right_sizes])

    left_mine = left_env[:, 0]
    left_halves = []
    for r in range(0, n_mpo, 2):
        start = lax.bitwise_xor(me - lax.rem(me, 2), r) * plan.rows
        left_halves.append(lax.dynamic_slice_in_dim(left_mine, start, 2 * plan.rows, 1))
    right_here, left_halves[0] = lax.optimization_barrier((right_env, left_halves[0]))
    left_halves = [from_near(both, 0, 2 * r) if r else both for r, both in enumerate(left_halves)]
    psi_arrays, before = exchange_all(psi[0], (left_halves, sites, sizes))
    left_halves, sites, sizes = before
    left_pieces = [piece for both in left_halves for piece in (both, from_near(both, 0, 1))]

    right_far = right_exchange(right_here, plan.far)

    field_shape = (PAIRS, 3 * width, width)
    left_shape = (plan.rows * plan.w_pad, 3 * width)
    x_shape = (PAIRS, plan.rows * plan.w_pad, width)
    y_shape = (PAIRS, plan.y_step * plan.w, width)
    row_shape = (PAIRS, plan.rows, width)

    first_shape = (STATES * plan.w, STATES * plan.w_pad)
    second_shape = (2 * STATES * plan.w,) * 2
    y_out_shape = (PAIRS, plan.w, plan.rows, width)
    ys, vector, left_rows, first, second = pl.pallas_call(
        functools.partial(first_kernel, plan),
        out_shape=(
            shape_of(y_out_shape, F32),
            shape_of(field_shape, BF16),
            shape_of(left_shape, BF16),
            shape_of(first_shape, BF16),
            shape_of(second_shape, BF16),
        ),
        in_specs=[SMEM] + [VMEM] * (plan.n_near + n_mpo + 1),
        out_specs=(ANY, ANY, ANY, VMEM, VMEM),
        scratch_shapes=[
            pltpu.VMEM(field_shape, BF16),
            pltpu.VMEM(left_shape, BF16),
            pltpu.VMEM((3, left_shape[0], width), F32),
            pltpu.VMEM(x_shape, F32),
            pltpu.VMEM(y_shape, F32),
            pltpu.SemaphoreType.DMA((2,)),
            pltpu.SemaphoreType.DMA((plan.rows // Y_BLOCK,)),
        ],
        compiler_params=PARAMS,
        cost_estimate=pl.CostEstimate(flops=COST_A, bytes_accessed=0, transcendentals=0),
        name="states_of_vector",
    )(
        sizes, *psi_arrays, *left_pieces, sites,
    )

    right_far, ys = lax.optimization_barrier((right_far, ys))
    right_pieces = handed_over(right_far, plan.far)
    right_scratch = pltpu.VMEM((plan.n_far + 1, plan.w, width, width), BF16)
    image_shape = (PAIRS + 1,) + row_shape[1:]
    image_rows = pl.pallas_call(
        functools.partial(image_kernel, plan),
        out_shape=shape_of(image_shape, BF16),
        in_specs=[SMEM] + [ANY] * (3 + plan.n_far),
        out_specs=VMEM,
        scratch_shapes=[
            pltpu.VMEM((PAIRS, plan.w * plan.rows, width), F32),
            right_scratch,
            pltpu.VMEM(row_shape, BF16),
            pltpu.SemaphoreType.DMA((PAIRS,)),
            pltpu.SemaphoreType.DMA((1 + plan.n_far,)),
            pltpu.SemaphoreType.DMA,
        ],
        compiler_params=PARAMS_B,
        cost_estimate=pl.CostEstimate(flops=COST_B, bytes_accessed=0, transcendentals=0),
        name="image_rows",
    )(sizes, ys.reshape(PAIRS, plan.w * plan.rows, width), vector, right_env, *right_pieces)

    image_here, image_first, image_mine = exchange(image_rows)
    blocks, _ = lax.optimization_barrier((image_here, image_mine[0]))
    sums = merged([sums_of(blocks[r]) for r in range(n_mpo)])
    near = n_bond == 4
    sums = far_sums(sums) if near else summed_over_bond(sums)
    last = max(image_mine)
    image_mine[last], sums = lax.optimization_barrier((image_mine[last], sums))
    image_other = handed_pairs(image_mine)
    if near:
        sums = sums + [from_near(sums[1], 0, 1)]

    count_all = n_bond * PAIRS * width * width
    *second_rows, image = pl.pallas_call(
        functools.partial(second_kernel, plan, float(count_all), len(sums), near),
        out_shape=(shape_of((STATES,) + row_shape[1:], BF16),) * n_mpo + (shape_of(psi.shape, BF16),),
        in_specs=[SMEM] + [VMEM] * (len(sums) + plan.n_near) + [ANY] * 2 + [VMEM] * 2 + [ANY] * (1 + plan.n_far),
        out_specs=(VMEM,) * n_mpo + (ANY,),
        scratch_shapes=[
            pltpu.VMEM(field_shape, BF16),
            pltpu.VMEM(x_shape, F32),
            pltpu.VMEM(y_shape, F32),
            pltpu.VMEM(field_shape, BF16),
            pltpu.VMEM(left_shape, BF16),
            right_scratch,
            pltpu.SemaphoreType.DMA((2,)),
            pltpu.SemaphoreType.DMA((1 + plan.n_far,)),
            pltpu.SemaphoreType.DMA((n_mpo,)),
        ],
        compiler_params=PARAMS,
        cost_estimate=pl.CostEstimate(flops=COST_A, bytes_accessed=0, transcendentals=0),
        name="correction_image_rows",
    )(
        sizes, *sums, *by_place(image_here, image_first, image_mine, image_other), vector, left_rows,
        first, second, right_env, *right_pieces,
    )

    result = jnp.zeros((STATES, width, width), BF16)
    for r, block in enumerate(second_rows):
        block = from_near(block, 0, r) if r else block
        start = lax.bitwise_xor(me, r) * plan.rows
        result = lax.dynamic_update_slice_in_dim(result, block, start, 1)
    return (image, result[None])


def solution(mesh):
    in_specs = (
        P(("groups", "bond"), "mpo", None, None),
        P("mpo", ("groups", "bond"), None, None),
        P(None, ("groups", "bond"), None, None),
        P("groups", None, None, None),
        P("groups", None, None, None),
        P(),
        P("groups"),
        P("groups"),
    )
    out_specs = (P(("groups", "bond"), "mpo", None, None), P(("groups", "bond"), "mpo", None, None))
    return jax.shard_map(shards, mesh=mesh, in_specs=in_specs, out_specs=out_specs, check_vma=False)
```

```python
import functools

import jax
import jax.numpy as jnp
from jax import lax
from jax.experimental import pallas as pl
from jax.experimental.pallas import tpu as pltpu
from jax.sharding import PartitionSpec as P

EPSILON = 1e-06
STATE_CHARGES = (0, 1, 1, 2)
STATES = len(STATE_CHARGES)
PAIRS = STATES * STATES
RIM = 4
F32 = jnp.float32
BF16 = jnp.bfloat16
NT = (((1,), (1,)), ((), ()))


def pair_charges():
    return [left + right for left in STATE_CHARGES for right in STATE_CHARGES]


def round_up(value, step):
    return -(-value // step) * step


def from_near(value, step, flip):
    n_bond, n_mpo = lax.axis_size("bond"), lax.axis_size("mpo")
    pairs = [
        ((i + step) * n_mpo + (j ^ flip), i * n_mpo + j)
        for i in range(n_bond)
        for j in range(n_mpo)
        if 0 <= i + step < n_bond
    ]
    return lax.ppermute(value, ("bond", "mpo"), pairs)


def mpo_bits():
    count = lax.axis_size("mpo")
    bits = []
    while count > 1:
        count //= 2
        bits.append(count)
    return bits


def exchange(own):
    n_bond, n_mpo = lax.axis_size("bond"), lax.axis_size("mpo")
    pairs = [
        (i * n_mpo + j, (i + 1 - 2 * (j % 2)) * n_mpo + j)
        for i in range(n_bond)
        for j in range(n_mpo)
        if 0 <= i + 1 - 2 * (j % 2) < n_bond
    ]
    here = own_sector(own)
    first = jnp.stack([here[0], here[1]])
    mine = {}
    for r in range(0, n_mpo, 2):
        pair = jnp.stack([here[r], here[r ^ 1]]) if r else first
        mine[r] = lax.ppermute(pair, ("bond", "mpo"), pairs)
    return here, first, mine


def own_sector(own):
    here = {0: own, 1: from_near(own, 0, 1)}
    for bit in mpo_bits()[:-1]:
        here.update({r ^ bit: from_near(here[r], 0, bit) for r in sorted(here) if r % 2 == 0})
    for r in range(2, len(here) * 2 - 2, 2):
        here[r ^ 1] = from_near(here[r], 0, 1)
    return here


def exchange_all(own, before):
    n_mpo = lax.axis_size("mpo")
    low, high = from_near(own, -1, 0), from_near(own, 1, 0)
    here = own_sector(own)
    (low, high), _, before = lax.optimization_barrier(((low, high), here[n_mpo // 2], before))
    both = {0: jnp.stack([low, high])}
    for bit in mpo_bits():
        both.update({r ^ bit: from_near(pair, 0, bit) for r, pair in list(both.items())})
    rest = [here[r] for r in range(2, n_mpo)]
    return [jnp.stack([here[0], here[1]])] + rest + [both[r] for r in range(n_mpo)], before


def all_places(n_mpo):
    places = [(0, 0, 0, 0), (0, 1, 1, 0)] + [(r - 1, None, r, 0) for r in range(2, n_mpo)]
    return places + [(n_mpo - 1 + r, side, r, 3 + side) for r in range(n_mpo) for side in range(2)]


def handed_pairs(mine):
    return {r: from_near(pair, 0, 1) for r, pair in mine.items()}


def by_place(here, first, mine, other):
    evens = sorted(mine)
    rest = [here[r] for r in sorted(here) if r > 1]
    return [first] + rest + [mine[r] for r in evens] + [other[r] for r in evens]


def block_places(n_mpo):
    places = [(0, 0, 0, 0), (0, 1, 1, 0)] + [(r - 1, None, r, 0) for r in range(2, n_mpo)]
    for kind in (1, 2):
        for r in range(0, n_mpo, 2):
            array = n_mpo - 1 + (kind - 1) * (n_mpo // 2) + r // 2
            order = (r, r ^ 1) if kind == 1 else (r ^ 1, r)
            places += [(array, index, member, kind) for index, member in enumerate(order)]
    return places


def sector_of(kind):
    odd = lax.rem(lax.axis_index("mpo"), 2)
    if kind == 0:
        return 0, 0
    if kind > 2:
        return kind - 2, 2 * kind - 7
    above = odd if kind == 1 else 1 - odd
    return 1 + above, 2 * above - 1


def right_exchange(own, far):
    n_bond, n_mpo = lax.axis_size("bond"), lax.axis_size("mpo")
    pairs = [
        ((i + 1 + j % 2) * n_mpo + j, i * n_mpo + j)
        for i in range(n_bond)
        for j in range(n_mpo)
        if 1 + j % 2 <= far and i + 1 + j % 2 < n_bond
    ]
    arrays = [lax.ppermute(own, ("bond", "mpo"), pairs)]
    half = own.shape[0] // 2
    part = lax.dynamic_slice_in_dim(own, lax.rem(lax.axis_index("mpo"), 2) * half, half, 0)
    return arrays + [from_near(part, d, 0) for d in range(3, far + 1)]


def handed_over(arrays):
    return [piece for array in arrays for piece in (array, from_near(array, 0, 1))]


def merged(parts):
    along = sum(part[0:1] for part in parts)
    norm = sum(part[1:2] for part in parts)
    ratio = jnp.where(norm > 0, along / jnp.where(norm > 0, norm, 1.0), 0.0)
    across = jnp.zeros_like(along)
    for part in parts:
        own = jnp.where(part[1:2] > 0, part[0:1] / jnp.where(part[1:2] > 0, part[1:2], 1.0), 0.0)
        gap = own - ratio
        across = across + part[2:3] + gap * gap * part[1:2]
    rest = jnp.zeros((parts[0].shape[0] - 3, parts[0].shape[1]), F32)
    return jnp.concatenate([along, norm, across, rest], 0)


def summed_over_bond(sums):
    n_bond = lax.axis_size("bond")
    reach, parts = 1, [sums]
    while reach < n_bond:
        if reach > 1:
            parts = [merged(parts)]
        radix = min(4, n_bond // reach)
        parts = parts + [
            lax.ppermute(parts[0], "bond", [(i ^ (reach * k), i) for i in range(n_bond)])
            for k in range(1, radix)
        ]
        reach *= radix
    return parts


def far_sums(sums):
    n_bond, n_mpo = lax.axis_size("bond"), lax.axis_size("mpo")
    pairs = [((i ^ (2 + j % 2)) * n_mpo + j, i * n_mpo + j) for i in range(n_bond) for j in range(n_mpo)]
    return [sums, lax.ppermute(sums, ("bond", "mpo"), pairs)]


def near_sums(plan, blocks):
    here = lax.axis_index("bond")
    parts = []
    for place, (_, _, _, kind) in enumerate(block_places(plan.n_mpo)):
        if kind > 0:
            wanted = here + sector_of(kind)[1] == lax.bitwise_xor(here, 1)
            parts.append(sums_of(blocks[place]) * jnp.where(wanted, 1.0, 0.0).astype(F32))
    return parts


def sector_limits(sizes_ref, first, sector, count):
    inside = (sector >= 0) & (sector < count)
    return jnp.where(inside, sizes_ref[first + jnp.clip(sector, 0, count - 1)], 0)


def state_charge(state):
    return (state + 1) // 2


class Plan:
    def __init__(self, n_mpo, n_bond, width, mpo_width):
        self.n_mpo = n_mpo
        self.n_bond = n_bond
        self.width = width
        self.w = mpo_width
        self.w_here = mpo_width // n_mpo
        self.w_pad = round_up(mpo_width, 8)
        self.rows = width // n_mpo
        self.y_step = self.rows + 8
        self.far = min(RIM, n_bond - 1)
        self.n_near = 2 * n_mpo - 1
        self.slots = max(3, self.far + 1)
        self.n_far = 2 * max(1, self.far - 1)


def fill_left(plan, sizes_ref, left_refs, wide, ls):
    me = lax.axis_index("mpo")
    odd_rows = pl.ds(pl.multiple_of(lax.rem(me, 2) * plan.rows, plan.rows), plan.rows)
    wide[...] = jnp.zeros_like(wide)
    for r in range(plan.n_mpo):
        owner = lax.bitwise_xor(me, r)
        for t in range(plan.w_here):
            w = owner * plan.w_here + t
            block = left_refs[r][t, odd_rows, :].astype(F32)
            for c, charge in enumerate((0, 1, -1)):
                factor = jnp.where(sizes_ref[w] == charge, 1.0, 0.0).astype(F32)
                wide[c, pl.ds(w, plan.rows, stride=plan.w_pad), :] = block * factor
    for c in range(3):
        ls[:, c * plan.width : (c + 1) * plan.width] = wide[c].astype(BF16)


def fill_vector(plan, sizes_ref, psi_blocks, fs):
    me = lax.axis_index("mpo")
    here = lax.axis_index("bond")
    row = lax.broadcasted_iota(jnp.int32, (plan.width, plan.width), 0)
    column = lax.broadcasted_iota(jnp.int32, (plan.width, plan.width), 1)
    for place, (_, _, r, kind) in enumerate(all_places(plan.n_mpo)):
        slot, step = sector_of(kind)
        sector = here + step
        first = lax.bitwise_xor(me, r)
        row_ok = row < sector_limits(sizes_ref, plan.w, sector, plan.n_bond)
        where = pl.ds(pl.multiple_of(slot * plan.width, plan.width), plan.width)
        for second in range(STATES):
            target = sector + state_charge(first) + STATE_CHARGES[second]
            ok = row_ok & (column < sector_limits(sizes_ref, plan.w + plan.n_bond, target, plan.n_bond))
            block = psi_blocks[place][second].astype(F32)
            fs[first * STATES + second, where, :] = jnp.where(ok, block, 0.0).astype(BF16)


def left_phase(plan, fs, ls, xs):
    def step(index, carry):
        p = index * 2
        both = jnp.concatenate([fs[p], fs[p + 1]], axis=1)
        done = jnp.dot(ls[...], both, preferred_element_type=F32)
        xs[p] = done[:, : plan.width]
        xs[p + 1] = done[:, plan.width :]
        return carry

    lax.fori_loop(0, PAIRS // 2, step, 0, unroll=8)


def site_matrices(plan, sizes_ref, sites_ref, first_out, second_out):
    w, pad = plan.w, plan.w_pad
    size = STATES * w

    def index(shape, axis):
        return lax.broadcasted_iota(jnp.int32, shape, axis)

    def charges(bond):
        total = jnp.zeros(bond.shape, jnp.int32)
        for v in range(w):
            total = jnp.where(bond == v, sizes_ref[v], total)
        return total

    row, column = index((size, size), 0), index((size, size), 1)
    local_step = state_charge(row // w) - state_charge(column // w)
    allowed = local_step == charges(row % w) - charges(column % w)
    first = jnp.where(allowed, sites_ref[0].astype(F32), 0.0).astype(BF16)
    second = jnp.where(allowed, sites_ref[1].astype(F32), 0.0).astype(BF16)

    into = (size, STATES * pad)
    spread_w = (index(into, 0) // w == index(into, 1) // pad) & (index(into, 0) % w == index(into, 1) % pad)
    first = jnp.dot(first, jnp.where(spread_w, 1.0, 0.0).astype(BF16), preferred_element_type=F32)
    first_out[...] = first.astype(BF16)

    into = (size, 2 * size)
    of, to = index(into, 0), index(into, 1)
    halves = []
    for k in range(2):
        spread_v = to == (of // w) * 2 * w + k * w + of % w
        halves.append(jnp.dot(second, jnp.where(spread_v, 1.0, 0.0).astype(BF16), preferred_element_type=F32))
    second_out[...] = jnp.concatenate(halves, 0).astype(BF16)


def middle_phase(plan, groups, block, unroll, xs, first_ref, second_ref, ys, done):
    w, pad = plan.w, plan.w_pad
    first = first_ref[...]
    second = second_ref[...]
    size = STATES * w
    if groups > 1:
        column = lax.broadcasted_iota(jnp.int32, first.shape, 1) % pad
        wide = first.astype(F32)
        rows = []
        for g in range(groups):
            ok = (column >= g * plan.w_here) & (column < (g + 1) * plan.w_here)
            rows.append(jnp.where(ok, wide, 0.0))
        first = jnp.concatenate(rows, 0).astype(BF16)

    def step(index, carry):
        middle = []
        for b in range(STATES):
            columns = []
            for one in range(block):
                start = pl.multiple_of((index * block + one) * pad, pad)
                columns.append(
                    jnp.concatenate([xs[a * STATES + b, pl.ds(start, pad), :] for a in range(STATES)], 0)
                )
            column = jnp.concatenate(columns, 1).astype(BF16)
            middle.append(jnp.dot(first, column, preferred_element_type=F32))
        for half in range(STATES // 2):
            total = None
            for g in range(groups):
                at = g * size + half * 2 * w
                column = jnp.concatenate([z[at : at + 2 * w] for z in middle], 0).astype(BF16)
                term = jnp.dot(second, column, preferred_element_type=F32)
                if groups > 1:
                    term = term.astype(BF16).astype(F32)
                total = term if total is None else total + term
            for k in range(2):
                for s2 in range(STATES):
                    at = k * size + s2 * w
                    for one in range(block):
                        rows = pl.ds(index * block + one, w, stride=plan.y_step)
                        ys[(2 * half + k) * STATES + s2, rows, :] = total[
                            at : at + w, one * plan.width : (one + 1) * plan.width
                        ]
        done(index)
        return carry

    lax.fori_loop(0, plan.rows // block, step, 0, unroll=unroll)


def right_phase(plan, split, ys, y_step, right_near, ready):
    result = [None] * PAIRS
    for n in range(plan.far + 1):
        ready(n)
        members = [p for p, charge in enumerate(pair_charges()) if charge == n]
        total = None
        for first in range(0, plan.w, plan.w_here):
            group = range(first, first + plan.w_here)
            right = jnp.concatenate([right_near[n, u] for u in group], 1)
            lines = []
            for p in members:
                parts = [ys[p, pl.ds(u * y_step, plan.rows), :] for u in group]
                lines.append(jnp.concatenate(parts, 1))
            field = jnp.concatenate(lines, 0)
            high = field.astype(BF16)
            if split:
                low = (field - high.astype(F32)).astype(BF16)
                high = jnp.concatenate([high, low], 0)
            term = lax.dot_general(high, right, NT, preferred_element_type=F32)
            total = term if total is None else total + term
        if split:
            half = total.shape[0] // 2
            total = total[:half] + total[half:]
        for place, p in enumerate(members):
            result[p] = total[place * plan.rows : (place + 1) * plan.rows]
    return result


class RightCopy:
    def __init__(self, plan, source, target, sem, slot=None):
        self.copy = pltpu.make_async_copy(source.at[:, 0], target, sem)
        self.there = None if slot is None else slot <= plan.far

    def start(self):
        self.do(self.copy.start)

    def wait(self):
        self.do(self.copy.wait)

    def do(self, action):
        if self.there is None:
            action()
        else:
            pl.when(self.there)(action)


def right_copies(plan, own_ref, far_refs, right_near, sems):
    odd = lax.rem(lax.axis_index("mpo"), 2)
    half = plan.w // 2
    copies = [[] for _ in range(plan.far + 1)]
    copies[0].append(RightCopy(plan, own_ref, right_near.at[0], sems.at[0]))
    for place, source in enumerate(far_refs):
        side = 1 - odd if place % 2 else odd
        sem = sems.at[1 + place]
        if place < 2:
            copies[1].append(RightCopy(plan, source, right_near.at[1 + side], sem, 1 + side))
        else:
            n = 2 + place // 2
            copies[n].append(RightCopy(plan, source, right_near.at[n, pl.ds(side * half, half)], sem))
    return copies


def masked_rows(plan, sizes_ref, result):
    me = lax.axis_index("mpo")
    here = lax.axis_index("bond")
    shape = (plan.rows, plan.width)
    row = lax.broadcasted_iota(jnp.int32, shape, 0) + me * plan.rows
    column = lax.broadcasted_iota(jnp.int32, shape, 1)
    row_ok = row < sector_limits(sizes_ref, plan.w, here, plan.n_bond)
    blocks = []
    for p, charge in enumerate(pair_charges()):
        if result[p] is None:
            blocks.append(jnp.zeros(shape, BF16))
            continue
        ok = row_ok & (column < sector_limits(sizes_ref, plan.w + plan.n_bond, here + charge, plan.n_bond))
        blocks.append(jnp.where(ok, result[p], 0.0).astype(BF16))
    return blocks


def whole_sum(values):
    return jnp.sum(jnp.sum(values, axis=1, keepdims=True), axis=0, keepdims=True)


def near_blocks(places, refs):
    return [refs[array] if index is None else refs[array].at[index] for array, index, _, _ in places]


def first_kernel(plan, *refs):
    sizes_ref, refs = refs[0], refs[1:]
    psi_refs, refs = refs[: plan.n_near], refs[plan.n_near :]
    left_refs, refs = refs[: plan.n_mpo], refs[plan.n_mpo :]
    sites_ref, ys_out, fs_out, ls_out, first_out, second_out = refs[:6]
    fs, ls, wide, xs, ys, out_sem, y_sem = refs[6:]
    site_matrices(plan, sizes_ref, sites_ref, first_out, second_out)
    fill_left(plan, sizes_ref, left_refs, wide, ls)
    ls_copy = pltpu.make_async_copy(ls, ls_out, out_sem.at[0])
    ls_copy.start()
    fill_vector(plan, sizes_ref, near_blocks(all_places(plan.n_mpo), psi_refs), fs)
    fs_copy = pltpu.make_async_copy(fs, fs_out, out_sem.at[1])
    fs_copy.start()
    left_phase(plan, fs, ls, xs)
    tiles = ys.reshape(PAIRS, plan.w, plan.y_step, plan.width)

    def out_copy(index):
        rows = pl.ds(pl.multiple_of(index * Y_BLOCK, Y_BLOCK), Y_BLOCK)
        return pltpu.make_async_copy(tiles.at[:, :, rows, :], ys_out.at[:, :, rows, :], y_sem.at[index])

    middle_phase(
        plan, plan.n_mpo, Y_BLOCK, 2, xs, first_out, second_out, ys, lambda index: out_copy(index).start()
    )
    for index in range(plan.rows // Y_BLOCK):
        out_copy(index).wait()
    ls_copy.wait()
    fs_copy.wait()


def image_kernel(plan, sizes_ref, ys_ref, vector_ref, own_ref, *refs):
    far_refs, (image, ys, right_near, vector, y_sem, right_sem, v_sem) = refs[: plan.n_far], refs[plan.n_far :]
    me = lax.axis_index("mpo")
    rows_here = pl.ds(pl.multiple_of(me * plan.rows, plan.rows), plan.rows)
    charges = pair_charges()
    y_copies = {
        p: pltpu.make_async_copy(ys_ref.at[p], ys.at[p], y_sem.at[p]) for p in range(PAIRS) if charges[p] <= plan.far
    }
    r_copies = right_copies(plan, own_ref, far_refs, right_near, right_sem)
    v_copy = pltpu.make_async_copy(vector_ref.at[:, rows_here, :], vector, v_sem)
    stages = [r_copies[n] + [y_copies[p] for p in range(PAIRS) if charges[p] == n] for n in range(plan.far + 1)]
    for copy in [copy for some in stages[:AHEAD] for copy in some] + [v_copy]:
        copy.start()

    def ready(n):
        for copy in [copy for some in stages[n + AHEAD : n + AHEAD + 1] for copy in some]:
            copy.start()
        for copy in stages[n]:
            copy.wait()

    result = right_phase(plan, True, ys, plan.rows, right_near, ready)
    blocks = masked_rows(plan, sizes_ref, result)
    v_copy.wait()
    along = jnp.zeros((plan.rows, plan.width), F32)
    norm = jnp.zeros((plan.rows, plan.width), F32)
    for p, block in enumerate(blocks):
        image[p] = block
        field = vector[p].astype(F32)
        along = along + field * block.astype(F32)
        norm = norm + field * field
    along = whole_sum(along)
    norm = whole_sum(norm)
    ratio = jnp.where(norm > 0, along / jnp.where(norm > 0, norm, 1.0), 0.0)
    across = jnp.zeros((plan.rows, plan.width), F32)
    for p, block in enumerate(blocks):
        left_over = block.astype(F32) - ratio * vector[p].astype(F32)
        across = across + left_over * left_over
    across = whole_sum(across)
    line = lax.broadcasted_iota(jnp.int32, (8, plan.width), 0)
    sums = jnp.where(line == 0, along, jnp.where(line == 1, norm, jnp.where(line == 2, across, 0.0)))
    parts = []
    for _ in range(3):
        parts.append(sums.astype(BF16).astype(F32))
        sums = sums - parts[-1]
    parts.append(jnp.zeros((plan.rows - 24, plan.width), F32))
    image[PAIRS] = jnp.concatenate(parts, 0).astype(BF16)


def sums_of(piece):
    block = piece[PAIRS].astype(F32)
    return block[0:8] + block[8:16] + block[16:24]


def second_kernel(plan, count_all, n_parts, near, *refs):
    sizes_ref = refs[0]
    parts, refs = refs[1 : 1 + n_parts], refs[1 + n_parts :]
    image_refs, refs = refs[: plan.n_near], refs[plan.n_near :]
    vector_ref, ls_ref, first_ref, second_ref, own_ref = refs[:5]
    far_refs, refs = refs[5 : 5 + plan.n_far], refs[5 + plan.n_far :]
    outs, image_out = refs[: plan.n_mpo], refs[plan.n_mpo]
    fs, xs, ys, vector, ls, right_near, field_sem, right_sem, out_sem = refs[plan.n_mpo + 1 :]
    me = lax.axis_index("mpo")
    blocks = near_blocks(block_places(plan.n_mpo), image_refs)
    v_copy = pltpu.make_async_copy(vector_ref, vector, field_sem.at[0])
    l_copy = pltpu.make_async_copy(ls_ref, ls, field_sem.at[1])
    r_copies = right_copies(plan, own_ref, far_refs, right_near, right_sem)
    for copy in [v_copy, l_copy]:
        copy.start()
    sums = merged([part[...] for part in parts] + (near_sums(plan, blocks) if near else []))
    rayleigh = sums[0:1, :] / sums[1:2, :]
    scale = lax.rsqrt(sums[2:3, :] / count_all + EPSILON)
    v_copy.wait()
    for place, (_, _, r, kind) in enumerate(block_places(plan.n_mpo)):
        slot, _ = sector_of(kind)
        start = slot * plan.width + lax.bitwise_xor(me, r) * plan.rows
        where = pl.ds(pl.multiple_of(start, plan.rows), plan.rows)
        for p in range(PAIRS):
            block = blocks[place][p].astype(F32)
            residual = block - rayleigh * vector[p, where, :].astype(F32)
            fs[p, where, :] = (residual * scale).astype(BF16)
    out_copies = []
    pairs_here = pl.ds(me * STATES, STATES)
    for place, (_, _, r, kind) in enumerate(block_places(plan.n_mpo)):
        if kind == 0:
            start = lax.bitwise_xor(me, r) * plan.rows
            rows = pl.ds(pl.multiple_of(start, plan.rows), plan.rows)
            out_copies.append(
                pltpu.make_async_copy(blocks[place].at[pairs_here], image_out.at[0, :, rows, :], out_sem.at[r])
            )
    for copy in out_copies + [copy for some in r_copies for copy in some]:
        copy.start()
    l_copy.wait()
    left_phase(plan, fs, ls, xs)
    middle_phase(plan, 1, 2 * Y_BLOCK, 2, xs, first_ref, second_ref, ys, lambda index: None)

    def ready(n):
        for copy in r_copies[n]:
            copy.wait()

    result = right_phase(plan, False, ys, plan.y_step, right_near, ready)
    rows = masked_rows(plan, sizes_ref, result)
    for p in range(PAIRS):
        ys[p, : plan.rows, :] = rows[p].astype(F32)
    for r, out in enumerate(outs):
        first = lax.bitwise_xor(me, r) * STATES
        for second in range(STATES):
            out[second] = ys[first + second, : plan.rows, :].astype(BF16)
    for copy in out_copies:
        copy.wait()


Y_BLOCK = 8
AHEAD = 2
COST_A = 1_000
COST_B = 4_000_000_000
VMEM = pl.BlockSpec(memory_space=pltpu.VMEM)
ANY = pl.BlockSpec(memory_space=pl.ANY)
SMEM = pl.BlockSpec(memory_space=pltpu.SMEM)
PARAMS = pltpu.CompilerParams(vmem_limit_bytes=52 * 1024 * 1024)
PARAMS_B = pltpu.CompilerParams(vmem_limit_bytes=52 * 1024 * 1024)


def shape_of(shape, dtype):
    return jax.ShapeDtypeStruct(shape, dtype)


def shards(psi, left_env, right_env, site_one, site_two, mpo_charge, left_sizes, right_sizes):
    n_mpo = lax.axis_size("mpo")
    n_bond = lax.axis_size("bond")
    width = psi.shape[2]
    plan = Plan(n_mpo, n_bond, width, right_env.shape[0])
    me = lax.axis_index("mpo")

    sites = jnp.transpose(jnp.stack([site_one, site_two]), (0, 3, 2, 4, 1))
    sites = sites.reshape(2, STATES * plan.w, STATES * plan.w)

    sizes = jnp.concatenate([mpo_charge, left_sizes, right_sizes])

    left_mine = left_env[:, 0]
    left_halves = []
    for r in range(0, n_mpo, 2):
        start = lax.bitwise_xor(me - lax.rem(me, 2), r) * plan.rows
        left_halves.append(lax.dynamic_slice_in_dim(left_mine, start, 2 * plan.rows, 1))
    right_here, left_halves[0] = lax.optimization_barrier((right_env, left_halves[0]))
    left_halves = [from_near(both, 0, 2 * r) if r else both for r, both in enumerate(left_halves)]
    psi_arrays, before = exchange_all(psi[0], (left_halves, sites, sizes))
    left_halves, sites, sizes = before
    left_pieces = [piece for both in left_halves for piece in (both, from_near(both, 0, 1))]

    right_far = right_exchange(right_here, plan.far)

    field_shape = (PAIRS, 3 * width, width)
    left_shape = (plan.rows * plan.w_pad, 3 * width)
    x_shape = (PAIRS, plan.rows * plan.w_pad, width)
    y_shape = (PAIRS, plan.y_step * plan.w, width)
    row_shape = (PAIRS, plan.rows, width)

    first_shape = (STATES * plan.w, STATES * plan.w_pad)
    second_shape = (2 * STATES * plan.w,) * 2
    y_out_shape = (PAIRS, plan.w, plan.rows, width)
    ys, vector, left_rows, first, second = pl.pallas_call(
        functools.partial(first_kernel, plan),
        out_shape=(
            shape_of(y_out_shape, F32),
            shape_of(field_shape, BF16),
            shape_of(left_shape, BF16),
            shape_of(first_shape, BF16),
            shape_of(second_shape, BF16),
        ),
        in_specs=[SMEM] + [VMEM] * (plan.n_near + n_mpo + 1),
        out_specs=(ANY, ANY, ANY, VMEM, VMEM),
        scratch_shapes=[
            pltpu.VMEM(field_shape, BF16),
            pltpu.VMEM(left_shape, BF16),
            pltpu.VMEM((3, left_shape[0], width), F32),
            pltpu.VMEM(x_shape, F32),
            pltpu.VMEM(y_shape, F32),
            pltpu.SemaphoreType.DMA((2,)),
            pltpu.SemaphoreType.DMA((plan.rows // Y_BLOCK,)),
        ],
        compiler_params=PARAMS,
        cost_estimate=pl.CostEstimate(flops=COST_A, bytes_accessed=0, transcendentals=0),
        name="states_of_vector",
    )(
        sizes, *psi_arrays, *left_pieces, sites,
    )

    right_far, ys = lax.optimization_barrier((right_far, ys))
    right_pieces = handed_over(right_far)
    right_scratch = pltpu.VMEM((plan.slots, plan.w, width, width), BF16)
    image_shape = (PAIRS + 1,) + row_shape[1:]
    image_rows = pl.pallas_call(
        functools.partial(image_kernel, plan),
        out_shape=shape_of(image_shape, BF16),
        in_specs=[SMEM] + [ANY] * (3 + plan.n_far),
        out_specs=VMEM,
        scratch_shapes=[
            pltpu.VMEM((PAIRS, plan.w * plan.rows, width), F32),
            right_scratch,
            pltpu.VMEM(row_shape, BF16),
            pltpu.SemaphoreType.DMA((PAIRS,)),
            pltpu.SemaphoreType.DMA((1 + plan.n_far,)),
            pltpu.SemaphoreType.DMA,
        ],
        compiler_params=PARAMS_B,
        cost_estimate=pl.CostEstimate(flops=COST_B, bytes_accessed=0, transcendentals=0),
        name="image_rows",
    )(sizes, ys.reshape(PAIRS, plan.w * plan.rows, width), vector, right_env, *right_pieces)

    image_here, image_first, image_mine = exchange(image_rows)
    blocks, _ = lax.optimization_barrier((image_here, image_mine[0]))
    sums = merged([sums_of(blocks[r]) for r in range(n_mpo)])
    near = n_bond == 4
    sums = far_sums(sums) if near else summed_over_bond(sums)
    last = max(image_mine)
    image_mine[last], sums = lax.optimization_barrier((image_mine[last], sums))
    image_other = handed_pairs(image_mine)
    if near:
        sums = sums + [from_near(sums[1], 0, 1)]

    count_all = n_bond * PAIRS * width * width
    *second_rows, image = pl.pallas_call(
        functools.partial(second_kernel, plan, float(count_all), len(sums), near),
        out_shape=(shape_of((STATES,) + row_shape[1:], BF16),) * n_mpo + (shape_of(psi.shape, BF16),),
        in_specs=[SMEM] + [VMEM] * (len(sums) + plan.n_near) + [ANY] * 2 + [VMEM] * 2 + [ANY] * (1 + plan.n_far),
        out_specs=(VMEM,) * n_mpo + (ANY,),
        scratch_shapes=[
            pltpu.VMEM(field_shape, BF16),
            pltpu.VMEM(x_shape, F32),
            pltpu.VMEM(y_shape, F32),
            pltpu.VMEM(field_shape, BF16),
            pltpu.VMEM(left_shape, BF16),
            right_scratch,
            pltpu.SemaphoreType.DMA((2,)),
            pltpu.SemaphoreType.DMA((1 + plan.n_far,)),
            pltpu.SemaphoreType.DMA((n_mpo,)),
        ],
        compiler_params=PARAMS,
        cost_estimate=pl.CostEstimate(flops=COST_A, bytes_accessed=0, transcendentals=0),
        name="correction_image_rows",
    )(
        sizes, *sums, *by_place(image_here, image_first, image_mine, image_other), vector, left_rows,
        first, second, right_env, *right_pieces,
    )

    result = jnp.zeros((STATES, width, width), BF16)
    for r, block in enumerate(second_rows):
        block = from_near(block, 0, r) if r else block
        start = lax.bitwise_xor(me, r) * plan.rows
        result = lax.dynamic_update_slice_in_dim(result, block, start, 1)
    return (image, result[None])


def solution(mesh):
    in_specs = (
        P(("groups", "bond"), "mpo", None, None),
        P("mpo", ("groups", "bond"), None, None),
        P(None, ("groups", "bond"), None, None),
        P("groups", None, None, None),
        P("groups", None, None, None),
        P(),
        P("groups"),
        P("groups"),
    )
    out_specs = (P(("groups", "bond"), "mpo", None, None), P(("groups", "bond"), "mpo", None, None))
    return jax.shard_map(shards, mesh=mesh, in_specs=in_specs, out_specs=out_specs, check_vma=False)
```

```python
import functools

import jax
import jax.numpy as jnp
from jax import lax
from jax.experimental import pallas as pl
from jax.experimental.pallas import tpu as pltpu
from jax.sharding import PartitionSpec as P

EPSILON = 1e-06
STATE_CHARGES = (0, 1, 1, 2)
STATES = len(STATE_CHARGES)
PAIRS = STATES * STATES
RIM = 4
F32 = jnp.float32
BF16 = jnp.bfloat16
NT = (((1,), (1,)), ((), ()))


def pair_charges():
    return [left + right for left in STATE_CHARGES for right in STATE_CHARGES]


def round_up(value, step):
    return -(-value // step) * step


def from_near(value, step, flip):
    n_bond, n_mpo = lax.axis_size("bond"), lax.axis_size("mpo")
    pairs = [
        ((i + step) * n_mpo + (j ^ flip), i * n_mpo + j)
        for i in range(n_bond)
        for j in range(n_mpo)
        if 0 <= i + step < n_bond
    ]
    return lax.ppermute(value, ("bond", "mpo"), pairs)


def mpo_bits():
    count = lax.axis_size("mpo")
    bits = []
    while count > 1:
        count //= 2
        bits.append(count)
    return bits


def exchange(own):
    n_bond, n_mpo = lax.axis_size("bond"), lax.axis_size("mpo")
    pairs = [
        (i * n_mpo + j, (i + 1 - 2 * (j % 2)) * n_mpo + j)
        for i in range(n_bond)
        for j in range(n_mpo)
        if 0 <= i + 1 - 2 * (j % 2) < n_bond
    ]
    here = own_sector(own)
    first = jnp.stack([here[0], here[1]])
    mine = {}
    for r in range(0, n_mpo, 2):
        pair = jnp.stack([here[r], here[r ^ 1]]) if r else first
        mine[r] = lax.ppermute(pair, ("bond", "mpo"), pairs)
    return here, first, mine


def own_sector(own):
    here = {0: own, 1: from_near(own, 0, 1)}
    for bit in mpo_bits()[:-1]:
        here.update({r ^ bit: from_near(here[r], 0, bit) for r in sorted(here) if r % 2 == 0})
    for r in range(2, len(here) * 2 - 2, 2):
        here[r ^ 1] = from_near(here[r], 0, 1)
    return here


def exchange_all(own, before):
    n_mpo = lax.axis_size("mpo")
    low, high = from_near(own, -1, 0), from_near(own, 1, 0)
    here = own_sector(own)
    (low, high), _, before = lax.optimization_barrier(((low, high), here[n_mpo // 2], before))
    both = {0: jnp.stack([low, high])}
    for bit in mpo_bits():
        both.update({r ^ bit: from_near(pair, 0, bit) for r, pair in list(both.items())})
    rest = [here[r] for r in range(2, n_mpo)]
    return [jnp.stack([here[0], here[1]])] + rest + [both[r] for r in range(n_mpo)], before


def all_places(n_mpo):
    places = [(0, 0, 0, 0), (0, 1, 1, 0)] + [(r - 1, None, r, 0) for r in range(2, n_mpo)]
    return places + [(n_mpo - 1 + r, side, r, 3 + side) for r in range(n_mpo) for side in range(2)]


def handed_pairs(mine):
    return {r: from_near(pair, 0, 1) for r, pair in mine.items()}


def by_place(here, first, mine, other):
    evens = sorted(mine)
    rest = [here[r] for r in sorted(here) if r > 1]
    return [first] + rest + [mine[r] for r in evens] + [other[r] for r in evens]


def block_places(n_mpo):
    places = [(0, 0, 0, 0), (0, 1, 1, 0)] + [(r - 1, None, r, 0) for r in range(2, n_mpo)]
    for kind in (1, 2):
        for r in range(0, n_mpo, 2):
            array = n_mpo - 1 + (kind - 1) * (n_mpo // 2) + r // 2
            order = (r, r ^ 1) if kind == 1 else (r ^ 1, r)
            places += [(array, index, member, kind) for index, member in enumerate(order)]
    return places


def sector_of(kind):
    odd = lax.rem(lax.axis_index("mpo"), 2)
    if kind == 0:
        return 0, 0
    if kind > 2:
        return kind - 2, 2 * kind - 7
    above = odd if kind == 1 else 1 - odd
    return 1 + above, 2 * above - 1


def right_exchange(own, far):
    n_bond, n_mpo = lax.axis_size("bond"), lax.axis_size("mpo")
    pairs = [
        ((i + 1 + j % 2) * n_mpo + j, i * n_mpo + j)
        for i in range(n_bond)
        for j in range(n_mpo)
        if 1 + j % 2 <= far and i + 1 + j % 2 < n_bond
    ]
    arrays = [lax.ppermute(own, ("bond", "mpo"), pairs)]
    half = own.shape[0] // 2
    part = lax.dynamic_slice_in_dim(own, lax.rem(lax.axis_index("mpo"), 2) * half, half, 0)
    return arrays + [from_near(part, d, 0) for d in range(3, far + 1)]


def handed_over(arrays):
    n_bond, n_mpo = lax.axis_size("bond"), lax.axis_size("mpo")
    result = []
    for place, array in enumerate(arrays):
        pairs = [
            (i * n_mpo + j, i * n_mpo + (j ^ 1))
            for i in range(n_bond)
            for j in range(n_mpo)
            if i + (2 + place if place else 1 + j % 2) < n_bond
        ]
        result += [array, lax.ppermute(array, ("bond", "mpo"), pairs)]
    return result


def merged(parts):
    along = sum(part[0:1] for part in parts)
    norm = sum(part[1:2] for part in parts)
    ratio = jnp.where(norm > 0, along / jnp.where(norm > 0, norm, 1.0), 0.0)
    across = jnp.zeros_like(along)
    for part in parts:
        own = jnp.where(part[1:2] > 0, part[0:1] / jnp.where(part[1:2] > 0, part[1:2], 1.0), 0.0)
        gap = own - ratio
        across = across + part[2:3] + gap * gap * part[1:2]
    rest = jnp.zeros((parts[0].shape[0] - 3, parts[0].shape[1]), F32)
    return jnp.concatenate([along, norm, across, rest], 0)


def summed_over_bond(sums):
    n_bond = lax.axis_size("bond")
    reach, parts = 1, [sums]
    while reach < n_bond:
        if reach > 1:
            parts = [merged(parts)]
        radix = min(4, n_bond // reach)
        parts = parts + [
            lax.ppermute(parts[0], "bond", [(i ^ (reach * k), i) for i in range(n_bond)])
            for k in range(1, radix)
        ]
        reach *= radix
    return parts


def far_sums(sums):
    n_bond, n_mpo = lax.axis_size("bond"), lax.axis_size("mpo")
    pairs = [((i ^ (2 + j % 2)) * n_mpo + j, i * n_mpo + j) for i in range(n_bond) for j in range(n_mpo)]
    return [sums, lax.ppermute(sums, ("bond", "mpo"), pairs)]


def near_sums(plan, blocks):
    here = lax.axis_index("bond")
    parts = []
    for place, (_, _, _, kind) in enumerate(block_places(plan.n_mpo)):
        if kind > 0:
            wanted = here + sector_of(kind)[1] == lax.bitwise_xor(here, 1)
            parts.append(sums_of(blocks[place]) * jnp.where(wanted, 1.0, 0.0).astype(F32))
    return parts


def sector_limits(sizes_ref, first, sector, count):
    inside = (sector >= 0) & (sector < count)
    return jnp.where(inside, sizes_ref[first + jnp.clip(sector, 0, count - 1)], 0)


def state_charge(state):
    return (state + 1) // 2


class Plan:
    def __init__(self, n_mpo, n_bond, width, mpo_width):
        self.n_mpo = n_mpo
        self.n_bond = n_bond
        self.width = width
        self.w = mpo_width
        self.w_here = mpo_width // n_mpo
        self.w_pad = round_up(mpo_width, 8)
        self.rows = width // n_mpo
        self.y_step = self.rows + 8
        self.far = min(RIM, n_bond - 1)
        self.n_near = 2 * n_mpo - 1
        self.slots = max(3, self.far + 1)
        self.n_far = 2 * max(1, self.far - 1)


def fill_left(plan, sizes_ref, left_refs, wide, ls):
    me = lax.axis_index("mpo")
    odd_rows = pl.ds(pl.multiple_of(lax.rem(me, 2) * plan.rows, plan.rows), plan.rows)
    wide[...] = jnp.zeros_like(wide)
    for r in range(plan.n_mpo):
        owner = lax.bitwise_xor(me, r)
        for t in range(plan.w_here):
            w = owner * plan.w_here + t
            block = left_refs[r][t, odd_rows, :].astype(F32)
            for c, charge in enumerate((0, 1, -1)):
                factor = jnp.where(sizes_ref[w] == charge, 1.0, 0.0).astype(F32)
                wide[c, pl.ds(w, plan.rows, stride=plan.w_pad), :] = block * factor
    for c in range(3):
        ls[:, c * plan.width : (c + 1) * plan.width] = wide[c].astype(BF16)


def fill_vector(plan, sizes_ref, psi_blocks, fs):
    me = lax.axis_index("mpo")
    here = lax.axis_index("bond")
    row = lax.broadcasted_iota(jnp.int32, (plan.width, plan.width), 0)
    column = lax.broadcasted_iota(jnp.int32, (plan.width, plan.width), 1)
    for place, (_, _, r, kind) in enumerate(all_places(plan.n_mpo)):
        slot, step = sector_of(kind)
        sector = here + step
        first = lax.bitwise_xor(me, r)
        row_ok = row < sector_limits(sizes_ref, plan.w, sector, plan.n_bond)
        where = pl.ds(pl.multiple_of(slot * plan.width, plan.width), plan.width)
        for second in range(STATES):
            target = sector + state_charge(first) + STATE_CHARGES[second]
            ok = row_ok & (column < sector_limits(sizes_ref, plan.w + plan.n_bond, target, plan.n_bond))
            block = psi_blocks[place][second].astype(F32)
            fs[first * STATES + second, where, :] = jnp.where(ok, block, 0.0).astype(BF16)


def left_phase(plan, fs, ls, xs):
    def step(index, carry):
        p = index * 2
        both = jnp.concatenate([fs[p], fs[p + 1]], axis=1)
        done = jnp.dot(ls[...], both, preferred_element_type=F32)
        xs[p] = done[:, : plan.width]
        xs[p + 1] = done[:, plan.width :]
        return carry

    lax.fori_loop(0, PAIRS // 2, step, 0, unroll=8)


def site_matrices(plan, sizes_ref, sites_ref, first_out, second_out):
    w, pad = plan.w, plan.w_pad
    size = STATES * w

    def index(shape, axis):
        return lax.broadcasted_iota(jnp.int32, shape, axis)

    def charges(bond):
        total = jnp.zeros(bond.shape, jnp.int32)
        for v in range(w):
            total = jnp.where(bond == v, sizes_ref[v], total)
        return total

    row, column = index((size, size), 0), index((size, size), 1)
    local_step = state_charge(row // w) - state_charge(column // w)
    allowed = local_step == charges(row % w) - charges(column % w)
    first = jnp.where(allowed, sites_ref[0].astype(F32), 0.0).astype(BF16)
    second = jnp.where(allowed, sites_ref[1].astype(F32), 0.0).astype(BF16)

    into = (size, STATES * pad)
    spread_w = (index(into, 0) // w == index(into, 1) // pad) & (index(into, 0) % w == index(into, 1) % pad)
    first = jnp.dot(first, jnp.where(spread_w, 1.0, 0.0).astype(BF16), preferred_element_type=F32)
    first_out[...] = first.astype(BF16)

    into = (size, 2 * size)
    of, to = index(into, 0), index(into, 1)
    halves = []
    for k in range(2):
        spread_v = to == (of // w) * 2 * w + k * w + of % w
        halves.append(jnp.dot(second, jnp.where(spread_v, 1.0, 0.0).astype(BF16), preferred_element_type=F32))
    second_out[...] = jnp.concatenate(halves, 0).astype(BF16)


def middle_phase(plan, groups, block, unroll, xs, first_ref, second_ref, ys, done):
    w, pad = plan.w, plan.w_pad
    first = first_ref[...]
    second = second_ref[...]
    size = STATES * w
    if groups > 1:
        column = lax.broadcasted_iota(jnp.int32, first.shape, 1) % pad
        wide = first.astype(F32)
        rows = []
        for g in range(groups):
            ok = (column >= g * plan.w_here) & (column < (g + 1) * plan.w_here)
            rows.append(jnp.where(ok, wide, 0.0))
        first = jnp.concatenate(rows, 0).astype(BF16)

    def step(index, carry):
        middle = []
        for b in range(STATES):
            columns = []
            for one in range(block):
                start = pl.multiple_of((index * block + one) * pad, pad)
                columns.append(
                    jnp.concatenate([xs[a * STATES + b, pl.ds(start, pad), :] for a in range(STATES)], 0)
                )
            column = jnp.concatenate(columns, 1).astype(BF16)
            middle.append(jnp.dot(first, column, preferred_element_type=F32))
        for half in range(STATES // 2):
            total = None
            for g in range(groups):
                at = g * size + half * 2 * w
                column = jnp.concatenate([z[at : at + 2 * w] for z in middle], 0).astype(BF16)
                term = jnp.dot(second, column, preferred_element_type=F32)
                if groups > 1:
                    term = term.astype(BF16).astype(F32)
                total = term if total is None else total + term
            for k in range(2):
                for s2 in range(STATES):
                    at = k * size + s2 * w
                    for one in range(block):
                        rows = pl.ds(index * block + one, w, stride=plan.y_step)
                        ys[(2 * half + k) * STATES + s2, rows, :] = total[
                            at : at + w, one * plan.width : (one + 1) * plan.width
                        ]
        done(index)
        return carry

    lax.fori_loop(0, plan.rows // block, step, 0, unroll=unroll)


def right_phase(plan, split, ys, y_step, right_near, ready):
    result = [None] * PAIRS
    for n in range(plan.far + 1):
        ready(n)
        members = [p for p, charge in enumerate(pair_charges()) if charge == n]
        total = None
        for first in range(0, plan.w, plan.w_here):
            group = range(first, first + plan.w_here)
            right = jnp.concatenate([right_near[n, u] for u in group], 1)
            lines = []
            for p in members:
                parts = [ys[p, pl.ds(u * y_step, plan.rows), :] for u in group]
                lines.append(jnp.concatenate(parts, 1))
            field = jnp.concatenate(lines, 0)
            high = field.astype(BF16)
            if split:
                low = (field - high.astype(F32)).astype(BF16)
                high = jnp.concatenate([high, low], 0)
            term = lax.dot_general(high, right, NT, preferred_element_type=F32)
            total = term if total is None else total + term
        if split:
            half = total.shape[0] // 2
            total = total[:half] + total[half:]
        for place, p in enumerate(members):
            result[p] = total[place * plan.rows : (place + 1) * plan.rows]
    return result


class RightCopy:
    def __init__(self, plan, source, target, sem, slot=None):
        self.copy = pltpu.make_async_copy(source.at[:, 0], target, sem)
        self.there = None if slot is None else slot <= plan.far

    def start(self):
        self.do(self.copy.start)

    def wait(self):
        self.do(self.copy.wait)

    def do(self, action):
        if self.there is None:
            action()
        else:
            pl.when(self.there)(action)


def right_copies(plan, own_ref, far_refs, right_near, sems):
    odd = lax.rem(lax.axis_index("mpo"), 2)
    half = plan.w // 2
    copies = [[] for _ in range(plan.far + 1)]
    copies[0].append(RightCopy(plan, own_ref, right_near.at[0], sems.at[0]))
    for place, source in enumerate(far_refs):
        side = 1 - odd if place % 2 else odd
        sem = sems.at[1 + place]
        if place < 2:
            copies[1].append(RightCopy(plan, source, right_near.at[1 + side], sem, 1 + side))
        else:
            n = 2 + place // 2
            copies[n].append(RightCopy(plan, source, right_near.at[n, pl.ds(side * half, half)], sem))
    return copies


def masked_rows(plan, sizes_ref, result):
    me = lax.axis_index("mpo")
    here = lax.axis_index("bond")
    shape = (plan.rows, plan.width)
    row = lax.broadcasted_iota(jnp.int32, shape, 0) + me * plan.rows
    column = lax.broadcasted_iota(jnp.int32, shape, 1)
    row_ok = row < sector_limits(sizes_ref, plan.w, here, plan.n_bond)
    blocks = []
    for p, charge in enumerate(pair_charges()):
        if result[p] is None:
            blocks.append(jnp.zeros(shape, BF16))
            continue
        ok = row_ok & (column < sector_limits(sizes_ref, plan.w + plan.n_bond, here + charge, plan.n_bond))
        blocks.append(jnp.where(ok, result[p], 0.0).astype(BF16))
    return blocks


def whole_sum(values):
    return jnp.sum(jnp.sum(values, axis=1, keepdims=True), axis=0, keepdims=True)


def near_blocks(places, refs):
    return [refs[array] if index is None else refs[array].at[index] for array, index, _, _ in places]


def first_kernel(plan, *refs):
    sizes_ref, refs = refs[0], refs[1:]
    psi_refs, refs = refs[: plan.n_near], refs[plan.n_near :]
    left_refs, refs = refs[: plan.n_mpo], refs[plan.n_mpo :]
    sites_ref, ys_out, fs_out, ls_out, first_out, second_out = refs[:6]
    fs, ls, wide, xs, ys, out_sem, y_sem = refs[6:]
    site_matrices(plan, sizes_ref, sites_ref, first_out, second_out)
    fill_left(plan, sizes_ref, left_refs, wide, ls)
    ls_copy = pltpu.make_async_copy(ls, ls_out, out_sem.at[0])
    ls_copy.start()
    fill_vector(plan, sizes_ref, near_blocks(all_places(plan.n_mpo), psi_refs), fs)
    fs_copy = pltpu.make_async_copy(fs, fs_out, out_sem.at[1])
    fs_copy.start()
    left_phase(plan, fs, ls, xs)
    tiles = ys.reshape(PAIRS, plan.w, plan.y_step, plan.width)

    def out_copy(index):
        rows = pl.ds(pl.multiple_of(index * Y_BLOCK, Y_BLOCK), Y_BLOCK)
        return pltpu.make_async_copy(tiles.at[:, :, rows, :], ys_out.at[:, :, rows, :], y_sem.at[index])

    middle_phase(
        plan, plan.n_mpo, Y_BLOCK, 2, xs, first_out, second_out, ys, lambda index: out_copy(index).start()
    )
    for index in range(plan.rows // Y_BLOCK):
        out_copy(index).wait()
    ls_copy.wait()
    fs_copy.wait()


def image_kernel(plan, sizes_ref, ys_ref, vector_ref, own_ref, *refs):
    far_refs, (image, ys, right_near, vector, y_sem, right_sem, v_sem) = refs[: plan.n_far], refs[plan.n_far :]
    me = lax.axis_index("mpo")
    rows_here = pl.ds(pl.multiple_of(me * plan.rows, plan.rows), plan.rows)
    charges = pair_charges()
    y_copies = {
        p: pltpu.make_async_copy(ys_ref.at[p], ys.at[p], y_sem.at[p]) for p in range(PAIRS) if charges[p] <= plan.far
    }
    r_copies = right_copies(plan, own_ref, far_refs, right_near, right_sem)
    v_copy = pltpu.make_async_copy(vector_ref.at[:, rows_here, :], vector, v_sem)
    stages = [r_copies[n] + [y_copies[p] for p in range(PAIRS) if charges[p] == n] for n in range(plan.far + 1)]
    for copy in [copy for some in stages[:AHEAD] for copy in some] + [v_copy]:
        copy.start()

    def ready(n):
        for copy in [copy for some in stages[n + AHEAD : n + AHEAD + 1] for copy in some]:
            copy.start()
        for copy in stages[n]:
            copy.wait()

    result = right_phase(plan, True, ys, plan.rows, right_near, ready)
    blocks = masked_rows(plan, sizes_ref, result)
    v_copy.wait()
    along = jnp.zeros((plan.rows, plan.width), F32)
    norm = jnp.zeros((plan.rows, plan.width), F32)
    for p, block in enumerate(blocks):
        image[p] = block
        field = vector[p].astype(F32)
        along = along + field * block.astype(F32)
        norm = norm + field * field
    along = whole_sum(along)
    norm = whole_sum(norm)
    ratio = jnp.where(norm > 0, along / jnp.where(norm > 0, norm, 1.0), 0.0)
    across = jnp.zeros((plan.rows, plan.width), F32)
    for p, block in enumerate(blocks):
        left_over = block.astype(F32) - ratio * vector[p].astype(F32)
        across = across + left_over * left_over
    across = whole_sum(across)
    line = lax.broadcasted_iota(jnp.int32, (8, plan.width), 0)
    sums = jnp.where(line == 0, along, jnp.where(line == 1, norm, jnp.where(line == 2, across, 0.0)))
    parts = []
    for _ in range(3):
        parts.append(sums.astype(BF16).astype(F32))
        sums = sums - parts[-1]
    parts.append(jnp.zeros((plan.rows - 24, plan.width), F32))
    image[PAIRS] = jnp.concatenate(parts, 0).astype(BF16)


def sums_of(piece):
    block = piece[PAIRS].astype(F32)
    return block[0:8] + block[8:16] + block[16:24]


def second_kernel(plan, count_all, n_parts, near, *refs):
    sizes_ref = refs[0]
    parts, refs = refs[1 : 1 + n_parts], refs[1 + n_parts :]
    image_refs, refs = refs[: plan.n_near], refs[plan.n_near :]
    vector_ref, ls_ref, first_ref, second_ref, own_ref = refs[:5]
    far_refs, refs = refs[5 : 5 + plan.n_far], refs[5 + plan.n_far :]
    outs, image_out = refs[: plan.n_mpo], refs[plan.n_mpo]
    fs, xs, ys, vector, ls, right_near, field_sem, right_sem, out_sem = refs[plan.n_mpo + 1 :]
    me = lax.axis_index("mpo")
    blocks = near_blocks(block_places(plan.n_mpo), image_refs)
    v_copy = pltpu.make_async_copy(vector_ref, vector, field_sem.at[0])
    l_copy = pltpu.make_async_copy(ls_ref, ls, field_sem.at[1])
    r_copies = right_copies(plan, own_ref, far_refs, right_near, right_sem)
    for copy in [v_copy, l_copy]:
        copy.start()
    sums = merged([part[...] for part in parts] + (near_sums(plan, blocks) if near else []))
    rayleigh = sums[0:1, :] / sums[1:2, :]
    scale = lax.rsqrt(sums[2:3, :] / count_all + EPSILON)
    v_copy.wait()
    for place, (_, _, r, kind) in enumerate(block_places(plan.n_mpo)):
        slot, _ = sector_of(kind)
        start = slot * plan.width + lax.bitwise_xor(me, r) * plan.rows
        where = pl.ds(pl.multiple_of(start, plan.rows), plan.rows)
        for p in range(PAIRS):
            block = blocks[place][p].astype(F32)
            residual = block - rayleigh * vector[p, where, :].astype(F32)
            fs[p, where, :] = (residual * scale).astype(BF16)
    out_copies = []
    pairs_here = pl.ds(me * STATES, STATES)
    for place, (_, _, r, kind) in enumerate(block_places(plan.n_mpo)):
        if kind == 0:
            start = lax.bitwise_xor(me, r) * plan.rows
            rows = pl.ds(pl.multiple_of(start, plan.rows), plan.rows)
            out_copies.append(
                pltpu.make_async_copy(blocks[place].at[pairs_here], image_out.at[0, :, rows, :], out_sem.at[r])
            )
    for copy in out_copies + [copy for some in r_copies for copy in some]:
        copy.start()
    l_copy.wait()
    left_phase(plan, fs, ls, xs)
    middle_phase(plan, 1, 2 * Y_BLOCK, 2, xs, first_ref, second_ref, ys, lambda index: None)

    def ready(n):
        for copy in r_copies[n]:
            copy.wait()

    result = right_phase(plan, False, ys, plan.y_step, right_near, ready)
    rows = masked_rows(plan, sizes_ref, result)
    for p in range(PAIRS):
        ys[p, : plan.rows, :] = rows[p].astype(F32)
    for r, out in enumerate(outs):
        first = lax.bitwise_xor(me, r) * STATES
        for second in range(STATES):
            out[second] = ys[first + second, : plan.rows, :].astype(BF16)
    for copy in out_copies:
        copy.wait()


Y_BLOCK = 8
AHEAD = 2
COST_A = 1_000
COST_B = 4_000_000_000
VMEM = pl.BlockSpec(memory_space=pltpu.VMEM)
ANY = pl.BlockSpec(memory_space=pl.ANY)
SMEM = pl.BlockSpec(memory_space=pltpu.SMEM)
PARAMS = pltpu.CompilerParams(vmem_limit_bytes=52 * 1024 * 1024)
PARAMS_B = pltpu.CompilerParams(vmem_limit_bytes=52 * 1024 * 1024)


def shape_of(shape, dtype):
    return jax.ShapeDtypeStruct(shape, dtype)


def shards(psi, left_env, right_env, site_one, site_two, mpo_charge, left_sizes, right_sizes):
    n_mpo = lax.axis_size("mpo")
    n_bond = lax.axis_size("bond")
    width = psi.shape[2]
    plan = Plan(n_mpo, n_bond, width, right_env.shape[0])
    me = lax.axis_index("mpo")

    sites = jnp.transpose(jnp.stack([site_one, site_two]), (0, 3, 2, 4, 1))
    sites = sites.reshape(2, STATES * plan.w, STATES * plan.w)

    sizes = jnp.concatenate([mpo_charge, left_sizes, right_sizes])

    left_mine = left_env[:, 0]
    left_halves = []
    for r in range(0, n_mpo, 2):
        start = lax.bitwise_xor(me - lax.rem(me, 2), r) * plan.rows
        left_halves.append(lax.dynamic_slice_in_dim(left_mine, start, 2 * plan.rows, 1))
    right_here, left_halves[0] = lax.optimization_barrier((right_env, left_halves[0]))
    left_halves = [from_near(both, 0, 2 * r) if r else both for r, both in enumerate(left_halves)]
    psi_arrays, before = exchange_all(psi[0], (left_halves, sites, sizes))
    left_halves, sites, sizes = before
    left_pieces = [piece for both in left_halves for piece in (both, from_near(both, 0, 1))]

    right_far = right_exchange(right_here, plan.far)

    field_shape = (PAIRS, 3 * width, width)
    left_shape = (plan.rows * plan.w_pad, 3 * width)
    x_shape = (PAIRS, plan.rows * plan.w_pad, width)
    y_shape = (PAIRS, plan.y_step * plan.w, width)
    row_shape = (PAIRS, plan.rows, width)

    first_shape = (STATES * plan.w, STATES * plan.w_pad)
    second_shape = (2 * STATES * plan.w,) * 2
    y_out_shape = (PAIRS, plan.w, plan.rows, width)
    ys, vector, left_rows, first, second = pl.pallas_call(
        functools.partial(first_kernel, plan),
        out_shape=(
            shape_of(y_out_shape, F32),
            shape_of(field_shape, BF16),
            shape_of(left_shape, BF16),
            shape_of(first_shape, BF16),
            shape_of(second_shape, BF16),
        ),
        in_specs=[SMEM] + [VMEM] * (plan.n_near + n_mpo + 1),
        out_specs=(ANY, ANY, ANY, VMEM, VMEM),
        scratch_shapes=[
            pltpu.VMEM(field_shape, BF16),
            pltpu.VMEM(left_shape, BF16),
            pltpu.VMEM((3, left_shape[0], width), F32),
            pltpu.VMEM(x_shape, F32),
            pltpu.VMEM(y_shape, F32),
            pltpu.SemaphoreType.DMA((2,)),
            pltpu.SemaphoreType.DMA((plan.rows // Y_BLOCK,)),
        ],
        compiler_params=PARAMS,
        cost_estimate=pl.CostEstimate(flops=COST_A, bytes_accessed=0, transcendentals=0),
        name="states_of_vector",
    )(
        sizes, *psi_arrays, *left_pieces, sites,
    )

    right_far, ys = lax.optimization_barrier((right_far, ys))
    right_pieces = handed_over(right_far)
    right_scratch = pltpu.VMEM((plan.slots, plan.w, width, width), BF16)
    image_shape = (PAIRS + 1,) + row_shape[1:]
    image_rows = pl.pallas_call(
        functools.partial(image_kernel, plan),
        out_shape=shape_of(image_shape, BF16),
        in_specs=[SMEM] + [ANY] * (3 + plan.n_far),
        out_specs=VMEM,
        scratch_shapes=[
            pltpu.VMEM((PAIRS, plan.w * plan.rows, width), F32),
            right_scratch,
            pltpu.VMEM(row_shape, BF16),
            pltpu.SemaphoreType.DMA((PAIRS,)),
            pltpu.SemaphoreType.DMA((1 + plan.n_far,)),
            pltpu.SemaphoreType.DMA,
        ],
        compiler_params=PARAMS_B,
        cost_estimate=pl.CostEstimate(flops=COST_B, bytes_accessed=0, transcendentals=0),
        name="image_rows",
    )(sizes, ys.reshape(PAIRS, plan.w * plan.rows, width), vector, right_env, *right_pieces)

    image_here, image_first, image_mine = exchange(image_rows)
    blocks, _ = lax.optimization_barrier((image_here, image_mine[0]))
    sums = merged([sums_of(blocks[r]) for r in range(n_mpo)])
    near = n_bond == 4
    sums = far_sums(sums) if near else summed_over_bond(sums)
    last = max(image_mine)
    image_mine[last], sums = lax.optimization_barrier((image_mine[last], sums))
    image_other = handed_pairs(image_mine)
    if near:
        sums = sums + [from_near(sums[1], 0, 1)]

    count_all = n_bond * PAIRS * width * width
    *second_rows, image = pl.pallas_call(
        functools.partial(second_kernel, plan, float(count_all), len(sums), near),
        out_shape=(shape_of((STATES,) + row_shape[1:], BF16),) * n_mpo + (shape_of(psi.shape, BF16),),
        in_specs=[SMEM] + [VMEM] * (len(sums) + plan.n_near) + [ANY] * 2 + [VMEM] * 2 + [ANY] * (1 + plan.n_far),
        out_specs=(VMEM,) * n_mpo + (ANY,),
        scratch_shapes=[
            pltpu.VMEM(field_shape, BF16),
            pltpu.VMEM(x_shape, F32),
            pltpu.VMEM(y_shape, F32),
            pltpu.VMEM(field_shape, BF16),
            pltpu.VMEM(left_shape, BF16),
            right_scratch,
            pltpu.SemaphoreType.DMA((2,)),
            pltpu.SemaphoreType.DMA((1 + plan.n_far,)),
            pltpu.SemaphoreType.DMA((n_mpo,)),
        ],
        compiler_params=PARAMS,
        cost_estimate=pl.CostEstimate(flops=COST_A, bytes_accessed=0, transcendentals=0),
        name="correction_image_rows",
    )(
        sizes, *sums, *by_place(image_here, image_first, image_mine, image_other), vector, left_rows,
        first, second, right_env, *right_pieces,
    )

    result = jnp.zeros((STATES, width, width), BF16)
    for r, block in enumerate(second_rows):
        block = from_near(block, 0, r) if r else block
        start = lax.bitwise_xor(me, r) * plan.rows
        result = lax.dynamic_update_slice_in_dim(result, block, start, 1)
    return (image, result[None])


def solution(mesh):
    in_specs = (
        P(("groups", "bond"), "mpo", None, None),
        P("mpo", ("groups", "bond"), None, None),
        P(None, ("groups", "bond"), None, None),
        P("groups", None, None, None),
        P("groups", None, None, None),
        P(),
        P("groups"),
        P("groups"),
    )
    out_specs = (P(("groups", "bond"), "mpo", None, None), P(("groups", "bond"), "mpo", None, None))
    return jax.shard_map(shards, mesh=mesh, in_specs=in_specs, out_specs=out_specs, check_vma=False)
```
